32 devices in a mesh: tx: 4 (over z), ty: 4 (over y, core), src: 2 (over x).
Axes of the slice: x: 2, y: 2, z: 4, core: 2. Of those that a mesh axis runs over, the one named last changes fastest.
Arguments:
- adj_now: float32 [2, 3, 32, 64, 256], P('src', None, 'tx', 'ty'), may hold values from -6 to 6
- adj_later: float32 [2, 3, 32, 64, 256], P('src', None, 'tx', 'ty'), may hold values from -6 to 6
- forward_field: bfloat16 [2, 3, 3, 32, 64, 256], P('src', None, None, 'tx', 'ty'), may hold values from -6 to 6
- lame_first: float32 [32, 64, 256], P('tx', 'ty'), may hold values from 0.5 to 2
- shear: float32 [32, 64, 256], P('tx', 'ty'), may hold values from 0.3 to 1.5
- buoyancy: float32 [32, 64, 256], P('tx', 'ty'), may hold values from 0.5 to 1.5
- seafloor_depth: int32 [32, 64], P('tx', 'ty'), may hold values from 126 to 255
- station_columns: int32 [2, 64], P('src'), may hold values from 0 to 2047
- station_traces: float32 [2, 3, 64], P('src'), may hold values from -60 to 60
Outputs:
- adj_final: float32 [2, 3, 32, 64, 256], P('src', None, 'tx', 'ty')
- kernels: float32 [2, 32, 64, 256], P(None, 'tx', 'ty', 'src')
The draws below stay inside these ranges and needn't reach their ends.
All inputs are finite; a program needn't handle non-finite values.
Results may differ from the reference program's by a relative error of at most 0.0003.
Values may be sent and summed in bfloat16 or wider, within the bound.
No kernel may reach another device: no remote copies, remote signals or barrier semaphores. Data moves between devices by JAX's collectives and lax.ppermute only.
A program may use at most 64 MiB of HBM per device.

```python
import math
import jax
import jax.numpy as jnp
from jax import lax

CX = 8
CY = 16
NZ = 256
STEPS = 3
STATIONS = 64
NX = 32
NY = 64
SOURCES = 2


def draw_seafloor_depth(key, part):
    key_tile, key_rough = jax.random.split(jax.random.fold_in(key, 17))
    unit_cells = max(1, NZ // 32)
    levels = jnp.array([1, 2, 4, 8, 16], dtype=jnp.int32)
    picked = jax.random.randint(key_tile, (NX // CX, NY // CY), 0, 5)
    thickness = levels[picked] * unit_cells
    spread_tiles = jnp.repeat(jnp.repeat(thickness, CX, axis=0), CY, axis=1)
    rough = jax.random.randint(key_rough, (NX, NY), 0, 3)
    return (NZ - spread_tiles - rough).astype(jnp.int32)


def set_ends(entries, key, smallest, high):
    extent = entries.shape
    index_at = [jax.random.randint(jax.random.fold_in(key, axis), (), 0, extent[axis]) for axis in range(len(extent))]
    entries = entries.at[tuple(index_at)].set(smallest)
    longest = extent.index(max(extent))
    index_at[longest] = (index_at[longest] + 1) % extent[longest]
    return entries.at[tuple(index_at)].set(high)


def block_scale(own_key, shape, cuts, smallest, top_value):
    level = 1.0
    for dim, blocks in cuts:
        draws = jax.random.uniform(jax.random.fold_in(jax.random.fold_in(own_key, 6), dim), (blocks,), jnp.float32, smallest / len(cuts), top_value / len(cuts))
        level = level * jnp.repeat(jnp.exp(draws), shape[dim] // blocks).reshape((-1,) + (1,) * (len(shape) - 1 - dim))
    return level


def scatter_about(own_key, shape, spread, reach, cuts=(), kind=jnp.bfloat16):
    drawn = spread * jax.random.normal(own_key, shape, jnp.float32)
    if cuts:
        drawn = drawn * block_scale(own_key, shape, cuts, -0.22, 0.18)
    return jnp.clip(drawn, -reach, reach).astype(kind)


def setup_inputs(seed: int = 0) -> dict:
    key_list = jax.random.split(jax.random.key(seed), 10)
    adj_now = scatter_about(key_list[0], (SOURCES, 3, NX, NY, NZ), 1.0, 6.0, ((0, 2), (2, 4), (3, 4)), jnp.float32)
    adj_later = scatter_about(key_list[1], (SOURCES, 3, NX, NY, NZ), 1.0, 6.0, ((0, 2), (2, 4), (3, 4)), jnp.float32)
    forward_field = scatter_about(key_list[2], (SOURCES, STEPS, 3, NX, NY, NZ), 1.0, 6.0, ((0, 2), (3, 4), (4, 4)))
    lame_first = jnp.clip(jnp.exp(math.log(2.0) - 1.3862944 * jax.random.uniform(key_list[3], (NX, NY, NZ), jnp.float32) ** block_scale(key_list[3], (NX, NY, NZ), ((0, 4), (1, 4)), -0.2, 0.2)), 0.5, 2.0)
    shear = jnp.clip(jnp.exp(math.log(1.5) - 1.60943787 * jax.random.uniform(key_list[4], (NX, NY, NZ), jnp.float32) ** block_scale(key_list[4], (NX, NY, NZ), ((0, 4), (1, 4)), -0.2, 0.2)), 0.3, 1.5)
    buoyancy = jnp.clip(jnp.exp(math.log(1.5) - 1.0986123 * jax.random.uniform(key_list[5], (NX, NY, NZ), jnp.float32) ** block_scale(key_list[5], (NX, NY, NZ), ((0, 4), (1, 4)), -0.2, 0.2)), 0.5, 1.5)
    seafloor_depth = draw_seafloor_depth(jax.random.fold_in(key_list[9], 71), 0)
    station_columns = set_ends(jax.random.randint(key_list[7], (SOURCES, STATIONS), 0, NX * NY), jax.random.fold_in(key_list[7], 1), 0, (NX * NY) - 1).astype(jnp.int32)
    station_traces = scatter_about(key_list[8], (SOURCES, STEPS, STATIONS), 10.0, 60.0, ((0, 2),), jnp.float32)
    return dict(adj_now=adj_now, adj_later=adj_later, forward_field=forward_field, lame_first=lame_first, shear=shear, buoyancy=buoyancy, seafloor_depth=seafloor_depth, station_columns=station_columns, station_traces=station_traces)


step_squared = 0.04


def shifted(padded, dx, dy, dz):
    span_x = padded.shape[-3] - 2
    span_y = padded.shape[-2] - 2
    span_z = padded.shape[-1] - 2
    return padded[..., 1 + dx:1 + dx + span_x, 1 + dy:1 + dy + span_y, 1 + dz:1 + dz + span_z]


def unit_axis(k, sign):
    offset = [0, 0, 0]
    offset[k] = sign
    return offset


def pair_offset(k, sk, d, sd):
    offset = [0, 0, 0]
    offset[k] = offset[k] + sk
    offset[d] = offset[d] + sd
    return offset


def depth_pad(field):
    return jnp.pad(field, [(0, 0)] * (field.ndim - 1) + [(1, 1)])


def elastic_force(field, lame, mu_eff, buoy):
    padded = depth_pad(field)
    parts = []
    for k in range(3):
        piece = padded[..., k, :, :, :]
        centre = shifted(piece, 0, 0, 0)
        laplace = -6.0 * centre
        for d in range(3):
            laplace = laplace + shifted(piece, *unit_axis(d, 1)) + shifted(piece, *unit_axis(d, -1))
        grad_div = shifted(piece, *unit_axis(k, 1)) - 2.0 * centre + shifted(piece, *unit_axis(k, -1))
        for d in range(3):
            if d != k:
                other = padded[..., d, :, :, :]
                grad_div = grad_div + 0.25 * (shifted(other, *pair_offset(k, 1, d, 1)) - shifted(other, *pair_offset(k, 1, d, -1)) - shifted(other, *pair_offset(k, -1, d, 1)) + shifted(other, *pair_offset(k, -1, d, -1)))
        parts.append(buoy * (mu_eff * laplace + (lame + mu_eff) * grad_div))
    return jnp.stack(parts, axis=-4)


def gradients(field):
    padded = depth_pad(field)
    table = []
    for k in range(3):
        piece = padded[..., k, :, :, :]
        table.append([0.5 * (shifted(piece, *unit_axis(d, 1)) - shifted(piece, *unit_axis(d, -1))) for d in range(3)])
    return table


def accumulate(kernel_lam, kernel_mu, adj_padded, fwd_padded, solid_mask):
    grad_adj = gradients(adj_padded)
    grad_fwd = gradients(fwd_padded)
    div_adj = grad_adj[0][0] + grad_adj[1][1] + grad_adj[2][2]
    div_fwd = grad_fwd[0][0] + grad_fwd[1][1] + grad_fwd[2][2]
    contraction = grad_adj[0][0] * grad_fwd[0][0]
    for k in range(3):
        for d in range(3):
            if k + d > 0:
                contraction = contraction + grad_adj[k][d] * grad_fwd[k][d]
    kernel_lam = kernel_lam + jnp.sum(div_adj * div_fwd, axis=0)
    kernel_mu = kernel_mu + jnp.sum(solid_mask * contraction, axis=0)
    return kernel_lam, kernel_mu


def vertical_source(columns, amps, depth_region, anchor_x, anchor_y, total_y, depth_cells):
    ext_x, ext_y = depth_region.shape
    loc_x = columns // total_y - anchor_x
    loc_y = columns % total_y - anchor_y
    inside = (loc_x >= 0) & (loc_x < ext_x) & (loc_y >= 0) & (loc_y < ext_y)
    loc_x = jnp.clip(loc_x, 0, ext_x - 1).astype(jnp.int32)
    loc_y = jnp.clip(loc_y, 0, ext_y - 1).astype(jnp.int32)
    cell_z = depth_region[loc_x, loc_y].astype(jnp.int32)
    values = jnp.where(inside, amps, jnp.zeros_like(amps))
    rows = lax.broadcasted_iota(jnp.int32, columns.shape, 0)
    field = jnp.zeros((columns.shape[0], ext_x * ext_y, depth_cells), amps.dtype)
    field = field.at[rows, loc_x * ext_y + loc_y, cell_z].add(values)
    return field.reshape(columns.shape[0], ext_x, ext_y, depth_cells)


def pad_plane(field):
    return jnp.pad(field, ((0, 0), (0, 0), (1, 1), (1, 1), (0, 0)))


def reference(adj_now, adj_later, forward_field, lame_first, shear, buoyancy, seafloor_depth, station_columns, station_traces):
    levels = lax.broadcasted_iota(jnp.int32, (NX, NY, NZ), 2)
    solid_mask = (levels >= seafloor_depth[:, :, None]).astype(lame_first.dtype)
    mu_eff = shear * solid_mask

    def one_source(items):
        adj_cur, adj_prev, forward_one, columns_one, traces_one = items
        adj_cur = adj_cur[None]
        adj_prev = adj_prev[None]
        forward_one = forward_one[None]
        columns_one = columns_one[None]
        traces_one = traces_one[None]
        kernel_lam = jnp.zeros((NX, NY, NZ), jnp.float32)
        kernel_mu = jnp.zeros((NX, NY, NZ), jnp.float32)
        for step_index in range(STEPS):
            padded = pad_plane(adj_cur)
            source = vertical_source(columns_one, traces_one[:, step_index], seafloor_depth, 0, 0, NY, NZ)
            force_now = elastic_force(padded, lame_first, mu_eff, buoyancy)
            force_now = force_now.at[:, 2].add(buoyancy * source)
            fresh_now = 2.0 * adj_cur - adj_prev + step_squared * force_now
            forward_now = forward_one[:, step_index].astype(jnp.float32)
            kernel_lam, kernel_mu = accumulate(kernel_lam, kernel_mu, padded, pad_plane(forward_now), solid_mask)
            adj_prev = adj_cur
            adj_cur = fresh_now
        return adj_cur[0], kernel_lam, kernel_mu

    finals, lam_parts, mu_parts = lax.map(one_source, (adj_now, adj_later, forward_field, station_columns, station_traces))
    kernels = jnp.stack([jnp.sum(lam_parts, axis=0), jnp.sum(mu_parts, axis=0)]) * (1.0 / SOURCES)
    return finals, kernels
```

```python
import functools

import jax
import jax.numpy as jnp
from jax import lax
from jax.experimental import pallas as pl
from jax.experimental.pallas import tpu as pltpu
from jax.sharding import PartitionSpec as P

STEPS = 3
STEP_SQUARED = 0.04
RING = 3
PAD = 4
AXES = ("tx", "ty", "src")
F32 = jnp.float32
BF16 = jnp.bfloat16


def halo_units():
    units = []
    for name, count, rings in (("u", 3, 3), ("p", 3, 2), ("c", 2, 2), ("s", 1, 1)):
        for k in range(count):
            for ring in range(1, rings + 1):
                units.append((name, k, ring, "hi"))
                if ring == 1:
                    units.append((name, k, ring, "lo"))
    cornered = len(units)
    for k in range(3 * STEPS):
        units.append(("f", k, 1, "hi"))
    return units, cornered


UNITS, CORNERED = halo_units()
FACE_BLOCKS = len(UNITS)
SIDE_BLOCKS = (len(UNITS) + 1) // 2
CORNER_BLOCKS = ((CORNERED + 1) // 2 * 8 + 15) // 16


def split(value):
    top = value.astype(BF16).astype(F32)
    return top, value - top


def corner_rows(units, first):
    blocks = []
    row = lax.broadcasted_iota(jnp.int32, units[0].shape, 0)
    zero = jnp.zeros_like(units[0])
    packed = []
    for n in range(0, CORNERED, 2):
        a = pltpu.roll(units[n], (8 - first) % 8, 0) if first else units[n]
        b = pltpu.roll(units[n + 1], (8 - first + 4) % 8, 0) if n + 1 < CORNERED else zero
        packed.append(jnp.where(row < 4, a, b))
    while len(packed) % 2:
        packed.append(zero)
    for n in range(0, len(packed), 2):
        blocks.append(jnp.concatenate([packed[n], packed[n + 1]], axis=0))
    return blocks


def pack_kernel(
    place,
    u_ref,
    v_ref,
    f_ref,
    lame_ref,
    shear_ref,
    buoy_ref,
    depth_ref,
    cols_ref,
    amps_ref,
    p_ref,
    c_ref,
    s_ref,
    y0_ref,
    y1_ref,
    x0_ref,
    x1_ref,
    c0_ref,
    c1_ref,
):
    nx, ny, nz = lame_ref.shape
    even_i, even_j, base, total_y = place[0], place[1], place[2], place[3]
    levels = lax.broadcasted_iota(jnp.int32, (ny, nz), 1).astype(F32)
    eye = lax.broadcasted_iota(jnp.int32, (ny, ny), 0) == lax.broadcasted_iota(
        jnp.int32, (ny, ny), 1
    )
    own_y = lax.broadcasted_iota(jnp.int32, (ny, cols_ref.shape[1]), 0)
    depth_all = depth_ref[...].astype(F32)
    for x in range(nx):
        depth = jnp.sum(jnp.where(eye, depth_all[x : x + 1, :], 0.0), axis=1, keepdims=True)
        buoy = STEP_SQUARED * buoy_ref[x]
        mu = jnp.where(levels >= depth, shear_ref[x], 0.0)
        c_ref[0, x] = buoy * mu
        c_ref[1, x] = buoy * (lame_ref[x] + mu)
        here = cols_ref[...] == own_y + (base + x * total_y)
        floor = levels == depth
        drive = []
        for t in range(STEPS):
            amp = jnp.sum(jnp.where(here, amps_ref[0, t : t + 1, :], 0.0), axis=1, keepdims=True)
            drive.append(jnp.where(floor, buoy * amp, 0.0))
        s_ref[0, x] = drive[1]
        s_ref[1, x] = drive[2]
        for k in range(3):
            p = 2.0 * u_ref[0, k, x] - v_ref[0, k, x]
            if k == 2:
                p = p + drive[0]
            p_ref[k, x] = p

    def line(name, k, x):
        if name == "u":
            return u_ref[0, k, x]
        if name == "p":
            return p_ref[k, x]
        if name == "c":
            return c_ref[k, x]
        if name == "s":
            return s_ref[k, x]
        return f_ref[0, k // 3, k % 3, x]

    def column(name, k, y):
        if name == "u":
            return u_ref[0, k, :, y, :]
        if name == "p":
            return p_ref[k, :, y, :]
        if name == "c":
            return c_ref[k, :, y, :]
        if name == "s":
            return s_ref[k, :, y, :]
        return f_ref[0, k // 3, k % 3].astype(F32)[:, y, :]

    for dst, high in ((x0_ref, even_i == 1), (x1_ref, even_i == 0)):
        for n, (name, k, ring, part) in enumerate(UNITS):
            x = jnp.where(high, nx - ring, ring - 1)
            value = line(name, k, x)
            if name == "f":
                dst[n] = value
            elif part == "hi":
                dst[n] = value.astype(BF16)
            else:
                dst[n] = split(value)[1].astype(BF16)

    sides = ([], [])
    for name, k, ring, part in UNITS:
        top = column(name, k, ny - ring)
        low = column(name, k, ring - 1)
        for side, high in ((0, even_j == 1), (1, even_j == 0)):
            value = jnp.where(high, top, low)
            sides[side].append(split(value)[1] if part == "lo" else value)
    for dst, units in ((y0_ref, sides[0]), (y1_ref, sides[1])):
        padded = units + [jnp.zeros_like(units[0])] * (len(units) % 2)
        for n in range(0, len(padded), 2):
            dst[n // 2] = jnp.concatenate([padded[n], padded[n + 1]], axis=0).astype(BF16)
    low = corner_rows(sides[1][:CORNERED], 0)
    top = corner_rows(sides[1][:CORNERED], nx - 3)
    for n in range(CORNER_BLOCKS):
        c0_ref[n] = jnp.where(even_j == 1, low[n], top[n]).astype(BF16)
        c1_ref[n] = jnp.where(even_j == 1, top[n], low[n]).astype(BF16)


def corner_kernel(place, y0_ref, x0_in, x1_in, x0_out, x1_out, stage, sems):
    nx = 8
    even_i = place[0]
    units = []
    for n in range(CORNERED):
        block = y0_ref[n // 2].astype(F32)
        units.append(block[8 * (n % 2) : 8 * (n % 2) + 8])
    low = corner_rows(units, 0)
    top = corner_rows(units, nx - 3)
    for n in range(CORNER_BLOCKS):
        stage[0, n] = jnp.where(even_i == 1, top[n], low[n]).astype(BF16)
        stage[1, n] = jnp.where(even_i == 1, low[n], top[n]).astype(BF16)
    copies = []
    for side, dst in ((0, x0_out), (1, x1_out)):
        copies.append(
            pltpu.make_async_copy(
                stage.at[side], dst.at[pl.ds(FACE_BLOCKS, CORNER_BLOCKS)], sems.at[side]
            )
        )
    for copy in copies:
        copy.start()
    for copy in copies:
        copy.wait()


def main_kernel(
    place,
    u_in,
    p_in,
    c_in,
    s_in,
    f_in,
    x0_in,
    x1_in,
    y0_in,
    y1_in,
    c0_in,
    c1_in,
    out_ref,
    keep_ref,
    u_ref,
    v_ref,
    w_ref,
    p_ref,
    c_ref,
    s_ref,
    f_ref,
    bc_ref,
):
    nx, ny, nz = c_in.shape[1:]
    even_i, even_j = place[0], place[1]
    ok_x1, ok_y1, ok_c0, ok_c1 = place[4], place[5], place[6], place[7]
    wide = u_ref.shape[2]

    for ref in (u_ref, p_ref, c_ref, s_ref, f_ref):
        ref[...] = jnp.zeros_like(ref)
    inner = slice(PAD, PAD + ny)

    refs = {"u": u_ref, "p": p_ref, "c": c_ref, "s": s_ref, "f": f_ref}
    for x in range(nx):
        for k in range(3):
            u_ref[k, RING + x, inner, :] = u_in[0, k, x]
            p_ref[k, RING + x, inner, :] = p_in[k, x]
        for k in range(2):
            c_ref[k, RING + x, inner, :] = c_in[k, x]
        for k in range(2):
            s_ref[k, RING + x, inner, :] = s_in[k, x]
        for k in range(3 * STEPS):
            f_ref[k, RING + x, inner, :] = f_in[0, k // 3, k % 3, x].astype(F32)

    def joined(get):
        n = 0
        while n < len(UNITS):
            name, k, ring, _ = UNITS[n]
            value = get(n)
            if value is None:
                return
            if name != "f" and ring == 1:
                value = value + get(n + 1)
                n += 1
            n += 1
            yield name, k, ring, value

    for src, high, ok in ((x0_in, even_i == 1, None), (x1_in, even_i == 0, ok_x1)):
        for name, k, ring, value in joined(lambda n: src[n].astype(F32)):
            if ok is not None:
                value = jnp.where(ok == 1, value, 0.0)
            x = jnp.where(high, RING + nx - 1 + ring, RING - ring)
            refs[name][k, x, inner, :] = value

    def side(src):
        blocks = [src[n].astype(F32) for n in range(SIDE_BLOCKS)]
        return [blocks[n // 2][8 * (n % 2) : 8 * (n % 2) + 8] for n in range(FACE_BLOCKS)]

    near, far = side(y0_in), side(y1_in)
    far = [jnp.where(ok_y1 == 1, value, 0.0) for value in far]
    top = [jnp.where(even_j == 1, a, b) for a, b in zip(near, far)]
    low = [jnp.where(even_j == 1, b, a) for a, b in zip(near, far)]
    for values, high in ((top, True), (low, False)):
        for name, k, ring, value in joined(lambda n: values[n]):
            y = PAD + ny - 1 + ring if high else PAD - ring
            for x in range(nx):
                refs[name][k, RING + x, y : y + 1, :] = value[x : x + 1]

    def corner(src, first):
        blocks = [src[first + n].astype(F32) for n in range(CORNER_BLOCKS)]

        def get(n):
            if n >= CORNERED:
                return None
            half = blocks[n // 4][8 * (n // 2 % 2) : 8 * (n // 2 % 2) + 8]
            return half[4 * (n % 2) : 4 * (n % 2) + 3]

        return [get(n) for n in range(CORNERED)]

    e0 = corner(x0_in, FACE_BLOCKS)
    e1 = corner(x1_in, FACE_BLOCKS)
    e1 = [jnp.where(ok_x1 == 1, value, 0.0) for value in e1]
    d0 = [jnp.where(ok_c0 == 1, value, 0.0) for value in corner(c0_in, 0)]
    d1 = [jnp.where(ok_c1 == 1, value, 0.0) for value in corner(c1_in, 0)]
    pick = lambda flag, a, b: [jnp.where(flag == 1, s, t) for s, t in zip(a, b)]
    y0_top = pick(even_i, e0, e1)
    y0_low = pick(even_i, e1, e0)
    y1_top = pick(even_j, d1, d0)
    y1_low = pick(even_j, d0, d1)
    for x_high in (True, False):
        near, far = (y0_top, y1_top) if x_high else (y0_low, y1_low)
        for y_high in (True, False):
            values = pick(even_j, near, far) if y_high else pick(even_j, far, near)
            start = RING + nx if x_high else 0
            for name, k, ring, value in joined(lambda n: values[n] if n < CORNERED else None):
                y = PAD + ny - 1 + ring if y_high else PAD - ring
                for row in range(3):
                    away = row + 1 if x_high else 3 - row
                    if away <= {"u": 3, "p": 2, "c": 2, "s": 1}[name]:
                        refs[name][k, start + row, y : y + 1, :] = value[row : row + 1]

    lane = lax.broadcasted_iota(jnp.int32, (wide, nz), 1)

    def beside_y(a):
        return pltpu.roll(a, wide - 1, 0), pltpu.roll(a, 1, 0)

    def beside_z(a):
        return (
            jnp.where(lane == nz - 1, 0.0, pltpu.roll(a, nz - 1, 1)),
            jnp.where(lane == 0, 0.0, pltpu.roll(a, 1, 1)),
        )

    def spread(ref, x):
        yp, ym = beside_y(ref[1, x])
        zp, zm = beside_z(ref[2, x])
        bc_ref[x] = (yp - ym) + (zp - zm)

    def advance(cur, before, after, t, x):
        um = [cur[k, x - 1] for k in range(3)]
        uc = [cur[k, x] for k in range(3)]
        up = [cur[k, x + 1] for k in range(3)]
        ys = [beside_y(uc[k]) for k in range(3)]
        zs = [beside_z(uc[k]) for k in range(3)]
        a = up[0] - um[0]
        b = ys[1][0] - ys[1][1]
        c = zs[2][0] - zs[2][1]
        ac = beside_y(a + c)
        ab = beside_z(a + b)
        cross = (bc_ref[x + 1] - bc_ref[x - 1], ac[0] - ac[1], ab[0] - ab[1])
        rigid, bulk = c_ref[0, x], c_ref[1, x]
        for k in range(3):
            pairs = (um[k] + up[k], ys[k][0] + ys[k][1], zs[k][0] + zs[k][1])
            laplace = pairs[0] + pairs[1] + pairs[2] - 6.0 * uc[k]
            grad_div = pairs[k] - 2.0 * uc[k] + 0.25 * cross[k]
            if t == 0:
                carry = p_ref[k, x]
            else:
                carry = 2.0 * uc[k] - before[k, x]
                if k == 2:
                    carry = carry + s_ref[t - 1, x]
            after(k, x, carry + rigid * laplace + bulk * grad_div)

    def slopes(read, x):
        table = []
        for k in range(3):
            c = read(k, x)
            yp, ym = beside_y(c)
            zp, zm = beside_z(c)
            table.append((read(k, x + 1) - read(k, x - 1), yp - ym, zp - zm))
        return table

    def imprint(cur, t, x):
        ga = slopes(lambda k, r: cur[k, r], x)
        gf = slopes(lambda k, r: f_ref[3 * t + k, r], x)
        div = (ga[0][0] + ga[1][1] + ga[2][2]) * (gf[0][0] + gf[1][1] + gf[2][2])
        both = ga[0][0] * gf[0][0]
        for k in range(3):
            for d in range(3):
                if k + d > 0:
                    both = both + ga[k][d] * gf[k][d]
        both = jnp.where(c_ref[0, x] > 0.0, both, 0.0)
        if t == 0:
            keep_ref[0, x - RING] = div[inner]
            keep_ref[1, x - RING] = both[inner]
        else:
            keep_ref[0, x - RING] += div[inner]
            keep_ref[1, x - RING] += both[inner]

    fields = (u_ref, v_ref, w_ref)
    for t in range(STEPS):
        cur = fields[t]
        before = fields[t - 1]

        @pl.loop(t, 2 * RING + nx - t)
        def _(x):
            spread(cur, x)

        if t < STEPS - 1:
            nxt = fields[t + 1]

            def store(k, x, value):
                nxt[k, x] = value

        else:

            def store(k, x, value):
                out_ref[0, k, x - RING] = value[inner]

        @pl.loop(t + 1, 2 * RING + nx - t - 1)
        def _(x):
            advance(cur, before, store, t, x)

        @pl.loop(RING, RING + nx)
        def _(x):
            imprint(cur, t, x)


def swap_map(mesh_sizes, partner):
    nx, ny, ns = mesh_sizes
    pairs = []
    for i in range(nx):
        for j in range(ny):
            to = partner(i, j)
            if not (0 <= to[0] < nx and 0 <= to[1] < ny):
                to = None
            for s in range(ns):
                here = (i * ny + j) * ns + s
                if to is None:
                    there = (i * ny + j) * ns + ((s ^ 1) if (s ^ 1) < ns else s)
                else:
                    there = (to[0] * ny + to[1]) * ns + s
                pairs.append((here, there))
    return pairs


def body(
    adj_now,
    adj_later,
    forward_field,
    lame_first,
    shear,
    buoyancy,
    seafloor_depth,
    station_columns,
    station_traces,
):
    nx, ny, nz = lame_first.shape
    sizes = tuple(lax.axis_size(axis) for axis in AXES)
    count_x, count_y, count_s = sizes
    i, j, s = (lax.axis_index(axis) for axis in AXES)
    even_i, even_j = (i + 1) % 2, (j + 1) % 2
    total_y = ny * count_y
    x_out = jnp.where(even_i == 1, i - 1, i + 1)
    y_out = jnp.where(even_j == 1, j - 1, j + 1)
    x_c0 = jnp.where(even_j == 1, i - 1, i + 1)
    x_c1 = jnp.where(even_j == 1, i + 1, i - 1)
    inside = lambda v, n: (v >= 0) & (v < n)
    ok_y1 = inside(y_out, count_y)
    place = jnp.stack(
        [
            even_i,
            even_j,
            i * nx * total_y + j * ny,
            total_y + 0 * i,
            inside(x_out, count_x).astype(jnp.int32),
            ok_y1.astype(jnp.int32),
            (ok_y1 & inside(x_c0, count_x)).astype(jnp.int32),
            (ok_y1 & inside(x_c1, count_x)).astype(jnp.int32),
        ]
    ).astype(jnp.int32)

    smem = pl.BlockSpec(memory_space=pltpu.SMEM)
    vmem = pl.BlockSpec(memory_space=pltpu.VMEM)
    anywhere = pl.BlockSpec(memory_space=pl.ANY)
    limit = 30 * 1024 * 1024
    params = pltpu.CompilerParams(vmem_limit_bytes=limit)
    face = jax.ShapeDtypeStruct((FACE_BLOCKS + CORNER_BLOCKS, ny, nz), BF16)
    edge = jax.ShapeDtypeStruct((SIDE_BLOCKS, 2 * nx, nz), BF16)
    corner = jax.ShapeDtypeStruct((CORNER_BLOCKS, 16, nz), BF16)
    grid = lambda n: jax.ShapeDtypeStruct((n, nx, ny, nz), F32)

    carry, coeff, drive, y0, y1, x0, x1, c0, c1 = pl.pallas_call(
        pack_kernel,
        out_shape=(grid(3), grid(2), grid(2), edge, edge, face, face, corner, corner),
        in_specs=[smem] + [vmem] * 9,
        out_specs=(vmem,) * 9,
        compiler_params=params,
        name="pack",
    )(
        place,
        adj_now,
        adj_later,
        forward_field,
        lame_first,
        shear,
        buoyancy,
        seafloor_depth,
        station_columns,
        station_traces,
    )

    def exchange(value, partner):
        return lax.ppermute(value, AXES, swap_map(sizes, partner))

    flip = lambda n: n + 1 if n % 2 == 0 else n - 1
    back = lambda n: n - 1 if n % 2 == 0 else n + 1
    y0 = exchange(y0, lambda a, b: (a, flip(b)))
    x0, x1 = pl.pallas_call(
        corner_kernel,
        out_shape=(face, face),
        in_specs=[smem, vmem, anywhere, anywhere],
        out_specs=(anywhere, anywhere),
        scratch_shapes=[
            pltpu.VMEM((2, CORNER_BLOCKS, 16, nz), BF16),
            pltpu.SemaphoreType.DMA((2,)),
        ],
        input_output_aliases={2: 0, 3: 1},
        compiler_params=params,
        name="corners",
    )(place, y0, x0, x1)
    x0 = exchange(x0, lambda a, b: (flip(a), b))
    x1 = exchange(x1, lambda a, b: (back(a), b))
    y1 = exchange(y1, lambda a, b: (a, back(b)))
    c0 = exchange(c0, lambda a, b: (a - 1 if b % 2 == 0 else a + 1, back(b)))
    c1 = exchange(c1, lambda a, b: (a + 1 if b % 2 == 0 else a - 1, back(b)))

    wide_x, wide_y = nx + 2 * RING, ny + 2 * PAD
    padded = lambda n: pltpu.VMEM((n, wide_x, wide_y, nz), F32)
    final, sums = pl.pallas_call(
        main_kernel,
        out_shape=(jax.ShapeDtypeStruct((1, 3, nx, ny, nz), F32), grid(2)),
        in_specs=[smem] + [vmem] * 11,
        out_specs=(vmem, vmem),
        scratch_shapes=[
            padded(3),
            padded(3),
            padded(3),
            padded(3),
            padded(2),
            padded(2),
            padded(3 * STEPS),
            pltpu.VMEM((wide_x, wide_y, nz), F32),
        ],
        compiler_params=params,
        name="steps",
    )(place, adj_now, carry, coeff, drive, forward_field, x0, x1, y0, y1, c0, c1)

    scale = 0.25 / (adj_now.shape[0] * count_s)
    if count_s == 2:
        half = nz // 2
        mine = lax.dynamic_slice_in_dim(sums, s * half, half, 3)
        theirs = lax.dynamic_slice_in_dim(sums, (1 - s) * half, half, 3)
        theirs = lax.ppermute(theirs, "src", [(0, 1), (1, 0)])
        return final, (mine + theirs) * scale
    summed = lax.psum_scatter(sums, "src", scatter_dimension=3, tiled=True)
    return final, summed * scale


def solution(mesh):
    in_specs = (
        P("src", None, "tx", "ty", None),
        P("src", None, "tx", "ty", None),
        P("src", None, None, "tx", "ty", None),
        P("tx", "ty", None),
        P("tx", "ty", None),
        P("tx", "ty", None),
        P("tx", "ty"),
        P("src", None),
        P("src", None, None),
    )
    out_specs = (P("src", None, "tx", "ty", None), P(None, "tx", "ty", "src"))
    return jax.shard_map(body, mesh=mesh, in_specs=in_specs, out_specs=out_specs, check_vma=False)
```

```python
import jax
import jax.numpy as jnp
from jax import lax
from jax.experimental import pallas as pl
from jax.experimental.pallas import tpu as pltpu
from jax.sharding import PartitionSpec as P

STEPS = 3
STEP_SQUARED = 0.04
RING = 3
PAD = 8
AXES = ("tx", "ty", "src")
F32 = jnp.float32
BF16 = jnp.bfloat16
UNROLL = 8


def halo_units():
    units = []
    for name, count, rings in (("u", 3, 3), ("p", 3, 2), ("c", 2, 2), ("s", 1, 1)):
        for k in range(count):
            for ring in range(1, rings + 1):
                units.append((name, k, ring, "hi"))
                if ring == 1:
                    units.append((name, k, ring, "lo"))
    cornered = len(units)
    for k in range(3 * STEPS):
        units.append(("f", k, 1, "hi"))
    return units, cornered


UNITS, CORNERED = halo_units()
FACE_BLOCKS = len(UNITS)
SIDE_BLOCKS = (len(UNITS) + 1) // 2
CORNER_BLOCKS = ((CORNERED + 1) // 2 * 8 + 15) // 16


def split(value):
    top = value.astype(BF16).astype(F32)
    return top, value - top


def corner_rows(units, first):
    blocks = []
    row = lax.broadcasted_iota(jnp.int32, units[0].shape, 0)
    zero = jnp.zeros_like(units[0])
    packed = []
    for n in range(0, CORNERED, 2):
        a = pltpu.roll(units[n], (8 - first) % 8, 0) if first else units[n]
        b = pltpu.roll(units[n + 1], (8 - first + 4) % 8, 0) if n + 1 < CORNERED else zero
        packed.append(jnp.where(row < 4, a, b))
    while len(packed) % 2:
        packed.append(zero)
    for n in range(0, len(packed), 2):
        blocks.append(jnp.concatenate([packed[n], packed[n + 1]], axis=0))
    return blocks


def pack_kernel(
    place,
    u_in,
    v_in,
    f_in,
    lame_in,
    shear_in,
    buoy_in,
    depth_in,
    cols_in,
    amps_in,
    u_ref,
    f_ref,
    p_ref,
    c_ref,
    s_ref,
    y0_ref,
    y1_ref,
    x0_ref,
    x1_ref,
    c0_ref,
    c1_ref,
    v_ref,
    lame_ref,
    shear_ref,
    buoy_ref,
    depth_ref,
    cols_ref,
    amps_ref,
    sems,
):
    copies = [
        pltpu.make_async_copy(src, dst, sems.at[n])
        for n, (src, dst) in enumerate(
            (
                (depth_in, depth_ref),
                (cols_in, cols_ref),
                (amps_in, amps_ref),
                (buoy_in, buoy_ref),
                (shear_in, shear_ref),
                (lame_in, lame_ref),
                (u_in, u_ref),
                (v_in, v_ref),
                (f_in, f_ref),
            )
        )
    ]
    for copy in copies:
        copy.start()
    for copy in copies:
        copy.wait()
    nx, ny, nz = lame_ref.shape
    even_i, even_j, base, total_y = place[0], place[1], place[2], place[3]
    levels = lax.broadcasted_iota(jnp.int32, (ny, nz), 1).astype(F32)
    eye = lax.broadcasted_iota(jnp.int32, (ny, ny), 0) == lax.broadcasted_iota(
        jnp.int32, (ny, ny), 1
    )
    own_y = lax.broadcasted_iota(jnp.int32, (ny, cols_ref.shape[1]), 0)
    depth_all = depth_ref[...].astype(F32)
    for x in range(nx):
        depth = jnp.sum(jnp.where(eye, depth_all[x : x + 1, :], 0.0), axis=1, keepdims=True)
        buoy = STEP_SQUARED * buoy_ref[x]
        mu = jnp.where(levels >= depth, shear_ref[x], 0.0)
        c_ref[0, x] = buoy * mu
        c_ref[1, x] = buoy * (lame_ref[x] + mu)
        here = cols_ref[...] == own_y + (base + x * total_y)
        floor = levels == depth
        drive = []
        for t in range(STEPS):
            amp = jnp.sum(jnp.where(here, amps_ref[t], 0.0), axis=1, keepdims=True)
            drive.append(jnp.where(floor, buoy * amp, 0.0))
        s_ref[0, x] = drive[1]
        s_ref[1, x] = drive[2]
        for k in range(3):
            p = 2.0 * u_ref[0, k, x] - v_ref[0, k, x]
            if k == 2:
                p = p + drive[0]
            p_ref[k, x] = p

    def line(name, k, x):
        if name == "u":
            return u_ref[0, k, x]
        if name == "p":
            return p_ref[k, x]
        if name == "c":
            return c_ref[k, x]
        if name == "s":
            return s_ref[k, x]
        return f_ref[0, k // 3, k % 3, x]

    def column(name, k, y):
        if name == "u":
            return u_ref[0, k, :, y, :]
        if name == "p":
            return p_ref[k, :, y, :]
        if name == "c":
            return c_ref[k, :, y, :]
        if name == "s":
            return s_ref[k, :, y, :]
        return f_ref[0, k // 3, k % 3].astype(F32)[:, y, :]

    for dst, high in ((x0_ref, even_i == 1), (x1_ref, even_i == 0)):
        for n, (name, k, ring, part) in enumerate(UNITS):
            x = jnp.where(high, nx - ring, ring - 1)
            value = line(name, k, x)
            if name == "f":
                dst[n] = value
            elif part == "hi":
                dst[n] = value.astype(BF16)
            else:
                dst[n] = split(value)[1].astype(BF16)

    sides = ([], [])
    for name, k, ring, part in UNITS:
        top = column(name, k, ny - ring)
        low = column(name, k, ring - 1)
        for side, high in ((0, even_j == 1), (1, even_j == 0)):
            value = jnp.where(high, top, low)
            sides[side].append(split(value)[1] if part == "lo" else value)
    for dst, units in ((y0_ref, sides[0]), (y1_ref, sides[1])):
        padded = units + [jnp.zeros_like(units[0])] * (len(units) % 2)
        for n in range(0, len(padded), 2):
            dst[n // 2] = jnp.concatenate([padded[n], padded[n + 1]], axis=0).astype(BF16)
    low = corner_rows(sides[1][:CORNERED], 0)
    top = corner_rows(sides[1][:CORNERED], nx - 3)
    for n in range(CORNER_BLOCKS):
        c0_ref[n] = jnp.where(even_j == 1, low[n], top[n]).astype(BF16)
        c1_ref[n] = jnp.where(even_j == 1, top[n], low[n]).astype(BF16)


def corner_kernel(place, y0_ref, x0_in, x1_in, x0_out, x1_out, stage, sems):
    nx = 8
    even_i = place[0]
    units = []
    for n in range(CORNERED):
        block = y0_ref[n // 2].astype(F32)
        units.append(block[8 * (n % 2) : 8 * (n % 2) + 8])
    low = corner_rows(units, 0)
    top = corner_rows(units, nx - 3)
    for n in range(CORNER_BLOCKS):
        stage[0, n] = jnp.where(even_i == 1, top[n], low[n]).astype(BF16)
        stage[1, n] = jnp.where(even_i == 1, low[n], top[n]).astype(BF16)
    copies = []
    for side, dst in ((0, x0_out), (1, x1_out)):
        copies.append(
            pltpu.make_async_copy(
                stage.at[side], dst.at[pl.ds(FACE_BLOCKS, CORNER_BLOCKS)], sems.at[side]
            )
        )
    for copy in copies:
        copy.start()
    for copy in copies:
        copy.wait()


def stage_kernel(u_in, p_in, c_in, s_in, f_in, order, u_ref, p_ref, c_ref, s_ref, f_ref, fz_ref):
    del order
    nx, ny, nz = c_in.shape[1:]
    for src, ref in ((u_in, u_ref), (p_in, p_ref), (c_in, c_ref), (s_in, s_ref)):
        lead = (0,) if src is u_in else ()
        for k in range(ref.shape[0]):
            for x in range(ref.shape[1]):
                if RING <= x < RING + nx:
                    ref[k, x, :ny, :] = src[lead + (k, x - RING)]
                    ref[k, x, ny:, :] = jnp.zeros((ref.shape[2] - ny, nz), F32)
                else:
                    ref[k, x] = jnp.zeros(ref.shape[2:], F32)

    @pl.loop(0, nx)
    def _(x):
        for k in range(3 * STEPS):
            value = f_in[0, k // 3, k % 3, x].astype(F32)
            f_ref[k, x + 1, :ny, :] = value
            f_ref[k, x + 1, ny:, :] = jnp.zeros((f_ref.shape[2] - ny, nz), F32)
            up, down = beside_z(value)
            fz_ref[k, x] = up - down


def beside_z(value):
    tiles = [value[:, n : n + 128] for n in range(0, value.shape[1], 128)]
    lane = lax.broadcasted_iota(jnp.int32, tiles[0].shape, 1)
    zero = jnp.zeros_like(tiles[0])
    ups = [pltpu.roll(tile, 127, 1) for tile in tiles] + [zero]
    downs = [zero] + [pltpu.roll(tile, 1, 1) for tile in tiles]
    up = [jnp.where(lane == 127, ups[n + 1], ups[n]) for n in range(len(tiles))]
    down = [jnp.where(lane == 0, downs[n], downs[n + 1]) for n in range(len(tiles))]
    return jnp.concatenate(up, axis=1), jnp.concatenate(down, axis=1)


def beside_y(value):
    return pltpu.roll(value, value.shape[0] - 1, 0), pltpu.roll(value, 1, 0)


def advance_row(t, x, cur, before, p_ref, c_ref, s_ref, zd, zs, rows):
    um = [cur[k, x - 1] for k in range(3)]
    uc = [cur[k, x] for k in range(3)]
    up = [cur[k, x + 1] for k in range(3)]
    dx = [up[k] - um[k] for k in range(3)]
    dz1 = zd[1, x]
    ys = [beside_y(uc[k]) for k in range(3)]
    tilt = [beside_y(value) for value in (dx[1], dx[0] + zd[2, x], dz1)]
    cross = (
        (tilt[0][0] - tilt[0][1]) + (zd[2, x + 1] - zd[2, x - 1]),
        tilt[1][0] - tilt[1][1],
        (tilt[2][0] - tilt[2][1]) + (zd[0, x + 1] - zd[0, x - 1]),
    )
    rigid, bulk = c_ref[0, x, :rows], c_ref[1, x, :rows]
    fresh = []
    for k in range(3):
        pairs = (um[k] + up[k], ys[k][0] + ys[k][1], zs[k, x])
        laplace = pairs[0] + pairs[1] + pairs[2] - 6.0 * uc[k]
        grad_div = pairs[k] - 2.0 * uc[k] + 0.25 * cross[k]
        if t == 0:
            carry = p_ref[k, x, :rows]
        else:
            carry = 2.0 * uc[k][:rows] - before[k, x, :rows]
            if k == 2:
                carry = carry + s_ref[t - 1, x, :rows]
        fresh.append(carry + rigid * laplace[:rows] + bulk * grad_div[:rows])
    return fresh


def imprint_row(t, x, cur, zd, c_ref, f_ref, fz_ref, rows):
    ga, gf = [], []
    for k in range(3):
        yp, ym = beside_y(cur[k, x])
        ga.append(
            (
                cur[k, x + 1, :rows] - cur[k, x - 1, :rows],
                (yp - ym)[:rows],
                zd[k, x, :rows],
            )
        )
        n, r = 3 * t + k, x - RING + 1
        yp, ym = beside_y(f_ref[n, r])
        gf.append(
            (
                f_ref[n, r + 1, :rows] - f_ref[n, r - 1, :rows],
                (yp - ym)[:rows],
                fz_ref[n, x - RING],
            )
        )
    div = (ga[0][0] + ga[1][1] + ga[2][2]) * (gf[0][0] + gf[1][1] + gf[2][2])
    both = ga[0][0] * gf[0][0]
    for k in range(3):
        for d in range(3):
            if k + d > 0:
                both = both + ga[k][d] * gf[k][d]
    return div, jnp.where(c_ref[0, x, :rows] > 0.0, both, 0.0)


def main_kernel(
    place,
    u_in,
    p_in,
    c_in,
    s_in,
    f_in,
    fz_ref,
    x0_in,
    x1_in,
    y0_in,
    y1_in,
    c0_in,
    c1_in,
    u_ref,
    p_ref,
    c_ref,
    s_ref,
    f_ref,
    v_ref,
    w_ref,
    wd_ref,
    ws_ref,
    *outs,
):
    *sums, ud_ref, us_ref, vd_ref, vs_ref, sum_ref = outs
    nx, ny, nz = fz_ref.shape[1:]
    even_i, even_j = place[0], place[1]
    ok_x1, ok_y1, ok_c0, ok_c1 = place[4], place[5], place[6], place[7]
    wide = u_ref.shape[2]
    refs = {"u": u_ref, "p": p_ref, "c": c_ref, "s": s_ref, "f": f_ref}
    start = {"u": RING, "p": RING, "c": RING, "s": RING, "f": 1}

    def joined(get, count):
        n = 0
        while n < count:
            name, k, ring, _ = UNITS[n]
            value = get(n)
            if name != "f" and ring == 1:
                value = value + get(n + 1)
                n += 1
            n += 1
            yield name, k, ring, value

    for src, high, ok in ((x0_in, even_i == 1, None), (x1_in, even_i == 0, ok_x1)):
        for name, k, ring, value in joined(lambda n: src[n].astype(F32), FACE_BLOCKS):
            if ok is not None:
                value = jnp.where(ok == 1, value, 0.0)
            x = jnp.where(high, start[name] + nx - 1 + ring, start[name] - ring)
            refs[name][k, x, :ny, :] = value
            if name == "f":
                refs[name][k, x, ny:, :] = jnp.zeros((wide - ny, nz), F32)

    def side(src):
        blocks = [src[n].astype(F32) for n in range(SIDE_BLOCKS)]
        return [blocks[n // 2][8 * (n % 2) : 8 * (n % 2) + 8] for n in range(FACE_BLOCKS)]

    row_y = lambda high, ring: ny - 1 + ring if high else wide - ring
    near, far = side(y0_in), side(y1_in)
    far = [jnp.where(ok_y1 == 1, value, 0.0) for value in far]
    top = [jnp.where(even_j == 1, a, b) for a, b in zip(near, far)]
    low = [jnp.where(even_j == 1, b, a) for a, b in zip(near, far)]
    for values, high in ((top, True), (low, False)):
        for name, k, ring, value in joined(lambda n: values[n], FACE_BLOCKS):
            y = row_y(high, ring)
            for x in range(nx):
                refs[name][k, start[name] + x, y : y + 1, :] = value[x : x + 1]

    def corner(src, first):
        blocks = [src[first + n].astype(F32) for n in range(CORNER_BLOCKS)]

        def get(n):
            half = blocks[n // 4][8 * (n // 2 % 2) : 8 * (n // 2 % 2) + 8]
            return half[4 * (n % 2) : 4 * (n % 2) + 3]

        return [get(n) for n in range(CORNERED)]

    e0 = corner(x0_in, FACE_BLOCKS)
    e1 = corner(x1_in, FACE_BLOCKS)
    e1 = [jnp.where(ok_x1 == 1, value, 0.0) for value in e1]
    d0 = [jnp.where(ok_c0 == 1, value, 0.0) for value in corner(c0_in, 0)]
    d1 = [jnp.where(ok_c1 == 1, value, 0.0) for value in corner(c1_in, 0)]
    pick = lambda flag, a, b: [jnp.where(flag == 1, s, t) for s, t in zip(a, b)]
    y0_top = pick(even_i, e0, e1)
    y0_low = pick(even_i, e1, e0)
    y1_top = pick(even_j, d1, d0)
    y1_low = pick(even_j, d0, d1)
    for x_high in (True, False):
        near, far = (y0_top, y1_top) if x_high else (y0_low, y1_low)
        for y_high in (True, False):
            values = pick(even_j, near, far) if y_high else pick(even_j, far, near)
            first = RING + nx if x_high else 0
            for name, k, ring, value in joined(lambda n: values[n], CORNERED):
                y = row_y(y_high, ring)
                for row in range(3):
                    away = row + 1 if x_high else 3 - row
                    if away <= {"u": 3, "p": 2, "c": 2, "s": 1}[name]:
                        refs[name][k, first + row, y : y + 1, :] = value[row : row + 1]

    def keep_z(k, x, value, zd, zs):
        up, down = beside_z(value)
        zd[k, x] = up - down
        zs[k, x] = up + down

    @pl.loop(0, 2 * RING + nx, unroll=UNROLL)
    def _(x):
        for k in range(3):
            keep_z(k, x, u_ref[k, x], ud_ref, us_ref)

    fields = ((u_ref, ud_ref, us_ref), (v_ref, vd_ref, vs_ref), (w_ref, wd_ref, ws_ref))
    for t in range(STEPS):
        cur, zd, zs = fields[t]

        def onward(x):
            if t == STEPS - 1:
                return
            nxt, nd, ns = fields[t + 1]
            fresh = advance_row(
                t, x, cur, fields[t - 1][0], p_ref, c_ref, s_ref, zd, zs, wide
            )
            for k in range(3):
                nxt[k, x] = fresh[k]
                keep_z(k, x, fresh[k], nd, ns)

        for x in (*range(t + 1, RING), *range(RING + nx, 2 * RING + nx - t - 1)):
            onward(x)

        @pl.loop(RING, RING + nx, unroll=UNROLL)
        def _(x):
            onward(x)
            terms = imprint_row(t, x, cur, zd, c_ref, f_ref, fz_ref, ny)
            for n in range(2):
                value = terms[n]
                if t > 0:
                    value = value + sum_ref[n, x - RING]
                if t < STEPS - 1:
                    sum_ref[n, x - RING] = value
                elif len(sums) == 1:
                    sums[0][n, x - RING] = value
                else:
                    half = nz // 2
                    first = place[8] == 0
                    sums[0][n, x - RING] = jnp.where(first, value[:, :half], value[:, half:])
                    sums[1][n, x - RING] = jnp.where(first, value[:, half:], value[:, :half])


def last_kernel(w_ref, wd_ref, ws_ref, v_ref, c_ref, s_ref, out_ref):
    nx, ny = out_ref.shape[2:4]

    @pl.loop(RING, RING + nx, unroll=UNROLL)
    def _(x):
        fresh = advance_row(
            STEPS - 1, x, w_ref, v_ref, None, c_ref, s_ref, wd_ref, ws_ref, ny
        )
        for k in range(3):
            out_ref[0, k, x - RING] = fresh[k]


def swap_map(mesh_sizes, partner):
    nx, ny, ns = mesh_sizes
    pairs = []
    for i in range(nx):
        for j in range(ny):
            to = partner(i, j)
            if not (0 <= to[0] < nx and 0 <= to[1] < ny):
                to = None
            for s in range(ns):
                here = (i * ny + j) * ns + s
                if to is None:
                    there = (i * ny + j) * ns + ((s ^ 1) if (s ^ 1) < ns else s)
                else:
                    there = (to[0] * ny + to[1]) * ns + s
                pairs.append((here, there))
    return pairs


def body(
    adj_now,
    adj_later,
    forward_field,
    lame_first,
    shear,
    buoyancy,
    seafloor_depth,
    station_columns,
    station_traces,
):
    nx, ny, nz = lame_first.shape
    sizes = tuple(lax.axis_size(axis) for axis in AXES)
    count_x, count_y, count_s = sizes
    i, j, s = (lax.axis_index(axis) for axis in AXES)
    even_i, even_j = (i + 1) % 2, (j + 1) % 2
    total_y = ny * count_y
    x_out = jnp.where(even_i == 1, i - 1, i + 1)
    y_out = jnp.where(even_j == 1, j - 1, j + 1)
    x_c0 = jnp.where(even_j == 1, i - 1, i + 1)
    x_c1 = jnp.where(even_j == 1, i + 1, i - 1)
    inside = lambda v, n: (v >= 0) & (v < n)
    ok_y1 = inside(y_out, count_y)
    place = jnp.stack(
        [
            even_i,
            even_j,
            i * nx * total_y + j * ny,
            total_y + 0 * i,
            inside(x_out, count_x).astype(jnp.int32),
            ok_y1.astype(jnp.int32),
            (ok_y1 & inside(x_c0, count_x)).astype(jnp.int32),
            (ok_y1 & inside(x_c1, count_x)).astype(jnp.int32),
            s,
        ]
    ).astype(jnp.int32)

    smem = pl.BlockSpec(memory_space=pltpu.SMEM)
    vmem = pl.BlockSpec(memory_space=pltpu.VMEM)
    anywhere = pl.BlockSpec(memory_space=pl.ANY)
    hbm = pl.BlockSpec(memory_space=pltpu.HBM)
    limit = 30 * 1024 * 1024
    params = pltpu.CompilerParams(vmem_limit_bytes=limit)
    face = jax.ShapeDtypeStruct((FACE_BLOCKS + CORNER_BLOCKS, ny, nz), BF16)
    edge = jax.ShapeDtypeStruct((SIDE_BLOCKS, 2 * nx, nz), BF16)
    corner = jax.ShapeDtypeStruct((CORNER_BLOCKS, 16, nz), BF16)
    grid = lambda n: jax.ShapeDtypeStruct((n, nx, ny, nz), F32)

    like = lambda value: jax.ShapeDtypeStruct(value.shape, value.dtype)
    traces = jnp.transpose(station_traces, (1, 0, 2))
    held = (adj_later, lame_first, shear, buoyancy, seafloor_depth, station_columns, traces)
    u0, fwd, carry, coeff, drive, y0, y1, x0, x1, c0, c1 = pl.pallas_call(
        pack_kernel,
        out_shape=(
            like(adj_now),
            like(forward_field),
            grid(3),
            grid(2),
            grid(2),
            edge,
            edge,
            face,
            face,
            corner,
            corner,
        ),
        in_specs=[smem] + [hbm] * 9,
        out_specs=(vmem,) * 11,
        scratch_shapes=[pltpu.VMEM(value.shape, value.dtype) for value in held]
        + [pltpu.SemaphoreType.DMA((9,))],
        compiler_params=params,
        name="pack",
    )(place, adj_now, adj_later, forward_field, *held[1:])

    def exchange(value, partner):
        return lax.ppermute(value, AXES, swap_map(sizes, partner))

    flip = lambda n: n + 1 if n % 2 == 0 else n - 1
    back = lambda n: n - 1 if n % 2 == 0 else n + 1
    y0 = exchange(y0, lambda a, b: (a, flip(b)))
    x0, x1 = pl.pallas_call(
        corner_kernel,
        out_shape=(face, face),
        in_specs=[smem, vmem, anywhere, anywhere],
        out_specs=(anywhere, anywhere),
        scratch_shapes=[
            pltpu.VMEM((2, CORNER_BLOCKS, 16, nz), BF16),
            pltpu.SemaphoreType.DMA((2,)),
        ],
        input_output_aliases={2: 0, 3: 1},
        compiler_params=params,
        name="corners",
    )(place, y0, x0, x1)
    wide_x, wide_y = nx + 2 * RING, ny + PAD
    padded = lambda n, x=wide_x: jax.ShapeDtypeStruct((n, x, wide_y, nz), F32)
    tile = (padded(3), padded(3), padded(2), padded(2), padded(3 * STEPS, nx + 2))
    u0, carry, coeff, drive, fwd, fwd_z = pl.pallas_call(
        stage_kernel,
        out_shape=(*tile, grid(3 * STEPS)),
        in_specs=[vmem] * 5 + [anywhere],
        out_specs=(vmem,) * 6,
        compiler_params=params,
        name="stage",
    )(u0, carry, coeff, drive, fwd, x0)

    x0 = exchange(x0, lambda a, b: (flip(a), b))
    x1 = exchange(x1, lambda a, b: (back(a), b))
    y1 = exchange(y1, lambda a, b: (a, back(b)))
    c0 = exchange(c0, lambda a, b: (a - 1 if b % 2 == 0 else a + 1, back(b)))
    c1 = exchange(c1, lambda a, b: (a + 1 if b % 2 == 0 else a - 1, back(b)))

    half = jax.ShapeDtypeStruct((2, nx, ny, nz // 2), F32)
    sums = (half, half) if count_s == 2 else (grid(2),)
    scratch = lambda value: pltpu.VMEM(value.shape, value.dtype)
    outs = pl.pallas_call(
        main_kernel,
        out_shape=(*tile, *(padded(3),) * 4, *sums),
        in_specs=[smem] + [vmem] * 12,
        out_specs=(vmem,) * (9 + len(sums)),
        scratch_shapes=[scratch(padded(3))] * 4 + [scratch(grid(2))],
        input_output_aliases={n + 1: n for n in range(5)},
        compiler_params=params,
        name="steps",
    )(place, u0, carry, coeff, drive, fwd, fwd_z, x0, x1, y0, y1, c0, c1)
    coeff, drive = outs[2:4]
    u1, u2, u2_d, u2_s = outs[5:9]
    sums = outs[9:]

    scale = 0.25 / (adj_now.shape[0] * count_s)
    if count_s == 2:
        theirs = lax.ppermute(sums[1], "src", [(0, 1), (1, 0)])
        summed = sums[0] + theirs
    else:
        summed = lax.psum_scatter(sums[0], "src", scatter_dimension=3, tiled=True)
    final = pl.pallas_call(
        last_kernel,
        out_shape=like(adj_now),
        in_specs=[vmem] * 6,
        out_specs=vmem,
        compiler_params=params,
        name="last",
    )(u2, u2_d, u2_s, u1, coeff, drive)
    return final, summed * scale


def solution(mesh):
    in_specs = (
        P("src", None, "tx", "ty", None),
        P("src", None, "tx", "ty", None),
        P("src", None, None, "tx", "ty", None),
        P("tx", "ty", None),
        P("tx", "ty", None),
        P("tx", "ty", None),
        P("tx", "ty"),
        P("src", None),
        P("src", None, None),
    )
    out_specs = (P("src", None, "tx", "ty", None), P(None, "tx", "ty", "src"))
    return jax.shard_map(body, mesh=mesh, in_specs=in_specs, out_specs=out_specs, check_vma=False)
```

```python
import jax
import jax.numpy as jnp
from jax import lax
from jax.experimental import pallas as pl
from jax.experimental.pallas import tpu as pltpu
from jax.sharding import PartitionSpec as P

STEPS = 3
STEP_SQUARED = 0.04
RING = 3
PAD = 8
AXES = ("tx", "ty", "src")
F32 = jnp.float32
BF16 = jnp.bfloat16
UNROLL = 8
PACK_VMEM = 30 * 1024 * 1024


def halo_units():
    units = []
    for name, count, rings in (("u", 3, 3), ("p", 3, 2), ("c", 2, 2), ("s", 1, 1)):
        for k in range(count):
            for ring in range(1, rings + 1):
                units.append((name, k, ring, "hi"))
                if ring == 1:
                    units.append((name, k, ring, "lo"))
    cornered = len(units)
    for k in range(3 * STEPS):
        units.append(("f", k, 1, "hi"))
    return units, cornered


UNITS, CORNERED = halo_units()
FACE_BLOCKS = len(UNITS)
SIDE_BLOCKS = (len(UNITS) + 1) // 2
CORNER_BLOCKS = ((CORNERED + 1) // 2 * 8 + 15) // 16


def position():
    i, j, s = (lax.axis_index(axis) for axis in AXES)
    return (i + 1) % 2, (j + 1) % 2, i, j, s


def split(value):
    top = value.astype(BF16).astype(F32)
    return top, value - top


def corner_rows(units, first):
    blocks = []
    row = lax.broadcasted_iota(jnp.int32, units[0].shape, 0)
    zero = jnp.zeros_like(units[0])
    packed = []
    for n in range(0, CORNERED, 2):
        a = pltpu.roll(units[n], (8 - first) % 8, 0) if first else units[n]
        b = pltpu.roll(units[n + 1], (8 - first + 4) % 8, 0) if n + 1 < CORNERED else zero
        packed.append(jnp.where(row < 4, a, b))
    while len(packed) % 2:
        packed.append(zero)
    for n in range(0, len(packed), 2):
        blocks.append(jnp.concatenate([packed[n], packed[n + 1]], axis=0))
    return blocks


def pack_kernel(
    u_in,
    v_in,
    f_in,
    lame_in,
    shear_in,
    buoy_in,
    depth_in,
    cols_in,
    amps_in,
    u_ref,
    f_ref,
    p_ref,
    c_ref,
    s_ref,
    y0_ref,
    y1_ref,
    x0_ref,
    x1_ref,
    c0_ref,
    c1_ref,
    e0_ref,
    e1_ref,
    v_ref,
    lame_ref,
    shear_ref,
    buoy_ref,
    depth_ref,
    cols_ref,
    amps_ref,
    sems,
):
    copies = [
        pltpu.make_async_copy(src, dst, sems.at[n])
        for n, (src, dst) in enumerate(
            (
                (depth_in, depth_ref),
                (cols_in, cols_ref),
                (amps_in, amps_ref),
                (buoy_in, buoy_ref),
                (shear_in, shear_ref),
                (lame_in, lame_ref),
                (u_in, u_ref),
                (v_in, v_ref),
                (f_in, f_ref),
            )
        )
    ]
    for copy in copies:
        copy.start()
    for copy in copies:
        copy.wait()
    nx, ny, nz = lame_ref.shape
    even_i, even_j, i, j, _ = position()
    total_y = ny * lax.axis_size("ty")
    base = i * nx * total_y + j * ny
    levels = lax.broadcasted_iota(jnp.int32, (ny, nz), 1).astype(F32)
    eye = lax.broadcasted_iota(jnp.int32, (ny, ny), 0) == lax.broadcasted_iota(
        jnp.int32, (ny, ny), 1
    )
    own_y = lax.broadcasted_iota(jnp.int32, (ny, cols_ref.shape[1]), 0)
    depth_all = depth_ref[...].astype(F32)
    for x in range(nx):
        depth = jnp.sum(jnp.where(eye, depth_all[x : x + 1, :], 0.0), axis=1, keepdims=True)
        buoy = STEP_SQUARED * buoy_ref[x]
        mu = jnp.where(levels >= depth, shear_ref[x], 0.0)
        c_ref[0, x] = buoy * mu
        c_ref[1, x] = buoy * (lame_ref[x] + mu)
        here = cols_ref[...] == own_y + (base + x * total_y)
        floor = levels == depth
        drive = []
        for t in range(STEPS):
            amp = jnp.sum(jnp.where(here, amps_ref[t], 0.0), axis=1, keepdims=True)
            drive.append(jnp.where(floor, buoy * amp, 0.0))
        s_ref[0, x] = drive[1]
        s_ref[1, x] = drive[2]
        for k in range(3):
            p = 2.0 * u_ref[0, k, x] - v_ref[0, k, x]
            if k == 2:
                p = p + drive[0]
            p_ref[k, x] = p

    def line(name, k, x):
        if name == "u":
            return u_ref[0, k, x]
        if name == "p":
            return p_ref[k, x]
        if name == "c":
            return c_ref[k, x]
        if name == "s":
            return s_ref[k, x]
        return f_ref[0, k // 3, k % 3, x]

    def column(name, k, y):
        if name == "u":
            return u_ref[0, k, :, y, :]
        if name == "p":
            return p_ref[k, :, y, :]
        if name == "c":
            return c_ref[k, :, y, :]
        if name == "s":
            return s_ref[k, :, y, :]
        return f_ref[0, k // 3, k % 3].astype(F32)[:, y, :]

    for dst, high in ((x0_ref, even_i == 1), (x1_ref, even_i == 0)):
        for n, (name, k, ring, part) in enumerate(UNITS):
            x = jnp.where(high, nx - ring, ring - 1)
            value = line(name, k, x)
            if name == "f":
                dst[n] = value
            elif part == "hi":
                dst[n] = value.astype(BF16)
            else:
                dst[n] = split(value)[1].astype(BF16)

    sides = ([], [])
    for name, k, ring, part in UNITS:
        top = column(name, k, ny - ring)
        low = column(name, k, ring - 1)
        for side, high in ((0, even_j == 1), (1, even_j == 0)):
            value = jnp.where(high, top, low)
            sides[side].append(split(value)[1] if part == "lo" else value)
    for dst, units in ((y0_ref, sides[0]), (y1_ref, sides[1])):
        padded = units + [jnp.zeros_like(units[0])] * (len(units) % 2)
        for n in range(0, len(padded), 2):
            dst[n // 2] = jnp.concatenate([padded[n], padded[n + 1]], axis=0).astype(BF16)
    for units, flags, first, second in (
        (sides[0], even_i, e0_ref, e1_ref),
        (sides[1], 1 - even_j, c0_ref, c1_ref),
    ):
        low = corner_rows(units[:CORNERED], 0)
        top = corner_rows(units[:CORNERED], nx - 3)
        for n in range(CORNER_BLOCKS):
            first[n] = jnp.where(flags == 1, top[n], low[n]).astype(BF16)
            second[n] = jnp.where(flags == 1, low[n], top[n]).astype(BF16)


def stage_kernel(u_in, p_in, c_in, s_in, f_in, u_ref, p_ref, c_ref, s_ref, f_ref, fz_ref):
    nx, ny, nz = c_in.shape[1:]
    for src, ref in ((u_in, u_ref), (p_in, p_ref), (c_in, c_ref), (s_in, s_ref)):
        lead = (0,) if src is u_in else ()
        for k in range(ref.shape[0]):
            for x in range(ref.shape[1]):
                if RING <= x < RING + nx:
                    ref[k, x, :ny, :] = src[lead + (k, x - RING)]
                    ref[k, x, ny:, :] = jnp.zeros((ref.shape[2] - ny, nz), F32)
                else:
                    ref[k, x] = jnp.zeros(ref.shape[2:], F32)

    @pl.loop(0, nx)
    def _(x):
        for k in range(3 * STEPS):
            value = f_in[0, k // 3, k % 3, x].astype(F32)
            f_ref[k, x + 1, :ny, :] = value
            f_ref[k, x + 1, ny:, :] = jnp.zeros((f_ref.shape[2] - ny, nz), F32)
            up, down = beside_z(value)
            fz_ref[k, x] = up - down


def beside_z(value):
    tiles = [value[:, n : n + 128] for n in range(0, value.shape[1], 128)]
    lane = lax.broadcasted_iota(jnp.int32, tiles[0].shape, 1)
    zero = jnp.zeros_like(tiles[0])
    ups = [pltpu.roll(tile, 127, 1) for tile in tiles] + [zero]
    downs = [zero] + [pltpu.roll(tile, 1, 1) for tile in tiles]
    up = [jnp.where(lane == 127, ups[n + 1], ups[n]) for n in range(len(tiles))]
    down = [jnp.where(lane == 0, downs[n], downs[n + 1]) for n in range(len(tiles))]
    return jnp.concatenate(up, axis=1), jnp.concatenate(down, axis=1)


def beside_y(value):
    return pltpu.roll(value, value.shape[0] - 1, 0), pltpu.roll(value, 1, 0)


def advance_row(t, x, cur, before, p_ref, c_ref, s_ref, zd, zs, rows):
    um = [cur[k, x - 1] for k in range(3)]
    uc = [cur[k, x] for k in range(3)]
    up = [cur[k, x + 1] for k in range(3)]
    dx = [up[k] - um[k] for k in range(3)]
    dz1 = zd[1, x]
    ys = [beside_y(uc[k]) for k in range(3)]
    tilt = [beside_y(value) for value in (dx[1], dx[0] + zd[2, x], dz1)]
    cross = (
        (tilt[0][0] - tilt[0][1]) + (zd[2, x + 1] - zd[2, x - 1]),
        tilt[1][0] - tilt[1][1],
        (tilt[2][0] - tilt[2][1]) + (zd[0, x + 1] - zd[0, x - 1]),
    )
    rigid, bulk = c_ref[0, x, :rows], c_ref[1, x, :rows]
    fresh = []
    for k in range(3):
        pairs = (um[k] + up[k], ys[k][0] + ys[k][1], zs[k, x])
        laplace = pairs[0] + pairs[1] + pairs[2] - 6.0 * uc[k]
        grad_div = pairs[k] - 2.0 * uc[k] + 0.25 * cross[k]
        if t == 0:
            carry = p_ref[k, x, :rows]
        else:
            carry = 2.0 * uc[k][:rows] - before[k, x, :rows]
            if k == 2:
                carry = carry + s_ref[t - 1, x, :rows]
        fresh.append(carry + rigid * laplace[:rows] + bulk * grad_div[:rows])
    return fresh


def imprint_row(t, x, cur, zd, c_ref, f_ref, fz_ref, rows):
    ga, gf = [], []
    for k in range(3):
        yp, ym = beside_y(cur[k, x])
        ga.append(
            (
                cur[k, x + 1, :rows] - cur[k, x - 1, :rows],
                (yp - ym)[:rows],
                zd[k, x, :rows],
            )
        )
        n, r = 3 * t + k, x - RING + 1
        yp, ym = beside_y(f_ref[n, r])
        gf.append(
            (
                f_ref[n, r + 1, :rows] - f_ref[n, r - 1, :rows],
                (yp - ym)[:rows],
                fz_ref[n, x - RING],
            )
        )
    div = (ga[0][0] + ga[1][1] + ga[2][2]) * (gf[0][0] + gf[1][1] + gf[2][2])
    both = ga[0][0] * gf[0][0]
    for k in range(3):
        for d in range(3):
            if k + d > 0:
                both = both + ga[k][d] * gf[k][d]
    return div, jnp.where(c_ref[0, x, :rows] > 0.0, both, 0.0)


def main_kernel(
    u_in,
    p_in,
    c_in,
    s_in,
    f_in,
    fz_ref,
    x0_in,
    x1_in,
    y0_in,
    y1_in,
    c0_in,
    c1_in,
    e0_in,
    e1_in,
    u_ref,
    p_ref,
    c_ref,
    s_ref,
    f_ref,
    v_ref,
    w_ref,
    wd_ref,
    ws_ref,
    *outs,
):
    *sums, ud_ref, us_ref, vd_ref, vs_ref, sum_ref = outs
    nx, ny, nz = fz_ref.shape[1:]
    even_i, even_j, i, j, s = position()
    inside = lambda v, axis: (v >= 0) & (v < lax.axis_size(axis))
    ok_x1 = inside(jnp.where(even_i == 1, i - 1, i + 1), "tx")
    ok_y1 = inside(jnp.where(even_j == 1, j - 1, j + 1), "ty")
    ok_c0 = ok_y1 & inside(jnp.where(even_j == 1, i - 1, i + 1), "tx")
    ok_c1 = ok_y1 & inside(jnp.where(even_j == 1, i + 1, i - 1), "tx")
    wide = u_ref.shape[2]
    refs = {"u": u_ref, "p": p_ref, "c": c_ref, "s": s_ref, "f": f_ref}
    start = {"u": RING, "p": RING, "c": RING, "s": RING, "f": 1}

    def joined(get, count):
        n = 0
        while n < count:
            name, k, ring, _ = UNITS[n]
            value = get(n)
            if name != "f" and ring == 1:
                value = value + get(n + 1)
                n += 1
            n += 1
            yield name, k, ring, value

    for src, high, ok in ((x0_in, even_i == 1, None), (x1_in, even_i == 0, ok_x1)):
        for name, k, ring, value in joined(lambda n: src[n].astype(F32), FACE_BLOCKS):
            if ok is not None:
                value = jnp.where(ok, value, 0.0)
            x = jnp.where(high, start[name] + nx - 1 + ring, start[name] - ring)
            refs[name][k, x, :ny, :] = value
            if name == "f":
                refs[name][k, x, ny:, :] = jnp.zeros((wide - ny, nz), F32)

    def side(src):
        blocks = [src[n].astype(F32) for n in range(SIDE_BLOCKS)]
        return [blocks[n // 2][8 * (n % 2) : 8 * (n % 2) + 8] for n in range(FACE_BLOCKS)]

    row_y = lambda high, ring: ny - 1 + ring if high else wide - ring
    near, far = side(y0_in), side(y1_in)
    far = [jnp.where(ok_y1, value, 0.0) for value in far]
    top = [jnp.where(even_j == 1, a, b) for a, b in zip(near, far)]
    low = [jnp.where(even_j == 1, b, a) for a, b in zip(near, far)]
    for values, high in ((top, True), (low, False)):
        for name, k, ring, value in joined(lambda n: values[n], FACE_BLOCKS):
            y = row_y(high, ring)
            for x in range(nx):
                refs[name][k, start[name] + x, y : y + 1, :] = value[x : x + 1]

    def corner(src):
        blocks = [src[n].astype(F32) for n in range(CORNER_BLOCKS)]

        def get(n):
            half = blocks[n // 4][8 * (n // 2 % 2) : 8 * (n // 2 % 2) + 8]
            return half[4 * (n % 2) : 4 * (n % 2) + 3]

        return [get(n) for n in range(CORNERED)]

    e0 = corner(e0_in)
    e1 = corner(e1_in)
    e1 = [jnp.where(ok_x1, value, 0.0) for value in e1]
    d0 = [jnp.where(ok_c0, value, 0.0) for value in corner(c0_in)]
    d1 = [jnp.where(ok_c1, value, 0.0) for value in corner(c1_in)]
    pick = lambda flag, a, b: [jnp.where(flag == 1, s, t) for s, t in zip(a, b)]
    y0_top = pick(even_i, e0, e1)
    y0_low = pick(even_i, e1, e0)
    y1_top = pick(even_j, d1, d0)
    y1_low = pick(even_j, d0, d1)
    for x_high in (True, False):
        near, far = (y0_top, y1_top) if x_high else (y0_low, y1_low)
        for y_high in (True, False):
            values = pick(even_j, near, far) if y_high else pick(even_j, far, near)
            first = RING + nx if x_high else 0
            for name, k, ring, value in joined(lambda n: values[n], CORNERED):
                y = row_y(y_high, ring)
                for row in range(3):
                    away = row + 1 if x_high else 3 - row
                    if away <= {"u": 3, "p": 2, "c": 2, "s": 1}[name]:
                        refs[name][k, first + row, y : y + 1, :] = value[row : row + 1]

    def keep_z(k, x, value, zd, zs):
        up, down = beside_z(value)
        zd[k, x] = up - down
        zs[k, x] = up + down

    @pl.loop(0, 2 * RING + nx, unroll=UNROLL)
    def _(x):
        for k in range(3):
            keep_z(k, x, u_ref[k, x], ud_ref, us_ref)

    fields = ((u_ref, ud_ref, us_ref), (v_ref, vd_ref, vs_ref), (w_ref, wd_ref, ws_ref))
    for t in range(STEPS):
        cur, zd, zs = fields[t]

        def onward(x):
            if t == STEPS - 1:
                return
            nxt, nd, ns = fields[t + 1]
            fresh = advance_row(
                t, x, cur, fields[t - 1][0], p_ref, c_ref, s_ref, zd, zs, wide
            )
            for k in range(3):
                nxt[k, x] = fresh[k]
                keep_z(k, x, fresh[k], nd, ns)

        for x in (*range(t + 1, RING), *range(RING + nx, 2 * RING + nx - t - 1)):
            onward(x)

        @pl.loop(RING, RING + nx, unroll=UNROLL)
        def _(x):
            onward(x)
            terms = imprint_row(t, x, cur, zd, c_ref, f_ref, fz_ref, ny)
            for n in range(2):
                value = terms[n]
                if t > 0:
                    value = value + sum_ref[n, x - RING]
                if t < STEPS - 1:
                    sum_ref[n, x - RING] = value
                elif len(sums) == 1:
                    sums[0][n, x - RING] = value
                else:
                    half = nz // 2
                    first = s == 0
                    sums[0][n, x - RING] = jnp.where(first, value[:, :half], value[:, half:])
                    sums[1][n, x - RING] = jnp.where(first, value[:, half:], value[:, :half])


def last_kernel(w_ref, wd_ref, ws_ref, v_ref, c_ref, s_ref, out_ref):
    nx, ny = out_ref.shape[2:4]

    @pl.loop(RING, RING + nx, unroll=UNROLL)
    def _(x):
        fresh = advance_row(
            STEPS - 1, x, w_ref, v_ref, None, c_ref, s_ref, wd_ref, ws_ref, ny
        )
        for k in range(3):
            out_ref[0, k, x - RING] = fresh[k]


def swap_map(sizes, partner, spare):
    nx, ny, ns = sizes
    pairs = []
    for i in range(nx):
        for j in range(ny):
            a, b = partner(i, j)
            for s in range(ns):
                to = (a, b, s)
                if not (0 <= a < nx and 0 <= b < ny):
                    to = (i, j ^ 1, s) if spare == "y" else (i, j, s ^ 1 if s ^ 1 < ns else s)
                pairs.append(((i * ny + j) * ns + s, (to[0] * ny + to[1]) * ns + to[2]))
    return pairs


def body(
    adj_now,
    adj_later,
    forward_field,
    lame_first,
    shear,
    buoyancy,
    seafloor_depth,
    station_columns,
    station_traces,
):
    nx, ny, nz = lame_first.shape
    sizes = tuple(lax.axis_size(axis) for axis in AXES)
    count_s = sizes[2]
    vmem = pl.BlockSpec(memory_space=pltpu.VMEM)
    anywhere = pl.BlockSpec(memory_space=pl.ANY)
    limit = 30 * 1024 * 1024
    params = pltpu.CompilerParams(vmem_limit_bytes=limit)
    face = jax.ShapeDtypeStruct((FACE_BLOCKS, ny, nz), BF16)
    edge = jax.ShapeDtypeStruct((SIDE_BLOCKS, 2 * nx, nz), BF16)
    corner = jax.ShapeDtypeStruct((CORNER_BLOCKS, 16, nz), BF16)
    grid = lambda n: jax.ShapeDtypeStruct((n, nx, ny, nz), F32)

    like = lambda value: jax.ShapeDtypeStruct(value.shape, value.dtype)
    traces = jnp.transpose(station_traces, (1, 0, 2))
    held = (adj_later, lame_first, shear, buoyancy, seafloor_depth, station_columns, traces)
    u0, fwd, carry, coeff, drive, y0, y1, x0, x1, c0, c1, e0, e1 = pl.pallas_call(
        pack_kernel,
        out_shape=(
            like(adj_now),
            like(forward_field),
            grid(3),
            grid(2),
            grid(2),
            edge,
            edge,
            face,
            face,
            *(corner,) * 4,
        ),
        in_specs=[anywhere] * 9,
        out_specs=(vmem,) * 13,
        scratch_shapes=[pltpu.VMEM(value.shape, value.dtype) for value in held]
        + [pltpu.SemaphoreType.DMA((9,))],
        compiler_params=pltpu.CompilerParams(vmem_limit_bytes=PACK_VMEM),
        name="pack",
    )(*(pltpu.with_memory_space_constraint(v, pltpu.HBM) for v in (adj_now, adj_later, forward_field, *held[1:])))

    wide_x, wide_y = nx + 2 * RING, ny + PAD
    padded = lambda n, x=wide_x: jax.ShapeDtypeStruct((n, x, wide_y, nz), F32)
    tile = (padded(3), padded(3), padded(2), padded(2), padded(3 * STEPS, nx + 2))
    u0, carry, coeff, drive, fwd, fwd_z = pl.pallas_call(
        stage_kernel,
        out_shape=(*tile, grid(3 * STEPS)),
        in_specs=[vmem] * 5,
        out_specs=(vmem,) * 6,
        compiler_params=params,
        name="stage",
    )(u0, carry, coeff, drive, fwd)

    def exchange(value, partner, spare="s"):
        return lax.ppermute(value, AXES, swap_map(sizes, partner, spare))

    flip = lambda n: n + 1 if n % 2 == 0 else n - 1
    back = lambda n: n - 1 if n % 2 == 0 else n + 1
    y0 = exchange(y0, lambda a, b: (a, flip(b)))
    e0 = exchange(e0, lambda a, b: (flip(a), flip(b)))
    e1 = exchange(e1, lambda a, b: (back(a), flip(b)), "y")
    x0, x1, y1, c0, c1, y0, e0, e1 = lax.optimization_barrier((x0, x1, y1, c0, c1, y0, e0, e1))
    x0 = exchange(x0, lambda a, b: (flip(a), b))
    x1 = exchange(x1, lambda a, b: (back(a), b), "y")
    y1 = exchange(y1, lambda a, b: (a, back(b)))
    c0 = exchange(c0, lambda a, b: (a - 1 if b % 2 == 0 else a + 1, back(b)))
    c1 = exchange(c1, lambda a, b: (a + 1 if b % 2 == 0 else a - 1, back(b)))

    half = jax.ShapeDtypeStruct((2, nx, ny, nz // 2), F32)
    sums = (half, half) if count_s == 2 else (grid(2),)
    scratch = lambda value: pltpu.VMEM(value.shape, value.dtype)
    outs = pl.pallas_call(
        main_kernel,
        out_shape=(*tile, *(padded(3),) * 4, *sums),
        in_specs=[vmem] * 14,
        out_specs=(vmem,) * (9 + len(sums)),
        scratch_shapes=[scratch(padded(3))] * 4 + [scratch(grid(2))],
        input_output_aliases={n: n for n in range(5)},
        compiler_params=params,
        name="steps",
    )(u0, carry, coeff, drive, fwd, fwd_z, x0, x1, y0, y1, c0, c1, e0, e1)
    coeff, drive = outs[2:4]
    u1, u2, u2_d, u2_s = outs[5:9]
    sums = outs[9:]

    scale = 0.25 / (adj_now.shape[0] * count_s)
    if count_s == 2:
        theirs = lax.ppermute(sums[1], "src", [(0, 1), (1, 0)])
        summed = sums[0] + theirs
    else:
        summed = lax.psum_scatter(sums[0], "src", scatter_dimension=3, tiled=True)
    final = pl.pallas_call(
        last_kernel,
        out_shape=like(adj_now),
        in_specs=[vmem] * 6,
        out_specs=vmem,
        compiler_params=params,
        name="last",
    )(u2, u2_d, u2_s, u1, coeff, drive)
    return final, summed * scale


def solution(mesh):
    in_specs = (
        P("src", None, "tx", "ty", None),
        P("src", None, "tx", "ty", None),
        P("src", None, None, "tx", "ty", None),
        P("tx", "ty", None),
        P("tx", "ty", None),
        P("tx", "ty", None),
        P("tx", "ty"),
        P("src", None),
        P("src", None, None),
    )
    out_specs = (P("src", None, "tx", "ty", None), P(None, "tx", "ty", "src"))
    return jax.shard_map(body, mesh=mesh, in_specs=in_specs, out_specs=out_specs, check_vma=False)
```

```python
import jax
import jax.numpy as jnp
from jax import lax
from jax.experimental import pallas as pl
from jax.experimental.pallas import tpu as pltpu
from jax.sharding import PartitionSpec as P

STEPS = 3
STEP_SQUARED = 0.04
RING = 3
PAD = 8
AXES = ("tx", "ty", "src")
F32 = jnp.float32
BF16 = jnp.bfloat16
UNROLL = 8


def halo_units():
    units = []
    for name, count, rings in (("u", 3, 3), ("p", 3, 2), ("c", 2, 2), ("s", 1, 1)):
        for k in range(count):
            for ring in range(1, rings + 1):
                units.append((name, k, ring, "hi"))
                if ring == 1:
                    units.append((name, k, ring, "lo"))
    for k in range(3 * STEPS):
        units.append(("f", k, 1, "hi"))
    return units


def corner_entries():
    entries = []
    for name, count, rings in (("u", 3, 3), ("p", 3, 2), ("c", 2, 2), ("s", 1, 1)):
        for k in range(count):
            for ring_x in range(1, rings + 1):
                for ring_y in range(1, rings + 1):
                    entries.append((name, k, ring_x, ring_y, "hi"))
                    if ring_x == 1 and ring_y == 1:
                        entries.append((name, k, ring_x, ring_y, "lo"))
    return entries


UNITS = halo_units()
CORNERS = corner_entries()
FACE_BLOCKS = len(UNITS)
SIDE_BLOCKS = (len(UNITS) + 1) // 2
CORNER_BLOCKS = (len(CORNERS) + 15) // 16


def position():
    i, j, s = (lax.axis_index(axis) for axis in AXES)
    return (i + 1) % 2, (j + 1) % 2, i, j, s


def split(value):
    top = value.astype(BF16).astype(F32)
    return top, value - top


def corner_blocks(units, high):
    at = {unit: value for unit, value in zip(UNITS, units)}
    nx = units[0].shape[0]
    rows = []
    for name, k, ring_x, ring_y, part in CORNERS:
        unit = at[name, k, ring_y, part]
        rows.append(
            jnp.where(high, unit[nx - ring_x : nx - ring_x + 1], unit[ring_x - 1 : ring_x])
        )
    rows += [jnp.zeros_like(rows[0])] * (-len(rows) % 16)
    return [
        jnp.concatenate(rows[n : n + 16], axis=0).astype(BF16) for n in range(0, len(rows), 16)
    ]


def side_units(ref, nx):
    blocks = [ref[n].astype(F32) for n in range(SIDE_BLOCKS)]
    return [blocks[n // 2][nx * (n % 2) : nx * (n % 2) + nx] for n in range(FACE_BLOCKS)]


def pack_kernel(
    u_in,
    v_in,
    f_in,
    lame_in,
    shear_in,
    buoy_in,
    depth_in,
    cols_in,
    amps_in,
    u_ref,
    f_ref,
    p_ref,
    c_ref,
    s_ref,
    y0_ref,
    y1_ref,
    c0_ref,
    c1_ref,
    v_ref,
    lame_ref,
    shear_ref,
    buoy_ref,
    depth_ref,
    cols_ref,
    amps_ref,
    sems,
):
    copies = [
        pltpu.make_async_copy(src, dst, sems.at[n])
        for n, (src, dst) in enumerate(
            (
                (depth_in, depth_ref),
                (cols_in, cols_ref),
                (amps_in, amps_ref),
                (buoy_in, buoy_ref),
                (shear_in, shear_ref),
                (lame_in, lame_ref),
                (u_in, u_ref),
                (v_in, v_ref),
                (f_in, f_ref),
            )
        )
    ]
    for copy in copies:
        copy.start()
    for copy in copies:
        copy.wait()
    nx, ny, nz = lame_ref.shape
    even_i, even_j, i, j, _ = position()
    total_y = ny * lax.axis_size("ty")
    base = i * nx * total_y + j * ny
    levels = lax.broadcasted_iota(jnp.int32, (ny, nz), 1).astype(F32)
    eye = lax.broadcasted_iota(jnp.int32, (ny, ny), 0) == lax.broadcasted_iota(
        jnp.int32, (ny, ny), 1
    )
    own_y = lax.broadcasted_iota(jnp.int32, (ny, cols_ref.shape[1]), 0)
    depth_all = depth_ref[...].astype(F32)
    for x in range(nx):
        depth = jnp.sum(jnp.where(eye, depth_all[x : x + 1, :], 0.0), axis=1, keepdims=True)
        buoy = STEP_SQUARED * buoy_ref[x]
        mu = jnp.where(levels >= depth, shear_ref[x], 0.0)
        c_ref[0, x] = buoy * mu
        c_ref[1, x] = buoy * (lame_ref[x] + mu)
        here = cols_ref[...] == own_y + (base + x * total_y)
        floor = levels == depth
        drive = []
        for t in range(STEPS):
            amp = jnp.sum(jnp.where(here, amps_ref[t], 0.0), axis=1, keepdims=True)
            drive.append(jnp.where(floor, buoy * amp, 0.0))
        s_ref[0, x] = drive[1]
        s_ref[1, x] = drive[2]
        for k in range(3):
            p = 2.0 * u_ref[0, k, x] - v_ref[0, k, x]
            if k == 2:
                p = p + drive[0]
            p_ref[k, x] = p

    def column(name, k, y):
        if name == "u":
            return u_ref[0, k, :, y, :]
        if name == "p":
            return p_ref[k, :, y, :]
        if name == "c":
            return c_ref[k, :, y, :]
        if name == "s":
            return s_ref[k, :, y, :]
        return f_ref[0, k // 3, k % 3].astype(F32)[:, y, :]

    sides = ([], [])
    for name, k, ring, part in UNITS:
        top = column(name, k, ny - ring)
        low = column(name, k, ring - 1)
        for side, high in ((0, even_j == 1), (1, even_j == 0)):
            value = jnp.where(high, top, low)
            sides[side].append(split(value)[1] if part == "lo" else value)
    for dst, units in ((y0_ref, sides[0]), (y1_ref, sides[1])):
        padded = units + [jnp.zeros_like(units[0])] * (len(units) % 2)
        for n in range(0, len(padded), 2):
            dst[n // 2] = jnp.concatenate([padded[n], padded[n + 1]], axis=0).astype(BF16)
    for ref, high in ((c0_ref, even_i == 1), (c1_ref, even_i == 0)):
        for n, block in enumerate(corner_blocks(sides[1], high)):
            ref[n] = block


def face_kernel(u_ref, f_ref, p_ref, c_ref, s_ref, x0_ref, x1_ref):
    nx = c_ref.shape[1]
    even_i = position()[0]
    for dst, high in ((x0_ref, even_i == 1), (x1_ref, even_i == 0)):
        for n, (name, k, ring, part) in enumerate(UNITS):
            x = jnp.where(high, nx - ring, ring - 1)
            if name == "f":
                dst[n] = f_ref[0, k // 3, k % 3, x]
                continue
            if name == "u":
                value = u_ref[0, k, x]
            else:
                value = {"p": p_ref, "c": c_ref, "s": s_ref}[name][k, x]
            dst[n] = (split(value)[1] if part == "lo" else value).astype(BF16)


def corner_kernel(y0_ref, x0_in, x1_in, x0_ref, x1_ref):
    del x0_in, x1_in
    even_i = position()[0]
    units = side_units(y0_ref, y0_ref.shape[1] // 2)
    for dst, high in ((x0_ref, even_i == 1), (x1_ref, even_i == 0)):
        for n, block in enumerate(corner_blocks(units, high)):
            dst[FACE_BLOCKS + n] = block


def beside_z(value):
    tiles = [value[:, n : n + 128] for n in range(0, value.shape[1], 128)]
    lane = lax.broadcasted_iota(jnp.int32, tiles[0].shape, 1)
    zero = jnp.zeros_like(tiles[0])
    ups = [pltpu.roll(tile, 127, 1) for tile in tiles] + [zero]
    downs = [zero] + [pltpu.roll(tile, 1, 1) for tile in tiles]
    up = [jnp.where(lane == 127, ups[n + 1], ups[n]) for n in range(len(tiles))]
    down = [jnp.where(lane == 0, downs[n], downs[n + 1]) for n in range(len(tiles))]
    return jnp.concatenate(up, axis=1), jnp.concatenate(down, axis=1)


def beside_y(value):
    return pltpu.roll(value, value.shape[0] - 1, 0), pltpu.roll(value, 1, 0)


def advance_row(t, x, cur, before, p_ref, c_ref, s_ref, zd, zs, rows):
    um = [cur[k, x - 1] for k in range(3)]
    uc = [cur[k, x] for k in range(3)]
    up = [cur[k, x + 1] for k in range(3)]
    dx = [up[k] - um[k] for k in range(3)]
    dz1 = zd[1, x]
    ys = [beside_y(uc[k]) for k in range(3)]
    tilt = [beside_y(value) for value in (dx[1], dx[0] + zd[2, x], dz1)]
    cross = (
        (tilt[0][0] - tilt[0][1]) + (zd[2, x + 1] - zd[2, x - 1]),
        tilt[1][0] - tilt[1][1],
        (tilt[2][0] - tilt[2][1]) + (zd[0, x + 1] - zd[0, x - 1]),
    )
    rigid, bulk = c_ref[0, x, :rows], c_ref[1, x, :rows]
    fresh = []
    for k in range(3):
        pairs = (um[k] + up[k], ys[k][0] + ys[k][1], zs[k, x])
        laplace = pairs[0] + pairs[1] + pairs[2] - 6.0 * uc[k]
        grad_div = pairs[k] - 2.0 * uc[k] + 0.25 * cross[k]
        if t == 0:
            carry = p_ref[k, x, :rows]
        else:
            carry = 2.0 * uc[k][:rows] - before[k, x, :rows]
            if k == 2:
                carry = carry + s_ref[t - 1, x, :rows]
        fresh.append(carry + rigid * laplace[:rows] + bulk * grad_div[:rows])
    return fresh


def imprint_row(t, x, cur, zd, c_ref, f_ref, fz_ref, rows):
    ga, gf = [], []
    for k in range(3):
        yp, ym = beside_y(cur[k, x])
        ga.append(
            (
                cur[k, x + 1, :rows] - cur[k, x - 1, :rows],
                (yp - ym)[:rows],
                zd[k, x, :rows],
            )
        )
        n, r = 3 * t + k, x - RING + 1
        yp, ym = beside_y(f_ref[n, r])
        gf.append(
            (
                f_ref[n, r + 1, :rows] - f_ref[n, r - 1, :rows],
                (yp - ym)[:rows],
                fz_ref[n, x - RING],
            )
        )
    div = (ga[0][0] + ga[1][1] + ga[2][2]) * (gf[0][0] + gf[1][1] + gf[2][2])
    both = ga[0][0] * gf[0][0]
    for k in range(3):
        for d in range(3):
            if k + d > 0:
                both = both + ga[k][d] * gf[k][d]
    return div, jnp.where(c_ref[0, x, :rows] > 0.0, both, 0.0)


def joined(get, count):
    n = 0
    while n < count:
        name, k, ring, _ = UNITS[n]
        value = get(n)
        if name != "f" and ring == 1:
            value = value + get(n + 1)
            n += 1
        n += 1
        yield name, k, ring, value


def run_steps(refs, fz_ref, sum_ref, sums, early):
    nx, ny, nz = fz_ref.shape[1:]
    fields, c_ref = refs["fields"], refs["c"]
    wide_x, wide_y = c_ref.shape[1:3]

    def keep_z(k, x, value, zd, zs):
        up, down = beside_z(value)
        zd[k, x] = up - down
        zs[k, x] = up + down

    for x in range(wide_x):
        if (RING <= x < RING + nx) == early:
            for k in range(3):
                keep_z(k, x, fields[0][0][k, x], *fields[0][1:])

    for t in range(STEPS):
        cur, zd, zs = fields[t]
        for x in range(t + 1, wide_x - t - 1):
            if (RING < x - t and x + t < RING + nx - 1) != early:
                continue
            if t < STEPS - 1:
                nxt, nd, ns = fields[t + 1]
                fresh = advance_row(
                    t, x, cur, fields[t - 1][0], refs["p"], c_ref, refs["s"], zd, zs, wide_y
                )
                for k in range(3):
                    nxt[k, x] = fresh[k]
                    keep_z(k, x, fresh[k], nd, ns)
            if not RING <= x < RING + nx:
                continue
            terms = imprint_row(t, x, cur, zd, c_ref, refs["f"], fz_ref, ny)
            for n in range(2):
                value = terms[n]
                if t > 0:
                    value = value + sum_ref[n, x - RING]
                if t < STEPS - 1:
                    sum_ref[n, x - RING] = value
                elif len(sums) == 1:
                    sums[0][n, x - RING] = value
                else:
                    half = nz // 2
                    first = position()[4] == 0
                    sums[0][n, x - RING] = jnp.where(first, value[:, :half], value[:, half:])
                    sums[1][n, x - RING] = jnp.where(first, value[:, half:], value[:, :half])


def early_kernel(u_in, p_in, c_in, s_in, f_in, y0_in, y1_in, *outs):
    (
        u_ref,
        p_ref,
        c_ref,
        s_ref,
        f_ref,
        v_ref,
        w_ref,
        ud_ref,
        us_ref,
        vd_ref,
        vs_ref,
        wd_ref,
        ws_ref,
        fz_ref,
        sum_ref,
        *sums,
    ) = outs
    nx, ny, nz = c_in.shape[1:]
    wide = u_ref.shape[2]
    even_j, j = position()[1], position()[3]
    beyond = jnp.where(even_j == 1, j - 1, j + 1)
    ok_y1 = (beyond >= 0) & (beyond < lax.axis_size("ty"))

    for src, ref in ((u_in, u_ref), (p_in, p_ref), (c_in, c_ref), (s_in, s_ref)):
        lead = (0,) if src is u_in else ()
        for k in range(ref.shape[0]):
            for x in range(ref.shape[1]):
                if RING <= x < RING + nx:
                    ref[k, x, :ny, :] = src[lead + (k, x - RING)]
                    ref[k, x, ny:, :] = jnp.zeros((wide - ny, nz), F32)
                else:
                    ref[k, x] = jnp.zeros(ref.shape[2:], F32)
    for k in range(3 * STEPS):
        for x in range(nx):
            value = f_in[0, k // 3, k % 3, x].astype(F32)
            f_ref[k, x + 1, :ny, :] = value
            f_ref[k, x + 1, ny:, :] = jnp.zeros((wide - ny, nz), F32)
            up, down = beside_z(value)
            fz_ref[k, x] = up - down
        for x in (0, nx + 1):
            f_ref[k, x] = jnp.zeros(f_ref.shape[2:], F32)

    refs = {"u": u_ref, "p": p_ref, "c": c_ref, "s": s_ref, "f": f_ref}
    near = side_units(y0_in, nx)
    far = [jnp.where(ok_y1, value, 0.0) for value in side_units(y1_in, nx)]
    top = [jnp.where(even_j == 1, a, b) for a, b in zip(near, far)]
    low = [jnp.where(even_j == 1, b, a) for a, b in zip(near, far)]
    for values, high in ((top, True), (low, False)):
        for name, k, ring, value in joined(lambda n: values[n], FACE_BLOCKS):
            y = ny - 1 + ring if high else wide - ring
            first = 1 if name == "f" else RING
            for x in range(nx):
                refs[name][k, first + x, y : y + 1, :] = value[x : x + 1]
    refs["fields"] = (
        (u_ref, ud_ref, us_ref),
        (v_ref, vd_ref, vs_ref),
        (w_ref, wd_ref, ws_ref),
    )
    run_steps(refs, fz_ref, sum_ref, sums, True)


def late_kernel(fz_ref, x0_in, x1_in, c0_in, c1_in, *rest):
    (
        u_ref,
        p_ref,
        c_ref,
        s_ref,
        f_ref,
        v_ref,
        w_ref,
        ud_ref,
        us_ref,
        vd_ref,
        vs_ref,
        wd_ref,
        ws_ref,
        sum_ref,
        *sums,
    ) = rest[len(rest) // 2 :]
    nx, ny, nz = fz_ref.shape[1:]
    wide = u_ref.shape[2]
    even_i, even_j, i, j, _ = position()
    inside = lambda v, axis: (v >= 0) & (v < lax.axis_size(axis))
    ok_x1 = inside(jnp.where(even_i == 1, i - 1, i + 1), "tx")
    ok_y1 = inside(jnp.where(even_j == 1, j - 1, j + 1), "ty")
    refs = {"u": u_ref, "p": p_ref, "c": c_ref, "s": s_ref, "f": f_ref}

    for faces, corners, high, ok_near, ok_far in (
        (x0_in, c0_in, even_i == 1, None, ok_y1),
        (x1_in, c1_in, even_i == 0, ok_x1, ok_x1 & ok_y1),
    ):
        for name, k, ring, value in joined(lambda n: faces[n].astype(F32), FACE_BLOCKS):
            if ok_near is not None:
                value = jnp.where(ok_near, value, 0.0)
            first = 1 if name == "f" else RING
            x = jnp.where(high, first + nx - 1 + ring, first - ring)
            refs[name][k, x, :ny, :] = value
        near = [faces[FACE_BLOCKS + n].astype(F32) for n in range(CORNER_BLOCKS)]
        if ok_near is not None:
            near = [jnp.where(ok_near, value, 0.0) for value in near]
        far = [
            jnp.where(ok_far, corners[n].astype(F32), 0.0) for n in range(CORNER_BLOCKS)
        ]
        for y_high in (True, False):
            flag = even_j == (1 if y_high else 0)
            values = [jnp.where(flag, a, b) for a, b in zip(near, far)]
            row = lambda n: values[n // 16][n % 16 : n % 16 + 1]
            n = 0
            while n < len(CORNERS):
                name, k, ring_x, ring_y, _ = CORNERS[n]
                value = row(n)
                if ring_x == 1 and ring_y == 1:
                    value = value + row(n + 1)
                    n += 1
                n += 1
                x = jnp.where(high, RING + nx - 1 + ring_x, RING - ring_x)
                y = ny - 1 + ring_y if y_high else wide - ring_y
                refs[name][k, x, y : y + 1, :] = value
    refs["fields"] = (
        (u_ref, ud_ref, us_ref),
        (v_ref, vd_ref, vs_ref),
        (w_ref, wd_ref, ws_ref),
    )
    run_steps(refs, fz_ref, sum_ref, sums, False)


def last_kernel(w_ref, wd_ref, ws_ref, v_ref, c_ref, s_ref, out_ref):
    nx, ny = out_ref.shape[2:4]

    @pl.loop(RING, RING + nx, unroll=UNROLL)
    def _(x):
        fresh = advance_row(
            STEPS - 1, x, w_ref, v_ref, None, c_ref, s_ref, wd_ref, ws_ref, ny
        )
        for k in range(3):
            out_ref[0, k, x - RING] = fresh[k]


def swap_map(sizes, partner, spare):
    nx, ny, ns = sizes
    pairs = []
    for i in range(nx):
        for j in range(ny):
            a, b = partner(i, j)
            for s in range(ns):
                to = (a, b, s)
                if not (0 <= a < nx and 0 <= b < ny):
                    to = (i, j ^ 1, s) if spare == "y" else (i, j, s ^ 1 if s ^ 1 < ns else s)
                pairs.append(((i * ny + j) * ns + s, (to[0] * ny + to[1]) * ns + to[2]))
    return pairs


def body(
    adj_now,
    adj_later,
    forward_field,
    lame_first,
    shear,
    buoyancy,
    seafloor_depth,
    station_columns,
    station_traces,
):
    nx, ny, nz = lame_first.shape
    sizes = tuple(lax.axis_size(axis) for axis in AXES)
    count_s = sizes[2]
    vmem = pl.BlockSpec(memory_space=pltpu.VMEM)
    anywhere = pl.BlockSpec(memory_space=pl.ANY)
    limit = 30 * 1024 * 1024
    params = pltpu.CompilerParams(vmem_limit_bytes=limit)
    face = jax.ShapeDtypeStruct((FACE_BLOCKS + CORNER_BLOCKS, ny, nz), BF16)
    edge = jax.ShapeDtypeStruct((SIDE_BLOCKS, 2 * nx, nz), BF16)
    corner = jax.ShapeDtypeStruct((CORNER_BLOCKS, 16, nz), BF16)
    grid = lambda n: jax.ShapeDtypeStruct((n, nx, ny, nz), F32)

    like = lambda value: jax.ShapeDtypeStruct(value.shape, value.dtype)
    traces = jnp.transpose(station_traces, (1, 0, 2))
    held = (adj_later, lame_first, shear, buoyancy, seafloor_depth, station_columns, traces)
    u0, fwd, carry, coeff, drive, y0, y1, c0, c1 = pl.pallas_call(
        pack_kernel,
        out_shape=(
            like(adj_now),
            like(forward_field),
            grid(3),
            grid(2),
            grid(2),
            edge,
            edge,
            corner,
            corner,
        ),
        in_specs=[anywhere] * 9,
        out_specs=(vmem,) * 9,
        scratch_shapes=[pltpu.VMEM(value.shape, value.dtype) for value in held]
        + [pltpu.SemaphoreType.DMA((9,))],
        compiler_params=params,
        name="pack",
    )(
        *(
            pltpu.with_memory_space_constraint(value, pltpu.HBM)
            for value in (adj_now, adj_later, forward_field, *held[1:])
        )
    )

    def exchange(value, partner, spare="s"):
        return lax.ppermute(value, AXES, swap_map(sizes, partner, spare))

    flip = lambda n: n + 1 if n % 2 == 0 else n - 1
    back = lambda n: n - 1 if n % 2 == 0 else n + 1
    y0 = exchange(y0, lambda a, b: (a, flip(b)))
    x0, x1 = pl.pallas_call(
        face_kernel,
        out_shape=(face, face),
        in_specs=[vmem] * 5,
        out_specs=(vmem,) * 2,
        compiler_params=params,
        name="faces",
    )(u0, fwd, carry, coeff, drive)
    x0, x1 = pl.pallas_call(
        corner_kernel,
        out_shape=(face, face),
        in_specs=[vmem] * 3,
        out_specs=(vmem,) * 2,
        input_output_aliases={1: 0, 2: 1},
        compiler_params=params,
        name="corners",
    )(y0, x0, x1)
    x0 = exchange(x0, lambda a, b: (flip(a), b))
    x1 = exchange(x1, lambda a, b: (back(a), b), "y")
    y1 = exchange(y1, lambda a, b: (a, back(b)))
    c0 = exchange(c0, lambda a, b: (flip(a), back(b)))
    c1 = exchange(c1, lambda a, b: (back(a), back(b)))

    wide_x, wide_y = nx + 2 * RING, ny + PAD
    padded = lambda n, x=wide_x: jax.ShapeDtypeStruct((n, x, wide_y, nz), F32)
    tile = (padded(3), padded(3), padded(2), padded(2), padded(3 * STEPS, nx + 2))
    half = jax.ShapeDtypeStruct((2, nx, ny, nz // 2), F32)
    sums = (half, half) if count_s == 2 else (grid(2),)
    shapes = (*tile, *(padded(3),) * 8, grid(3 * STEPS), grid(2), *sums)
    held = pl.pallas_call(
        early_kernel,
        out_shape=shapes,
        in_specs=[vmem] * 7,
        out_specs=(vmem,) * len(shapes),
        compiler_params=params,
        name="early",
    )(u0, carry, coeff, drive, fwd, y0, y1)
    fwd_z = held[13]
    held = (*held[:13], *held[14:])
    shapes = (*shapes[:13], *shapes[14:])
    held = pl.pallas_call(
        late_kernel,
        out_shape=shapes,
        in_specs=[vmem] * (5 + len(shapes)),
        out_specs=(vmem,) * len(shapes),
        input_output_aliases={5 + n: n for n in range(len(shapes))},
        compiler_params=params,
        name="late",
    )(fwd_z, x0, x1, c0, c1, *held)
    coeff, drive = held[2:4]
    u1, u2 = held[5:7]
    u2_d, u2_s = held[11:13]
    sums = held[14:]

    scale = 0.25 / (adj_now.shape[0] * count_s)
    if count_s == 2:
        theirs = lax.ppermute(sums[1], "src", [(0, 1), (1, 0)])
        summed = sums[0] + theirs
    else:
        summed = lax.psum_scatter(sums[0], "src", scatter_dimension=3, tiled=True)
    final = pl.pallas_call(
        last_kernel,
        out_shape=like(adj_now),
        in_specs=[vmem] * 6,
        out_specs=vmem,
        compiler_params=params,
        name="last",
    )(u2, u2_d, u2_s, u1, coeff, drive)
    return final, summed * scale


def solution(mesh):
    in_specs = (
        P("src", None, "tx", "ty", None),
        P("src", None, "tx", "ty", None),
        P("src", None, None, "tx", "ty", None),
        P("tx", "ty", None),
        P("tx", "ty", None),
        P("tx", "ty", None),
        P("tx", "ty"),
        P("src", None),
        P("src", None, None),
    )
    out_specs = (P("src", None, "tx", "ty", None), P(None, "tx", "ty", "src"))
    return jax.shard_map(body, mesh=mesh, in_specs=in_specs, out_specs=out_specs, check_vma=False)
```

```python
import functools

import jax
import jax.numpy as jnp
from jax import lax
from jax.experimental import pallas as pl
from jax.experimental.pallas import tpu as pltpu
from jax.sharding import PartitionSpec as P

STEPS = 3
STEP_SQUARED = 0.04
RING = 3
SOLID = 126
PAD = 8
AXES = ("tx", "ty", "src")
F32 = jnp.float32
BF16 = jnp.bfloat16
UNROLL = 8


def halo_units():
    units = []
    for name, count, rings in (("u", 3, 3), ("p", 3, 2), ("b", 1, 2)):
        for k in range(count):
            for ring in range(1, rings + 1):
                units.append((name, k, ring, "hi"))
                if ring == 1:
                    units.append((name, k, ring, "lo"))
    units += [("a", 0, 1, "hi"), ("a", 0, 2, "hi")]
    for k in range(3 * STEPS):
        units.append(("f", k, 1, "hi"))
    return units


def corner_entries():
    entries = []
    for name, count, rings in (("u", 3, 3), ("p", 3, 2), ("b", 1, 2), ("a", 1, 2)):
        for k in range(count):
            for ring_x in range(1, rings + 1):
                for ring_y in range(1, rings + 1):
                    entries.append((name, k, ring_x, ring_y, "hi"))
                    if ring_x == 1 and ring_y == 1 and name != "a":
                        entries.append((name, k, ring_x, ring_y, "lo"))
    return entries


UNITS = halo_units()
CORNERS = corner_entries()
FACE_BLOCKS = len(UNITS)
SIDE_BLOCKS = (len(UNITS) + 1) // 2
CORNER_BLOCKS = (len(CORNERS) + 15) // 16


def position():
    i, j, s = (lax.axis_index(axis) for axis in AXES)
    return (i + 1) % 2, (j + 1) % 2, i, j, s


def split(value):
    top = value.astype(BF16).astype(F32)
    return top, value - top


def rigid_units(ring1, ring2, drive):
    lane = lax.broadcasted_iota(jnp.int32, ring1.shape, 1)
    half = ring1.shape[1] // 2
    top, rest = split(ring1)
    turned = pltpu.roll(rest, half, 1)
    first = jnp.where(lane < SOLID, turned, top)
    second = jnp.where(
        lane < 2, pltpu.roll(turned, half + 2, 1), pltpu.roll(turned, 4, 1)
    )
    strength = jnp.sum(drive, axis=1, keepdims=True)
    where = jnp.sum(jnp.where(drive != 0.0, lane.astype(F32), 0.0), axis=1, keepdims=True)
    hi, lo = split(strength)
    extra = jnp.where(lane == 4, hi, jnp.where(lane == 5, lo, where))
    second = jnp.where(lane < 4, second, jnp.where(lane < 7, extra, 0.0))
    return first, jnp.where(lane < SOLID, second, ring2)


def rigid_rows(first, second):
    lane = lax.broadcasted_iota(jnp.int32, first.shape, 1)
    size = first.shape[1]
    half = size // 2
    rest = jnp.where(lane < half, pltpu.roll(second, half - 4, 1), pltpu.roll(first, half, 1))
    rest = jnp.where(lane < size - 2, rest, pltpu.roll(second, size - 2, 1))
    ring1 = jnp.where(lane >= SOLID, first + rest, 0.0)
    ring2 = jnp.where(lane >= SOLID, second, 0.0)
    strength = second[:, 4:5] + second[:, 5:6]
    return ring1, ring2, jnp.where(lane.astype(F32) == second[:, 6:7], strength, 0.0)


def corner_blocks(units, high):
    at = {unit: value for unit, value in zip(UNITS, units)}
    nx = units[0].shape[0]
    rows = []
    for name, k, ring_x, ring_y, part in CORNERS:
        unit = at[name, k, ring_y, part]
        rows.append(
            jnp.where(high, unit[nx - ring_x : nx - ring_x + 1], unit[ring_x - 1 : ring_x])
        )
    rows += [jnp.zeros_like(rows[0])] * (-len(rows) % 16)
    return [
        jnp.concatenate(rows[n : n + 16], axis=0).astype(BF16) for n in range(0, len(rows), 16)
    ]


def side_units(ref, nx):
    blocks = [ref[n].astype(F32) for n in range(SIDE_BLOCKS)]
    return [blocks[n // 2][nx * (n % 2) : nx * (n % 2) + nx] for n in range(FACE_BLOCKS)]


def edge_units(u_ref, f_ref, p_ref, c_ref, s_ref, high):
    nx, ny = c_ref.shape[1:3]

    def column(value, ring):
        return jnp.where(high, value[:, ny - ring, :], value[:, ring - 1, :])

    rigid = rigid_units(column(c_ref[0], 1), column(c_ref[0], 2), column(s_ref[0], 1))
    units = []
    for name, k, ring, part in UNITS:
        if name == "a":
            units.append(rigid[ring - 1])
            continue
        if name == "f":
            value = f_ref[0, k // 3, k % 3].astype(F32)
        else:
            value = u_ref[0, k] if name == "u" else p_ref[k] if name == "p" else c_ref[1]
        value = column(value, ring)
        units.append(split(value)[1] if part == "lo" else value)
    return units


def unit_blocks(units):
    units = units + [jnp.zeros_like(units[0])] * (len(units) % 2)
    return [
        jnp.concatenate(units[n : n + 2], axis=0).astype(BF16) for n in range(0, len(units), 2)
    ]


def pack_kernel(
    u_in,
    v_in,
    f_in,
    lame_in,
    shear_in,
    buoy_in,
    depth_in,
    cols_in,
    amps_in,
    u_ref,
    f_ref,
    p_ref,
    c_ref,
    s_ref,
    y0_ref,
    v_ref,
    lame_ref,
    shear_ref,
    buoy_ref,
    depth_ref,
    cols_ref,
    amps_ref,
    sems,
):
    copies = [
        pltpu.make_async_copy(src, dst, sems.at[n])
        for n, (src, dst) in enumerate(
            (
                (depth_in, depth_ref),
                (cols_in, cols_ref),
                (amps_in, amps_ref),
                (buoy_in, buoy_ref),
                (shear_in, shear_ref),
                (lame_in, lame_ref),
                (u_in, u_ref),
                (v_in, v_ref),
                (f_in, f_ref),
            )
        )
    ]
    for copy in copies:
        copy.start()
    for copy in copies[:6]:
        copy.wait()
    nx, ny, nz = lame_ref.shape
    _, even_j, i, j, _ = position()
    total_y = ny * lax.axis_size("ty")
    base = i * nx * total_y + j * ny
    levels = lax.broadcasted_iota(jnp.int32, (ny, nz), 1).astype(F32)
    eye = lax.broadcasted_iota(jnp.int32, (ny, ny), 0) == lax.broadcasted_iota(
        jnp.int32, (ny, ny), 1
    )
    own_y = lax.broadcasted_iota(jnp.int32, (ny, cols_ref.shape[1]), 0)
    depth_all = depth_ref[...].astype(F32)
    for x in range(nx):
        depth = jnp.sum(jnp.where(eye, depth_all[x : x + 1, :], 0.0), axis=1, keepdims=True)
        buoy = STEP_SQUARED * buoy_ref[x]
        mu = jnp.where(levels >= depth, shear_ref[x], 0.0)
        c_ref[0, x] = buoy * mu
        c_ref[1, x] = buoy * (lame_ref[x] + mu)
        here = cols_ref[...] == own_y + (base + x * total_y)
        floor = levels == depth
        drive = []
        for t in range(STEPS):
            amp = jnp.sum(jnp.where(here, amps_ref[t], 0.0), axis=1, keepdims=True)
            drive.append(jnp.where(floor, buoy * amp, 0.0))
        s_ref[0, x] = drive[1]
        s_ref[1, x] = drive[2]
        p_ref[2, x] = drive[0]
    for copy in copies[6:8]:
        copy.wait()
    for x in range(nx):
        for k in range(3):
            p = 2.0 * u_ref[0, k, x] - v_ref[0, k, x]
            p_ref[k, x] = p + p_ref[k, x] if k == 2 else p
    copies[8].wait()
    for n, block in enumerate(
        unit_blocks(edge_units(u_ref, f_ref, p_ref, c_ref, s_ref, even_j == 1))
    ):
        y0_ref[n] = block


def face_kernel(
    u_ref, f_ref, p_ref, c_ref, s_ref, x0_ref, x1_ref, y1_ref, c0_ref, c1_ref
):
    nx = c_ref.shape[1]
    even_i, even_j = position()[:2]
    units = edge_units(u_ref, f_ref, p_ref, c_ref, s_ref, even_j == 0)
    for n, block in enumerate(unit_blocks(units)):
        y1_ref[n] = block
    for ref, high in ((c0_ref, even_i == 1), (c1_ref, even_i == 0)):
        for n, block in enumerate(corner_blocks(units, high)):
            ref[n] = block
    for dst, high in ((x0_ref, even_i == 1), (x1_ref, even_i == 0)):
        at = [jnp.where(high, nx - ring, ring - 1) for ring in (1, 2, 3)]
        rigid = rigid_units(c_ref[0, at[0]], c_ref[0, at[1]], s_ref[0, at[0]])
        for n, (name, k, ring, part) in enumerate(UNITS):
            x = at[ring - 1]
            if name == "f":
                dst[n] = f_ref[0, k // 3, k % 3, x]
            elif name == "a":
                dst[n] = rigid[ring - 1].astype(BF16)
            else:
                value = u_ref[0, k, x] if name == "u" else p_ref[k, x] if name == "p" else c_ref[1, x]
                dst[n] = (split(value)[1] if part == "lo" else value).astype(BF16)


def corner_kernel(y0_ref, x0_in, x1_in, x0_ref, x1_ref):
    del x0_in, x1_in
    even_i = position()[0]
    units = side_units(y0_ref, y0_ref.shape[1] // 2)
    for dst, high in ((x0_ref, even_i == 1), (x1_ref, even_i == 0)):
        for n, block in enumerate(corner_blocks(units, high)):
            dst[FACE_BLOCKS + n] = block


def beside_z(value):
    tiles = [value[:, n : n + 128] for n in range(0, value.shape[1], 128)]
    lane = lax.broadcasted_iota(jnp.int32, tiles[0].shape, 1)
    zero = jnp.zeros_like(tiles[0])
    ups = [pltpu.roll(tile, 127, 1) for tile in tiles] + [zero]
    downs = [zero] + [pltpu.roll(tile, 1, 1) for tile in tiles]
    up = [jnp.where(lane == 127, ups[n + 1], ups[n]) for n in range(len(tiles))]
    down = [jnp.where(lane == 0, downs[n], downs[n + 1]) for n in range(len(tiles))]
    return jnp.concatenate(up, axis=1), jnp.concatenate(down, axis=1)


def beside_y(value):
    return pltpu.roll(value, value.shape[0] - 1, 0), pltpu.roll(value, 1, 0)


def advance_row(t, x, cur, before, p_ref, c_ref, s_ref, zd, zs, rows):
    um = [cur[k, x - 1] for k in range(3)]
    uc = [cur[k, x] for k in range(3)]
    up = [cur[k, x + 1] for k in range(3)]
    dx = [up[k] - um[k] for k in range(3)]
    dz1 = zd[1, x]
    ys = [beside_y(uc[k]) for k in range(3)]
    tilt = [beside_y(value) for value in (dx[1], dx[0] + zd[2, x], dz1)]
    cross = (
        (tilt[0][0] - tilt[0][1]) + (zd[2, x + 1] - zd[2, x - 1]),
        tilt[1][0] - tilt[1][1],
        (tilt[2][0] - tilt[2][1]) + (zd[0, x + 1] - zd[0, x - 1]),
    )
    rigid, bulk = c_ref[0, x, :rows], c_ref[1, x, :rows]
    fresh = []
    for k in range(3):
        pairs = (um[k] + up[k], ys[k][0] + ys[k][1], zs[k, x])
        laplace = pairs[0] + pairs[1] + pairs[2] - 6.0 * uc[k]
        grad_div = pairs[k] - 2.0 * uc[k] + 0.25 * cross[k]
        if t == 0:
            carry = p_ref[k, x, :rows]
        else:
            carry = 2.0 * uc[k][:rows] - before[k, x, :rows]
            if k == 2:
                carry = carry + s_ref[t - 1, x, :rows]
        fresh.append(carry + rigid * laplace[:rows] + bulk * grad_div[:rows])
    return fresh


def imprint_row(t, x, cur, zd, c_ref, f_ref, fz_ref, rows):
    ga, gf = [], []
    for k in range(3):
        yp, ym = beside_y(cur[k, x])
        ga.append(
            (
                cur[k, x + 1, :rows] - cur[k, x - 1, :rows],
                (yp - ym)[:rows],
                zd[k, x, :rows],
            )
        )
        n, r = 3 * t + k, x - RING + 1
        yp, ym = beside_y(f_ref[n, r])
        gf.append(
            (
                f_ref[n, r + 1, :rows] - f_ref[n, r - 1, :rows],
                (yp - ym)[:rows],
                fz_ref[n, x - RING],
            )
        )
    div = (ga[0][0] + ga[1][1] + ga[2][2]) * (gf[0][0] + gf[1][1] + gf[2][2])
    both = ga[0][0] * gf[0][0]
    for k in range(3):
        for d in range(3):
            if k + d > 0:
                both = both + ga[k][d] * gf[k][d]
    return div, jnp.where(c_ref[0, x, :rows] > 0.0, both, 0.0)


def joined(get):
    n = 0
    while n < len(UNITS):
        name, k, ring, _ = UNITS[n]
        if name == "a":
            for entry in zip("ccs", (0, 0, 0), (1, 2, 1), rigid_rows(get(n), get(n + 1))):
                yield entry
            n += 2
            continue
        value = get(n)
        if name != "f" and ring == 1:
            value = value + get(n + 1)
            n += 1
        n += 1
        yield ("c", 1, ring, value) if name == "b" else (name, k, ring, value)


def joined_corner(get):
    n = 0
    while n < len(CORNERS):
        name, k, ring_x, ring_y, _ = CORNERS[n]
        if name == "a":
            for x in (1, 2):
                ring1, ring2, drive = rigid_rows(get(n), get(n + 1))
                yield "c", 0, x, 1, ring1
                yield "c", 0, x, 2, ring2
                if x == 1:
                    yield "s", 0, 1, 1, drive
                n += 2
            continue
        value = get(n)
        if ring_x == 1 and ring_y == 1:
            value = value + get(n + 1)
            n += 1
        n += 1
        yield ("c", 1, ring_x, ring_y, value) if name == "b" else (name, k, ring_x, ring_y, value)


def keep_z(k, x, value, zd, zs, rows=slice(None)):
    up, down = beside_z(value)
    zd[k, x, rows] = up - down
    zs[k, x, rows] = up + down


def run_steps(refs, fz_ref, sum_ref, sums, early):
    nx, ny, nz = fz_ref.shape[1:]
    fields, c_ref = refs["fields"], refs["c"]
    wide_x, wide_y = c_ref.shape[1:3]

    for t in range(STEPS):
        cur, zd, zs = fields[t]
        for x in range(t + 1, wide_x - t - 1):
            if (RING < x - t and x + t < RING + nx - 1) != early:
                continue
            if t < STEPS - 1:
                nxt, nd, ns = fields[t + 1]
                fresh = advance_row(
                    t, x, cur, fields[t - 1][0], refs["p"], c_ref, refs["s"], zd, zs, wide_y
                )
                for k in range(3):
                    nxt[k, x] = fresh[k]
                    keep_z(k, x, fresh[k], nd, ns)
            if not RING <= x < RING + nx:
                continue
            terms = imprint_row(t, x, cur, zd, c_ref, refs["f"], fz_ref, ny)
            for n in range(2):
                value = terms[n]
                if t > 0:
                    value = value + sum_ref[n, x - RING]
                own = x - RING
                if t < STEPS - 1:
                    sum_ref[n, own] = value
                    continue
                row = own - STEPS if early else own if own < STEPS else own - (nx - 2 * STEPS)
                if len(sums) == 1:
                    sums[0][n, row] = value
                else:
                    half = nz // 2
                    first = position()[4] == 0
                    sums[0][n, row] = jnp.where(first, value[:, :half], value[:, half:])
                    sums[1][n, row] = jnp.where(first, value[:, half:], value[:, :half])


def stage_kernel(
    u_in, p_in, c_in, s_in, f_in, u_ref, p_ref, c_ref, s_ref, f_ref, ud_ref, us_ref, fz_ref
):
    nx, ny, nz = c_in.shape[1:]
    wide = u_ref.shape[2]
    for src, ref in ((u_in, u_ref), (p_in, p_ref), (c_in, c_ref), (s_in, s_ref)):
        lead = (0,) if src is u_in else ()
        for k in range(ref.shape[0]):
            for x in range(ref.shape[1]):
                if RING <= x < RING + nx:
                    value = src[lead + (k, x - RING)]
                    ref[k, x, :ny, :] = value
                    ref[k, x, ny:, :] = jnp.zeros((wide - ny, nz), F32)
                    if src is u_in:
                        keep_z(k, x, value, ud_ref, us_ref, slice(0, ny))
                else:
                    ref[k, x] = jnp.zeros(ref.shape[2:], F32)
    for k in range(3 * STEPS):
        for x in range(nx):
            value = f_in[0, k // 3, k % 3, x].astype(F32)
            f_ref[k, x + 1, :ny, :] = value
            f_ref[k, x + 1, ny:, :] = jnp.zeros((wide - ny, nz), F32)
            up, down = beside_z(value)
            fz_ref[k, x] = up - down
        for x in (0, nx + 1):
            f_ref[k, x] = jnp.zeros(f_ref.shape[2:], F32)


def early_kernel(fz_ref, y0_in, y1_in, *rest):
    (
        u_ref,
        p_ref,
        c_ref,
        s_ref,
        f_ref,
        ud_ref,
        us_ref,
        v_ref,
        w_ref,
        vd_ref,
        vs_ref,
        wd_ref,
        ws_ref,
        sum_ref,
        *sums,
    ) = rest[7:]
    nx, ny, nz = fz_ref.shape[1:]
    wide = u_ref.shape[2]
    even_j, j = position()[1], position()[3]
    beyond = jnp.where(even_j == 1, j - 1, j + 1)
    ok_y1 = (beyond >= 0) & (beyond < lax.axis_size("ty"))

    refs = {"u": u_ref, "p": p_ref, "c": c_ref, "s": s_ref, "f": f_ref}
    near = side_units(y0_in, nx)
    far = [jnp.where(ok_y1, value, 0.0) for value in side_units(y1_in, nx)]
    top = [jnp.where(even_j == 1, a, b) for a, b in zip(near, far)]
    low = [jnp.where(even_j == 1, b, a) for a, b in zip(near, far)]
    for values, high in ((top, True), (low, False)):
        for name, k, ring, value in joined(lambda n: values[n]):
            y = ny - 1 + ring if high else wide - ring
            first = 1 if name == "f" else RING
            for x in range(nx):
                refs[name][k, first + x, y : y + 1, :] = value[x : x + 1]
    for x in range(RING, RING + nx):
        for k in range(3):
            keep_z(k, x, u_ref[k, x, ny:], ud_ref, us_ref, slice(ny, wide))
    refs["fields"] = (
        (u_ref, ud_ref, us_ref),
        (v_ref, vd_ref, vs_ref),
        (w_ref, wd_ref, ws_ref),
    )
    run_steps(refs, fz_ref, sum_ref, sums, True)


def late_kernel(fz_ref, x0_in, x1_in, c0_in, c1_in, *rest):
    (
        u_ref,
        p_ref,
        c_ref,
        s_ref,
        f_ref,
        ud_ref,
        us_ref,
        v_ref,
        w_ref,
        vd_ref,
        vs_ref,
        wd_ref,
        ws_ref,
        sum_ref,
        *sums,
    ) = rest[14:]
    nx, ny, nz = fz_ref.shape[1:]
    wide = u_ref.shape[2]
    even_i, even_j, i, j, _ = position()
    inside = lambda v, axis: (v >= 0) & (v < lax.axis_size(axis))
    ok_x1 = inside(jnp.where(even_i == 1, i - 1, i + 1), "tx")
    ok_y1 = inside(jnp.where(even_j == 1, j - 1, j + 1), "ty")
    refs = {"u": u_ref, "p": p_ref, "c": c_ref, "s": s_ref, "f": f_ref}

    for faces, corners, high, ok_near, ok_far in (
        (x0_in, c0_in, even_i == 1, None, ok_y1),
        (x1_in, c1_in, even_i == 0, ok_x1, ok_x1 & ok_y1),
    ):
        for name, k, ring, value in joined(lambda n: faces[n].astype(F32)):
            if ok_near is not None:
                value = jnp.where(ok_near, value, 0.0)
            first = 1 if name == "f" else RING
            x = jnp.where(high, first + nx - 1 + ring, first - ring)
            refs[name][k, x, :ny, :] = value
        near = [faces[FACE_BLOCKS + n].astype(F32) for n in range(CORNER_BLOCKS)]
        if ok_near is not None:
            near = [jnp.where(ok_near, value, 0.0) for value in near]
        far = [
            jnp.where(ok_far, corners[n].astype(F32), 0.0) for n in range(CORNER_BLOCKS)
        ]
        for y_high in (True, False):
            flag = even_j == (1 if y_high else 0)
            values = [jnp.where(flag, a, b) for a, b in zip(near, far)]
            row = lambda n: values[n // 16][n % 16 : n % 16 + 1]
            for name, k, ring_x, ring_y, value in joined_corner(row):
                x = jnp.where(high, RING + nx - 1 + ring_x, RING - ring_x)
                y = ny - 1 + ring_y if y_high else wide - ring_y
                refs[name][k, x, y : y + 1, :] = value
    refs["fields"] = (
        (u_ref, ud_ref, us_ref),
        (v_ref, vd_ref, vs_ref),
        (w_ref, wd_ref, ws_ref),
    )
    for x in (*range(RING), *range(RING + nx, 2 * RING + nx)):
        for k in range(3):
            keep_z(k, x, u_ref[k, x], ud_ref, us_ref)
    run_steps(refs, fz_ref, sum_ref, sums, False)


def total_kernel(scale, mid_ref, rest_ref, mid_in, rest_in, out_ref):
    nx = out_ref.shape[1]
    for n in range(2):
        for x in range(nx):
            if STEPS <= x < nx - STEPS:
                value = mid_ref[n, x - STEPS] + mid_in[n, x - STEPS]
            else:
                row = x if x < STEPS else x - (nx - 2 * STEPS)
                value = rest_ref[n, row] + rest_in[n, row]
            out_ref[n, x] = value * scale


def last_kernel(w_ref, wd_ref, ws_ref, v_ref, c_ref, s_ref, out_ref):
    nx, ny = out_ref.shape[2:4]

    @pl.loop(RING, RING + nx, unroll=UNROLL)
    def _(x):
        fresh = advance_row(
            STEPS - 1, x, w_ref, v_ref, None, c_ref, s_ref, wd_ref, ws_ref, ny
        )
        for k in range(3):
            out_ref[0, k, x - RING] = fresh[k]


def swap_map(sizes, partner, spare):
    nx, ny, ns = sizes
    pairs = []
    for i in range(nx):
        for j in range(ny):
            a, b = partner(i, j)
            for s in range(ns):
                to = (a, b, s)
                if not (0 <= a < nx and 0 <= b < ny):
                    to = (i, j ^ 1, s) if spare == "y" else (i, j, s ^ 1 if s ^ 1 < ns else s)
                pairs.append(((i * ny + j) * ns + s, (to[0] * ny + to[1]) * ns + to[2]))
    return pairs


def body(
    adj_now,
    adj_later,
    forward_field,
    lame_first,
    shear,
    buoyancy,
    seafloor_depth,
    station_columns,
    station_traces,
):
    nx, ny, nz = lame_first.shape
    sizes = tuple(lax.axis_size(axis) for axis in AXES)
    count_s = sizes[2]
    vmem = pl.BlockSpec(memory_space=pltpu.VMEM)
    anywhere = pl.BlockSpec(memory_space=pl.ANY)
    limit = 30 * 1024 * 1024
    params = pltpu.CompilerParams(vmem_limit_bytes=limit)
    face = jax.ShapeDtypeStruct((FACE_BLOCKS + CORNER_BLOCKS, ny, nz), BF16)
    edge = jax.ShapeDtypeStruct((SIDE_BLOCKS, 2 * nx, nz), BF16)
    corner = jax.ShapeDtypeStruct((CORNER_BLOCKS, 16, nz), BF16)
    grid = lambda n: jax.ShapeDtypeStruct((n, nx, ny, nz), F32)

    like = lambda value: jax.ShapeDtypeStruct(value.shape, value.dtype)
    traces = jnp.transpose(station_traces, (1, 0, 2))
    held = (adj_later, lame_first, shear, buoyancy, seafloor_depth, station_columns, traces)
    u0, fwd, carry, coeff, drive, y0 = pl.pallas_call(
        pack_kernel,
        out_shape=(
            like(adj_now),
            like(forward_field),
            grid(3),
            grid(2),
            grid(2),
            edge,
        ),
        in_specs=[anywhere] * 9,
        out_specs=(vmem,) * 6,
        scratch_shapes=[pltpu.VMEM(value.shape, value.dtype) for value in held]
        + [pltpu.SemaphoreType.DMA((9,))],
        compiler_params=params,
        name="pack",
    )(
        *(
            pltpu.with_memory_space_constraint(value, pltpu.HBM)
            for value in (adj_now, adj_later, forward_field, *held[1:])
        )
    )

    def exchange(value, partner, spare="s"):
        return lax.ppermute(value, AXES, swap_map(sizes, partner, spare))

    flip = lambda n: n + 1 if n % 2 == 0 else n - 1
    back = lambda n: n - 1 if n % 2 == 0 else n + 1
    y0 = exchange(y0, lambda a, b: (a, flip(b)))
    x0, x1, y1, c0, c1 = pl.pallas_call(
        face_kernel,
        out_shape=(face, face, edge, corner, corner),
        in_specs=[vmem] * 5,
        out_specs=(vmem,) * 5,
        compiler_params=params,
        name="faces",
    )(u0, fwd, carry, coeff, drive)
    x0, x1 = pl.pallas_call(
        corner_kernel,
        out_shape=(face, face),
        in_specs=[vmem] * 3,
        out_specs=(vmem,) * 2,
        input_output_aliases={1: 0, 2: 1},
        compiler_params=params,
        name="corners",
    )(y0, x0, x1)
    x0 = exchange(x0, lambda a, b: (flip(a), b))
    x1 = exchange(x1, lambda a, b: (back(a), b), "y")
    y1 = exchange(y1, lambda a, b: (a, back(b)))
    c0 = exchange(c0, lambda a, b: (flip(a), back(b)))
    c1 = exchange(c1, lambda a, b: (back(a), back(b)))

    wide_x, wide_y = nx + 2 * RING, ny + PAD
    padded = lambda n, x=wide_x: jax.ShapeDtypeStruct((n, x, wide_y, nz), F32)
    tile = (padded(3), padded(3), padded(2), padded(2), padded(3 * STEPS, nx + 2))
    split_up = count_s == 2
    depth = nz // 2 if split_up else nz
    sums = lambda rows: (jax.ShapeDtypeStruct((2, rows, ny, depth), F32),) * (1 + split_up)
    mid, rest = sums(nx - 2 * STEPS), sums(2 * STEPS)
    staged = (*tile, padded(3), padded(3))
    *held, fwd_z = pl.pallas_call(
        stage_kernel,
        out_shape=(*staged, grid(3 * STEPS)),
        in_specs=[vmem] * 5,
        out_specs=(vmem,) * 8,
        compiler_params=params,
        name="stage",
    )(u0, carry, coeff, drive, fwd)
    shapes = (*staged, *(padded(3),) * 6, grid(2), *mid)
    held = pl.pallas_call(
        early_kernel,
        out_shape=shapes,
        in_specs=[vmem] * 10,
        out_specs=(vmem,) * len(shapes),
        input_output_aliases={3 + n: n for n in range(7)},
        compiler_params=params,
        name="early",
    )(fwd_z, y0, y1, *held)
    held, mid = held[:14], held[14:]
    swap = lambda value: lax.ppermute(value, "src", [(0, 1), (1, 0)])
    if split_up:
        mid = (mid[0], swap(mid[1]))
    shapes = (*shapes[:14], *rest)
    held = pl.pallas_call(
        late_kernel,
        out_shape=shapes,
        in_specs=[vmem] * 19,
        out_specs=(vmem,) * len(shapes),
        input_output_aliases={5 + n: n for n in range(14)},
        compiler_params=params,
        name="late",
    )(fwd_z, x0, x1, c0, c1, *held)
    coeff, drive = held[2:4]
    u1, u2 = held[7:9]
    u2_d, u2_s = held[11:13]
    rest = held[14:]

    scale = 0.25 / (adj_now.shape[0] * count_s)
    if split_up:
        summed = pl.pallas_call(
            functools.partial(total_kernel, scale),
            out_shape=jax.ShapeDtypeStruct((2, nx, ny, depth), F32),
            in_specs=[vmem] * 4,
            out_specs=vmem,
            compiler_params=params,
            name="total",
        )(mid[0], rest[0], mid[1], swap(rest[1]))
    else:
        parts = (rest[0][:, :STEPS], mid[0], rest[0][:, STEPS:])
        summed = lax.psum_scatter(
            jnp.concatenate(parts, axis=1) * scale, "src", scatter_dimension=3, tiled=True
        )
    final = pl.pallas_call(
        last_kernel,
        out_shape=like(adj_now),
        in_specs=[vmem] * 6,
        out_specs=vmem,
        compiler_params=params,
        name="last",
    )(u2, u2_d, u2_s, u1, coeff, drive)
    return final, summed


def solution(mesh):
    in_specs = (
        P("src", None, "tx", "ty", None),
        P("src", None, "tx", "ty", None),
        P("src", None, None, "tx", "ty", None),
        P("tx", "ty", None),
        P("tx", "ty", None),
        P("tx", "ty", None),
        P("tx", "ty"),
        P("src", None),
        P("src", None, None),
    )
    out_specs = (P("src", None, "tx", "ty", None), P(None, "tx", "ty", "src"))
    return jax.shard_map(body, mesh=mesh, in_specs=in_specs, out_specs=out_specs, check_vma=False)
```

```python
import functools
import math

import jax
import jax.numpy as jnp
from jax import lax
from jax.experimental import pallas as pl
from jax.experimental.pallas import tpu as pltpu
from jax.sharding import PartitionSpec as P

STEPS = 3
STEP_SQUARED = 0.04
RING = 3
SOLID = 126
PAD = 8
AXES = ("tx", "ty", "src")
F32 = jnp.float32
BF16 = jnp.bfloat16
UNROLL = 8
TARGET = 13.0


def halo_units():
    units = []
    for name, count, rings in (("u", 3, 3), ("p", 3, 2), ("b", 1, 2)):
        for k in range(count):
            for ring in range(1, rings + 1):
                units.append((name, k, ring, "hi"))
                if ring == 1:
                    units.append((name, k, ring, "lo"))
    units += [("a", 0, 1, "hi"), ("a", 0, 2, "hi")]
    for k in range(3 * STEPS):
        units.append(("f", k, 1, "hi"))
    return units


def corner_entries():
    entries = []
    for name, count, rings in (("u", 3, 3), ("p", 3, 2), ("b", 1, 2), ("a", 1, 2)):
        for k in range(count):
            for ring_x in range(1, rings + 1):
                for ring_y in range(1, rings + 1):
                    entries.append((name, k, ring_x, ring_y, "hi"))
    return entries


UNITS = halo_units()
CORNERS = corner_entries()
FACE_BLOCKS = len(UNITS)
SIDE_BLOCKS = (len(UNITS) + 1) // 2
CORNER_BLOCKS = (len(CORNERS) + 15) // 16


def position():
    i, j, s = (lax.axis_index(axis) for axis in AXES)
    return (i + 1) % 2, (j + 1) % 2, i, j, s


def split(value):
    top = value.astype(BF16).astype(F32)
    return top, value - top


def rigid_units(ring1, ring2, drive):
    lane = lax.broadcasted_iota(jnp.int32, ring1.shape, 1)
    half = ring1.shape[1] // 2
    top, rest = split(ring1)
    turned = pltpu.roll(rest, half, 1)
    first = jnp.where(lane < SOLID, turned, top)
    second = jnp.where(
        lane < 2, pltpu.roll(turned, half + 2, 1), pltpu.roll(turned, 4, 1)
    )
    strength = jnp.sum(drive, axis=1, keepdims=True)
    where = jnp.sum(jnp.where(drive != 0.0, lane.astype(F32), 0.0), axis=1, keepdims=True)
    hi, lo = split(strength)
    extra = jnp.where(lane == 4, hi, jnp.where(lane == 5, lo, where))
    second = jnp.where(lane < 4, second, jnp.where(lane < 7, extra, 0.0))
    return first, jnp.where(lane < SOLID, second, ring2)


def rigid_rows(first, second):
    lane = lax.broadcasted_iota(jnp.int32, first.shape, 1)
    size = first.shape[1]
    half = size // 2
    rest = jnp.where(lane < half, pltpu.roll(second, half - 4, 1), pltpu.roll(first, half, 1))
    rest = jnp.where(lane < size - 2, rest, pltpu.roll(second, size - 2, 1))
    ring1 = jnp.where(lane >= SOLID, first + rest, 0.0)
    ring2 = jnp.where(lane >= SOLID, second, 0.0)
    strength = second[:, 4:5] + second[:, 5:6]
    return ring1, ring2, jnp.where(lane.astype(F32) == second[:, 6:7], strength, 0.0)


def corner_blocks(units, high):
    at = {unit: value for unit, value in zip(UNITS, units)}
    nx = units[0].shape[0]
    rows = []
    for name, k, ring_x, ring_y, part in CORNERS:
        unit = at[name, k, ring_y, part]
        rows.append(
            jnp.where(high, unit[nx - ring_x : nx - ring_x + 1], unit[ring_x - 1 : ring_x])
        )
    rows += [jnp.zeros_like(rows[0])] * (-len(rows) % 16)
    return [
        jnp.concatenate(rows[n : n + 16], axis=0).astype(BF16) for n in range(0, len(rows), 16)
    ]


def side_units(ref, nx):
    blocks = [ref[n].astype(F32) for n in range(SIDE_BLOCKS)]
    return [blocks[n // 2][nx * (n % 2) : nx * (n % 2) + nx] for n in range(FACE_BLOCKS)]


def edge_units(u_ref, f_ref, p_ref, c_ref, s_ref, high):
    nx, ny = c_ref.shape[1:3]

    def column(value, ring):
        return jnp.where(high, value[:, ny - ring, :], value[:, ring - 1, :])

    rigid = rigid_units(column(c_ref[0], 1), column(c_ref[0], 2), column(s_ref[0], 1))
    units = []
    for name, k, ring, part in UNITS:
        if name == "a":
            units.append(rigid[ring - 1])
            continue
        if name == "f":
            value = f_ref[0, k // 3, k % 3].astype(F32)
        else:
            value = u_ref[0, k] if name == "u" else p_ref[k] if name == "p" else c_ref[1]
        value = column(value, ring)
        units.append(split(value)[1] if part == "lo" else value)
    return units


def unit_blocks(units):
    units = units + [jnp.zeros_like(units[0])] * (len(units) % 2)
    return [
        jnp.concatenate(units[n : n + 2], axis=0).astype(BF16) for n in range(0, len(units), 2)
    ]


def pack_kernel(
    u_in,
    v_in,
    f_in,
    lame_in,
    shear_in,
    buoy_in,
    depth_in,
    cols_in,
    amps_in,
    u_ref,
    f_ref,
    p_ref,
    c_ref,
    s_ref,
    y0_ref,
    v_ref,
    lame_ref,
    shear_ref,
    buoy_ref,
    depth_ref,
    cols_ref,
    amps_ref,
    sems,
):
    copies = [
        pltpu.make_async_copy(src, dst, sems.at[n])
        for n, (src, dst) in enumerate(
            (
                (depth_in, depth_ref),
                (cols_in, cols_ref),
                (amps_in, amps_ref),
                (buoy_in, buoy_ref),
                (shear_in, shear_ref),
                (lame_in, lame_ref),
                (u_in, u_ref),
                (v_in, v_ref),
                (f_in, f_ref),
            )
        )
    ]
    for copy in copies:
        copy.start()
    for copy in copies[:6]:
        copy.wait()
    nx, ny, nz = lame_ref.shape
    _, even_j, i, j, _ = position()
    total_y = ny * lax.axis_size("ty")
    base = i * nx * total_y + j * ny
    levels = lax.broadcasted_iota(jnp.int32, (ny, nz), 1).astype(F32)
    eye = lax.broadcasted_iota(jnp.int32, (ny, ny), 0) == lax.broadcasted_iota(
        jnp.int32, (ny, ny), 1
    )
    own_y = lax.broadcasted_iota(jnp.int32, (ny, cols_ref.shape[1]), 0)
    depth_all = depth_ref[...].astype(F32)
    for x in range(nx):
        depth = jnp.sum(jnp.where(eye, depth_all[x : x + 1, :], 0.0), axis=1, keepdims=True)
        buoy = STEP_SQUARED * buoy_ref[x]
        mu = jnp.where(levels >= depth, shear_ref[x], 0.0)
        c_ref[0, x] = buoy * mu
        c_ref[1, x] = buoy * (lame_ref[x] + mu)
        here = cols_ref[...] == own_y + (base + x * total_y)
        floor = levels == depth
        drive = []
        for t in range(STEPS):
            amp = jnp.sum(jnp.where(here, amps_ref[t], 0.0), axis=1, keepdims=True)
            drive.append(jnp.where(floor, buoy * amp, 0.0))
        s_ref[0, x] = drive[1]
        s_ref[1, x] = drive[2]
        p_ref[2, x] = drive[0]
    for copy in copies[6:8]:
        copy.wait()
    for x in range(nx):
        for k in range(3):
            p = 2.0 * u_ref[0, k, x] - v_ref[0, k, x]
            p_ref[k, x] = p + p_ref[k, x] if k == 2 else p
    copies[8].wait()
    for n, block in enumerate(
        unit_blocks(edge_units(u_ref, f_ref, p_ref, c_ref, s_ref, even_j == 1))
    ):
        y0_ref[n] = block


def face_kernel(
    u_ref, f_ref, p_ref, c_ref, s_ref, x0_ref, x1_ref, y1_ref, c0_ref, c1_ref
):
    nx = c_ref.shape[1]
    even_i, even_j = position()[:2]
    units = edge_units(u_ref, f_ref, p_ref, c_ref, s_ref, even_j == 0)
    for n, block in enumerate(unit_blocks(units)):
        y1_ref[n] = block
    for ref, high in ((c0_ref, even_i == 1), (c1_ref, even_i == 0)):
        for n, block in enumerate(corner_blocks(units, high)):
            ref[n] = block
    for dst, high in ((x0_ref, even_i == 1), (x1_ref, even_i == 0)):
        at = [jnp.where(high, nx - ring, ring - 1) for ring in (1, 2, 3)]
        rigid = rigid_units(c_ref[0, at[0]], c_ref[0, at[1]], s_ref[0, at[0]])
        for n, (name, k, ring, part) in enumerate(UNITS):
            x = at[ring - 1]
            if name == "f":
                dst[n] = f_ref[0, k // 3, k % 3, x]
            elif name == "a":
                dst[n] = rigid[ring - 1].astype(BF16)
            else:
                value = u_ref[0, k, x] if name == "u" else p_ref[k, x] if name == "p" else c_ref[1, x]
                dst[n] = (split(value)[1] if part == "lo" else value).astype(BF16)


def corner_kernel(y0_ref, x0_in, x1_in, x0_ref, x1_ref):
    del x0_in, x1_in
    even_i = position()[0]
    units = side_units(y0_ref, y0_ref.shape[1] // 2)
    for dst, high in ((x0_ref, even_i == 1), (x1_ref, even_i == 0)):
        for n, block in enumerate(corner_blocks(units, high)):
            dst[FACE_BLOCKS + n] = block


def beside_z(value):
    tiles = [value[:, n : n + 128] for n in range(0, value.shape[1], 128)]
    lane = lax.broadcasted_iota(jnp.int32, tiles[0].shape, 1)
    zero = jnp.zeros_like(tiles[0])
    ups = [pltpu.roll(tile, 127, 1) for tile in tiles] + [zero]
    downs = [zero] + [pltpu.roll(tile, 1, 1) for tile in tiles]
    up = [jnp.where(lane == 127, ups[n + 1], ups[n]) for n in range(len(tiles))]
    down = [jnp.where(lane == 0, downs[n], downs[n + 1]) for n in range(len(tiles))]
    return jnp.concatenate(up, axis=1), jnp.concatenate(down, axis=1)


def beside_y(value):
    return pltpu.roll(value, value.shape[0] - 1, 0), pltpu.roll(value, 1, 0)


def advance_row(t, x, cur, before, p_ref, c_ref, s_ref, zd, zs, rows):
    um = [cur[k, x - 1] for k in range(3)]
    uc = [cur[k, x] for k in range(3)]
    up = [cur[k, x + 1] for k in range(3)]
    dx = [up[k] - um[k] for k in range(3)]
    dz1 = zd[1, x]
    ys = [beside_y(uc[k]) for k in range(3)]
    tilt = [beside_y(value) for value in (dx[1], dx[0] + zd[2, x], dz1)]
    cross = (
        (tilt[0][0] - tilt[0][1]) + (zd[2, x + 1] - zd[2, x - 1]),
        tilt[1][0] - tilt[1][1],
        (tilt[2][0] - tilt[2][1]) + (zd[0, x + 1] - zd[0, x - 1]),
    )
    rigid, bulk = c_ref[0, x, :rows], c_ref[1, x, :rows]
    fresh = []
    for k in range(3):
        pairs = (um[k] + up[k], ys[k][0] + ys[k][1], zs[k, x])
        laplace = pairs[0] + pairs[1] + pairs[2] - 6.0 * uc[k]
        grad_div = pairs[k] - 2.0 * uc[k] + 0.25 * cross[k]
        if t == 0:
            carry = p_ref[k, x, :rows]
        else:
            carry = 2.0 * uc[k][:rows] - before[k, x, :rows]
            if k == 2:
                carry = carry + s_ref[t - 1, x, :rows]
        fresh.append(carry + rigid * laplace[:rows] + bulk * grad_div[:rows])
    return fresh


def imprint_row(t, x, cur, zd, c_ref, f_ref, fz_ref, rows):
    ga, gf = [], []
    for k in range(3):
        yp, ym = beside_y(cur[k, x])
        ga.append(
            (
                cur[k, x + 1, :rows] - cur[k, x - 1, :rows],
                (yp - ym)[:rows],
                zd[k, x, :rows],
            )
        )
        n, r = 3 * t + k, x - RING + 1
        yp, ym = beside_y(f_ref[n, r])
        gf.append(
            (
                f_ref[n, r + 1, :rows] - f_ref[n, r - 1, :rows],
                (yp - ym)[:rows],
                fz_ref[n, x - RING],
            )
        )
    div = (ga[0][0] + ga[1][1] + ga[2][2]) * (gf[0][0] + gf[1][1] + gf[2][2])
    both = ga[0][0] * gf[0][0]
    for k in range(3):
        for d in range(3):
            if k + d > 0:
                both = both + ga[k][d] * gf[k][d]
    return div, jnp.where(c_ref[0, x, :rows] > 0.0, both, 0.0)


def joined(get):
    n = 0
    while n < len(UNITS):
        name, k, ring, _ = UNITS[n]
        if name == "a":
            for entry in zip("ccs", (0, 0, 0), (1, 2, 1), rigid_rows(get(n), get(n + 1))):
                yield entry
            n += 2
            continue
        value = get(n)
        if name != "f" and ring == 1:
            value = value + get(n + 1)
            n += 1
        n += 1
        yield ("c", 1, ring, value) if name == "b" else (name, k, ring, value)


def joined_corner(get):
    n = 0
    while n < len(CORNERS):
        name, k, ring_x, ring_y, _ = CORNERS[n]
        if name == "a":
            for x in (1, 2):
                ring1, ring2, drive = rigid_rows(get(n), get(n + 1))
                yield "c", 0, x, 1, ring1
                yield "c", 0, x, 2, ring2
                if x == 1:
                    yield "s", 0, 1, 1, drive
                n += 2
            continue
        yield ("c", 1, ring_x, ring_y, get(n)) if name == "b" else (name, k, ring_x, ring_y, get(n))
        n += 1


def keep_z(k, x, value, zd, zs, rows=slice(None)):
    up, down = beside_z(value)
    zd[k, x, rows] = up - down
    zs[k, x, rows] = up + down


def middle_rows(nx):
    spans = [range(RING + 1 + t, RING + nx - 1 - t) for t in range(STEPS)]
    return [(span if t < STEPS - 1 else (), span) for t, span in enumerate(spans)]


def side_rows(nx, high):
    wide = nx + 2 * RING
    at = lambda rows: [jnp.where(high, wide - 1 - row, row) for row in rows]
    steps = []
    for t in range(STEPS):
        inner = range(RING, RING + 1 + t)
        outer = range(t + 1, RING + 1 + t) if t < STEPS - 1 else ()
        steps.append((at(outer), at(inner)))
    return steps


def run_steps(refs, fz_ref, sum_ref, sums, rows):
    nx, ny, nz = fz_ref.shape[1:]
    fields, c_ref = refs["fields"], refs["c"]
    wide_y = c_ref.shape[2]
    for t, (outer, inner) in enumerate(rows):
        cur, zd, zs = fields[t]
        for x in outer:
            nxt, nd, ns = fields[t + 1]
            fresh = advance_row(
                t, x, cur, fields[t - 1][0], refs["p"], c_ref, refs["s"], zd, zs, wide_y
            )
            for k in range(3):
                nxt[k, x] = fresh[k]
                keep_z(k, x, fresh[k], nd, ns)
        for x in inner:
            terms = imprint_row(t, x, cur, zd, c_ref, refs["f"], fz_ref, ny)
            for n in range(2):
                value = terms[n]
                own = x - RING
                if t > 0:
                    value = value + sum_ref[n, own]
                if t < STEPS - 1:
                    sum_ref[n, own] = value
                elif len(sums) == 1:
                    sums[0][n, own] = value
                else:
                    half = nz // 2
                    first = position()[4] == 0
                    sums[0][n, own] = jnp.where(first, value[:, :half], value[:, half:])
                    sums[1][n, own] = jnp.where(first, value[:, half:], value[:, :half])


def lay_out(theirs, message):
    top = jnp.zeros((1, 1), F32)
    for n in range(2):
        for row in range(theirs.shape[1]):
            top = jnp.maximum(top, jnp.max(jnp.abs(theirs[n, row]), axis=(0, 1), keepdims=True))
    power = jnp.floor(jnp.log(jnp.maximum(top, 1e-30)) * (1.0 / math.log(2.0)))
    scale = jnp.exp((TARGET - power) * math.log(2.0))
    for n in range(2):
        for row in range(theirs.shape[1]):
            message[n, row] = theirs[n, row] * scale
    message[0, theirs.shape[1]] = jnp.broadcast_to(power, theirs.shape[2:])
    message[1, theirs.shape[1]] = jnp.broadcast_to(power, theirs.shape[2:])


def run_side(refs, fz_ref, sum_ref, sums, high):
    nx = fz_ref.shape[1]
    wide = nx + 2 * RING
    field, zd, zs = refs["fields"][0]
    for row in range(RING):
        x = jnp.where(high, wide - 1 - row, row)
        for k in range(3):
            keep_z(k, x, field[k, x], zd, zs)
    run_steps(refs, fz_ref, sum_ref, sums, side_rows(nx, high))


def named(held):
    u, p, c, s, f, ud, us, v, w, vd, vs, wd, ws, under_way, *sums = held
    refs = {"u": u, "p": p, "c": c, "s": s, "f": f}
    refs["fields"] = ((u, ud, us), (v, vd, vs), (w, wd, ws))
    return refs, under_way, sums


def beyond(axis, even, index):
    other = jnp.where(even == 1, index - 1, index + 1)
    return (other >= 0) & (other < lax.axis_size(axis))


def stage_kernel(
    u_in, p_in, c_in, s_in, f_in, u_ref, p_ref, c_ref, s_ref, f_ref, ud_ref, us_ref, fz_ref
):
    nx, ny, nz = c_in.shape[1:]
    wide = u_ref.shape[2]
    for src, ref in ((u_in, u_ref), (p_in, p_ref), (c_in, c_ref), (s_in, s_ref)):
        lead = (0,) if src is u_in else ()
        for k in range(ref.shape[0]):
            for x in range(ref.shape[1]):
                if RING <= x < RING + nx:
                    value = src[lead + (k, x - RING)]
                    ref[k, x, :ny, :] = value
                    ref[k, x, ny:, :] = jnp.zeros((wide - ny, nz), F32)
                    if src is u_in:
                        keep_z(k, x, value, ud_ref, us_ref, slice(0, ny))
                else:
                    ref[k, x] = jnp.zeros(ref.shape[2:], F32)
    for k in range(3 * STEPS):
        for x in range(nx):
            value = f_in[0, k // 3, k % 3, x].astype(F32)
            f_ref[k, x + 1, :ny, :] = value
            f_ref[k, x + 1, ny:, :] = jnp.zeros((wide - ny, nz), F32)
            up, down = beside_z(value)
            fz_ref[k, x] = up - down
        for x in (0, nx + 1):
            f_ref[k, x] = jnp.zeros(f_ref.shape[2:], F32)


def early_kernel(fz_ref, y0_in, y1_in, *rest):
    refs, under_way, sums = named(rest[7:])
    u_ref, ud_ref, us_ref = refs["fields"][0]
    nx, ny, nz = fz_ref.shape[1:]
    wide = u_ref.shape[2]
    even_i, even_j, i, j, _ = position()
    ok_y1 = beyond("ty", even_j, j)

    near = side_units(y0_in, nx)
    far = [jnp.where(ok_y1, value, 0.0) for value in side_units(y1_in, nx)]
    top = [jnp.where(even_j == 1, a, b) for a, b in zip(near, far)]
    low = [jnp.where(even_j == 1, b, a) for a, b in zip(near, far)]
    for values, high in ((top, True), (low, False)):
        for name, k, ring, value in joined(lambda n: values[n]):
            y = ny - 1 + ring if high else wide - ring
            first = 1 if name == "f" else RING
            for x in range(nx):
                refs[name][k, first + x, y : y + 1, :] = value[x : x + 1]
    for x in range(RING, RING + nx):
        for k in range(3):
            keep_z(k, x, u_ref[k, x, ny:], ud_ref, us_ref, slice(ny, wide))
    run_steps(refs, fz_ref, under_way, sums, middle_rows(nx))

    @pl.when(jnp.logical_not(beyond("tx", even_i, i)))
    def _():
        run_side(refs, fz_ref, under_way, sums, even_i == 0)


def side_kernel(second, fz_ref, faces, corners, *rest):
    if second:
        *rest, message = rest
    refs, under_way, sums = named(rest[len(rest) // 2 :])
    nx, ny, nz = fz_ref.shape[1:]
    wide = refs["u"].shape[2]
    even_i, even_j, i, j, _ = position()
    high = even_i == (0 if second else 1)

    def run():
        for name, k, ring, value in joined(lambda n: faces[n].astype(F32)):
            first = 1 if name == "f" else RING
            x = jnp.where(high, first + nx - 1 + ring, first - ring)
            refs[name][k, x, :ny, :] = value
        near = [faces[FACE_BLOCKS + n].astype(F32) for n in range(CORNER_BLOCKS)]
        ok_y1 = beyond("ty", even_j, j)
        far = [jnp.where(ok_y1, corners[n].astype(F32), 0.0) for n in range(CORNER_BLOCKS)]
        for y_high in (True, False):
            flag = even_j == (1 if y_high else 0)
            values = [jnp.where(flag, a, b) for a, b in zip(near, far)]
            row = lambda n: values[n // 16][n % 16 : n % 16 + 1]
            for name, k, ring_x, ring_y, value in joined_corner(row):
                x = jnp.where(high, RING + nx - 1 + ring_x, RING - ring_x)
                y = ny - 1 + ring_y if y_high else wide - ring_y
                refs[name][k, x, y : y + 1, :] = value
        run_side(refs, fz_ref, under_way, sums, high)

    if second:
        pl.when(beyond("tx", even_i, i))(run)
    else:
        run()
    if second:
        lay_out(sums[-1], message)


def total_kernel(scale, own_ref, sent_ref, out_ref):
    nx = out_ref.shape[1]
    back = jnp.exp((sent_ref[0, nx] - TARGET) * math.log(2.0))
    for n in range(2):
        for x in range(nx):
            out_ref[n, x] = (own_ref[n, x] + sent_ref[n, x] * back) * scale


def last_kernel(w_ref, wd_ref, ws_ref, v_ref, c_ref, s_ref, out_ref):
    nx, ny = out_ref.shape[2:4]

    @pl.loop(RING, RING + nx, unroll=UNROLL)
    def _(x):
        fresh = advance_row(
            STEPS - 1, x, w_ref, v_ref, None, c_ref, s_ref, wd_ref, ws_ref, ny
        )
        for k in range(3):
            out_ref[0, k, x - RING] = fresh[k]


def swap_map(sizes, partner):
    nx, ny, ns = sizes

    def meets(i, j):
        a, b = partner(i, j)
        return 0 <= a < nx and 0 <= b < ny

    pairs = []
    for i in range(nx):
        for j in range(ny):
            for s in range(ns):
                if meets(i, j):
                    to = (*partner(i, j), s)
                elif not meets(i, j ^ 1):
                    to = (i, j ^ 1, s)
                else:
                    to = (i, j, s ^ 1 if s ^ 1 < ns else s)
                pairs.append(((i * ny + j) * ns + s, (to[0] * ny + to[1]) * ns + to[2]))
    return pairs


def body(
    adj_now,
    adj_later,
    forward_field,
    lame_first,
    shear,
    buoyancy,
    seafloor_depth,
    station_columns,
    station_traces,
):
    nx, ny, nz = lame_first.shape
    sizes = tuple(lax.axis_size(axis) for axis in AXES)
    count_s = sizes[2]
    vmem = pl.BlockSpec(memory_space=pltpu.VMEM)
    anywhere = pl.BlockSpec(memory_space=pl.ANY)
    limit = 30 * 1024 * 1024
    params = pltpu.CompilerParams(vmem_limit_bytes=limit)
    face = jax.ShapeDtypeStruct((FACE_BLOCKS + CORNER_BLOCKS, ny, nz), BF16)
    edge = jax.ShapeDtypeStruct((SIDE_BLOCKS, 2 * nx, nz), BF16)
    corner = jax.ShapeDtypeStruct((CORNER_BLOCKS + 1, 16, nz), BF16)
    grid = lambda n: jax.ShapeDtypeStruct((n, nx, ny, nz), F32)

    like = lambda value: jax.ShapeDtypeStruct(value.shape, value.dtype)
    traces = jnp.transpose(station_traces, (1, 0, 2))
    held = (adj_later, lame_first, shear, buoyancy, seafloor_depth, station_columns, traces)
    u0, fwd, carry, coeff, drive, y0 = pl.pallas_call(
        pack_kernel,
        out_shape=(
            like(adj_now),
            like(forward_field),
            grid(3),
            grid(2),
            grid(2),
            edge,
        ),
        in_specs=[anywhere] * 9,
        out_specs=(vmem,) * 6,
        scratch_shapes=[pltpu.VMEM(value.shape, value.dtype) for value in held]
        + [pltpu.SemaphoreType.DMA((9,))],
        compiler_params=params,
        name="pack",
    )(
        *(
            pltpu.with_memory_space_constraint(value, pltpu.HBM)
            for value in (adj_now, adj_later, forward_field, *held[1:])
        )
    )

    def exchange(value, partner):
        return lax.ppermute(value, AXES, swap_map(sizes, partner))

    flip = lambda n: n + 1 if n % 2 == 0 else n - 1
    back = lambda n: n - 1 if n % 2 == 0 else n + 1
    y0 = exchange(y0, lambda a, b: (a, flip(b)))
    x0, x1, y1, c0, c1 = pl.pallas_call(
        face_kernel,
        out_shape=(face, face, edge, corner, corner),
        in_specs=[vmem] * 5,
        out_specs=(vmem,) * 5,
        compiler_params=params,
        name="faces",
    )(u0, fwd, carry, coeff, drive)
    x0, x1 = pl.pallas_call(
        corner_kernel,
        out_shape=(face, face),
        in_specs=[vmem] * 3,
        out_specs=(vmem,) * 2,
        input_output_aliases={1: 0, 2: 1},
        compiler_params=params,
        name="corners",
    )(y0, x0, x1)
    x0 = exchange(x0, lambda a, b: (flip(a), b))
    x1 = exchange(x1, lambda a, b: (back(a), b))
    y1 = exchange(y1, lambda a, b: (a, back(b)))
    c0 = exchange(c0, lambda a, b: (flip(a), back(b)))
    c1 = exchange(c1, lambda a, b: (back(a), back(b)))

    wide_x, wide_y = nx + 2 * RING, ny + PAD
    padded = lambda n, x=wide_x: jax.ShapeDtypeStruct((n, x, wide_y, nz), F32)
    tile = (padded(3), padded(3), padded(2), padded(2), padded(3 * STEPS, nx + 2))
    split_up = count_s == 2
    depth = nz // 2 if split_up else nz
    sums = (jax.ShapeDtypeStruct((2, nx, ny, depth), F32),) * (1 + split_up)
    staged = (*tile, padded(3), padded(3))
    *held, fwd_z = pl.pallas_call(
        stage_kernel,
        out_shape=(*staged, grid(3 * STEPS)),
        in_specs=[vmem] * 5,
        out_specs=(vmem,) * 8,
        compiler_params=params,
        name="stage",
    )(u0, carry, coeff, drive, fwd)
    shapes = (*staged, *(padded(3),) * 6, grid(2), *sums)
    held = pl.pallas_call(
        early_kernel,
        out_shape=shapes,
        in_specs=[vmem] * 10,
        out_specs=(vmem,) * len(shapes),
        input_output_aliases={3 + n: n for n in range(7)},
        compiler_params=params,
        name="early",
    )(fwd_z, y0, y1, *held)

    def side(second, faces, corners, held):
        message = (jax.ShapeDtypeStruct((2, nx + 1, ny, depth), F32),) * second
        return pl.pallas_call(
            functools.partial(side_kernel, second),
            out_shape=(*shapes, *message),
            in_specs=[vmem] * (3 + len(shapes)),
            out_specs=(vmem,) * (len(shapes) + second),
            input_output_aliases={3 + n: n for n in range(len(shapes))},
            compiler_params=params,
            name="second" if second else "first",
        )(fwd_z, faces, corners, *held)

    held = side(False, x0, c0, held)
    *held, message = side(True, x1, c1, held)
    coeff, drive = held[2:4]
    u1, u2 = held[7:9]
    u2_d, u2_s = held[11:13]

    sums = held[14:]
    scale = 0.25 / (adj_now.shape[0] * count_s)
    if split_up:
        sent = lax.ppermute(message.astype(jnp.float16), "src", [(0, 1), (1, 0)])
        summed = pl.pallas_call(
            functools.partial(total_kernel, scale),
            out_shape=like(sums[0]),
            in_specs=[vmem] * 2,
            out_specs=vmem,
            compiler_params=params,
            name="total",
        )(sums[0], sent.astype(F32))
    else:
        summed = lax.psum_scatter(sums[0] * scale, "src", scatter_dimension=3, tiled=True)
    final = pl.pallas_call(
        last_kernel,
        out_shape=like(adj_now),
        in_specs=[vmem] * 6,
        out_specs=vmem,
        compiler_params=params,
        name="last",
    )(u2, u2_d, u2_s, u1, coeff, drive)
    return final, summed


def solution(mesh):
    in_specs = (
        P("src", None, "tx", "ty", None),
        P("src", None, "tx", "ty", None),
        P("src", None, None, "tx", "ty", None),
        P("tx", "ty", None),
        P("tx", "ty", None),
        P("tx", "ty", None),
        P("tx", "ty"),
        P("src", None),
        P("src", None, None),
    )
    out_specs = (P("src", None, "tx", "ty", None), P(None, "tx", "ty", "src"))
    return jax.shard_map(body, mesh=mesh, in_specs=in_specs, out_specs=out_specs, check_vma=False)
```

```python
import functools
import math

import jax
import jax.numpy as jnp
from jax import lax
from jax.experimental import pallas as pl
from jax.experimental.pallas import tpu as pltpu
from jax.sharding import PartitionSpec as P

STEPS = 3
STEP_SQUARED = 0.04
RING = 3
SOLID = 126
PAD = 8
AXES = ("tx", "ty", "src")
F32 = jnp.float32
BF16 = jnp.bfloat16
UNROLL = 8
TARGET = 13.0


def halo_units():
    units = []
    for name, count, rings in (("u", 3, 3), ("p", 3, 2), ("b", 1, 2)):
        for k in range(count):
            for ring in range(1, rings + 1):
                units.append((name, k, ring, "hi"))
                if ring == 1 and name != "b":
                    units.append((name, k, ring, "lo"))
    units += [("a", 0, 1, "hi"), ("a", 0, 2, "hi")]
    for k in range(3 * STEPS):
        units.append(("f", k, 1, "hi"))
    return units


def corner_entries():
    entries = []
    for name, count, rings in (("u", 3, 3), ("p", 3, 2), ("b", 1, 2), ("a", 1, 2)):
        for k in range(count):
            for ring_x in range(1, rings + 1):
                for ring_y in range(1, rings + 1):
                    entries.append((name, k, ring_x, ring_y, "hi"))
    return entries


UNITS = halo_units()
CORNERS = corner_entries()
FACE_BLOCKS = len(UNITS)
SIDE_BLOCKS = (len(UNITS) + 1) // 2
CORNER_BLOCKS = (len(CORNERS) + 15) // 16


def position():
    i, j, s = (lax.axis_index(axis) for axis in AXES)
    return (i + 1) % 2, (j + 1) % 2, i, j, s


def split(value):
    top = value.astype(BF16).astype(F32)
    return top, value - top


def rigid_units(ring1, ring2, drive):
    lane = lax.broadcasted_iota(jnp.int32, ring1.shape, 1)
    half = ring1.shape[1] // 2
    top, rest = split(ring1)
    turned = pltpu.roll(rest, half, 1)
    first = jnp.where(lane < SOLID, turned, top)
    second = jnp.where(
        lane < 2, pltpu.roll(turned, half + 2, 1), pltpu.roll(turned, 4, 1)
    )
    strength = jnp.sum(drive, axis=1, keepdims=True)
    where = jnp.sum(jnp.where(drive != 0.0, lane.astype(F32), 0.0), axis=1, keepdims=True)
    hi, lo = split(strength)
    extra = jnp.where(lane == 4, hi, jnp.where(lane == 5, lo, where))
    second = jnp.where(lane < 4, second, jnp.where(lane < 7, extra, 0.0))
    return first, jnp.where(lane < SOLID, second, ring2)


def rigid_rows(first, second):
    lane = lax.broadcasted_iota(jnp.int32, first.shape, 1)
    size = first.shape[1]
    half = size // 2
    rest = jnp.where(lane < half, pltpu.roll(second, half - 4, 1), pltpu.roll(first, half, 1))
    rest = jnp.where(lane < size - 2, rest, pltpu.roll(second, size - 2, 1))
    ring1 = jnp.where(lane >= SOLID, first + rest, 0.0)
    ring2 = jnp.where(lane >= SOLID, second, 0.0)
    strength = second[:, 4:5] + second[:, 5:6]
    return ring1, ring2, jnp.where(lane.astype(F32) == second[:, 6:7], strength, 0.0)


def corner_blocks(units, high):
    at = {unit: value for unit, value in zip(UNITS, units)}
    nx = units[0].shape[0]
    rows = []
    for name, k, ring_x, ring_y, part in CORNERS:
        unit = at[name, k, ring_y, part]
        rows.append(
            jnp.where(high, unit[nx - ring_x : nx - ring_x + 1], unit[ring_x - 1 : ring_x])
        )
    rows += [jnp.zeros_like(rows[0])] * (-len(rows) % 16)
    return [
        jnp.concatenate(rows[n : n + 16], axis=0).astype(BF16) for n in range(0, len(rows), 16)
    ]


def side_units(ref, nx):
    blocks = [ref[n].astype(F32) for n in range(SIDE_BLOCKS)]
    return [blocks[n // 2][nx * (n % 2) : nx * (n % 2) + nx] for n in range(FACE_BLOCKS)]


def edge_units(u_ref, f_ref, p_ref, c_ref, s_ref, high, ready=lambda name: None):
    nx, ny = c_ref.shape[1:3]

    def column(value, ring):
        return jnp.where(high, value[:, ny - ring, :], value[:, ring - 1, :])

    rigid = rigid_units(column(c_ref[0], 1), column(c_ref[0], 2), column(s_ref[0], 1))
    made = {}
    for wanted in "abfup":
        ready(wanted)
        for unit in UNITS:
            name, k, ring, part = unit
            if name != wanted:
                continue
            if name == "a":
                made[unit] = rigid[ring - 1]
                continue
            if name == "f":
                value = f_ref[0, k // 3, k % 3].astype(F32)
            else:
                value = u_ref[0, k] if name == "u" else p_ref[k] if name == "p" else c_ref[1]
            value = column(value, ring)
            made[unit] = split(value)[1] if part == "lo" else value
    return [made[unit] for unit in UNITS]


def unit_blocks(units):
    units = units + [jnp.zeros_like(units[0])] * (len(units) % 2)
    return [
        jnp.concatenate(units[n : n + 2], axis=0).astype(BF16) for n in range(0, len(units), 2)
    ]


def pack_kernel(
    u_in,
    v_in,
    f_in,
    lame_in,
    shear_in,
    buoy_in,
    depth_in,
    cols_in,
    amps_in,
    u_ref,
    f_ref,
    p_ref,
    c_ref,
    s_ref,
    y0_ref,
    v_ref,
    lame_ref,
    shear_ref,
    buoy_ref,
    depth_ref,
    cols_ref,
    amps_ref,
    sems,
):
    copies = [
        pltpu.make_async_copy(src, dst, sems.at[n])
        for n, (src, dst) in enumerate(
            (
                (depth_in, depth_ref),
                (cols_in, cols_ref),
                (amps_in, amps_ref),
                (buoy_in, buoy_ref),
                (shear_in, shear_ref),
                (lame_in, lame_ref),
                (f_in, f_ref),
                (u_in, u_ref),
                (v_in, v_ref),
            )
        )
    ]
    for copy in copies:
        copy.start()
    for copy in copies[:6]:
        copy.wait()
    nx, ny, nz = lame_ref.shape
    _, even_j, i, j, _ = position()
    total_y = ny * lax.axis_size("ty")
    base = i * nx * total_y + j * ny
    levels = lax.broadcasted_iota(jnp.int32, (ny, nz), 1).astype(F32)
    eye = lax.broadcasted_iota(jnp.int32, (ny, ny), 0) == lax.broadcasted_iota(
        jnp.int32, (ny, ny), 1
    )
    own_y = lax.broadcasted_iota(jnp.int32, (ny, cols_ref.shape[1]), 0)
    depth_all = depth_ref[...].astype(F32)
    for x in range(nx):
        depth = jnp.sum(jnp.where(eye, depth_all[x : x + 1, :], 0.0), axis=1, keepdims=True)
        buoy = STEP_SQUARED * buoy_ref[x]
        mu = jnp.where(levels >= depth, shear_ref[x], 0.0)
        c_ref[0, x] = buoy * mu
        c_ref[1, x] = buoy * (lame_ref[x] + mu)
        here = cols_ref[...] == own_y + (base + x * total_y)
        floor = levels == depth
        drive = []
        for t in range(STEPS):
            amp = jnp.sum(jnp.where(here, amps_ref[t], 0.0), axis=1, keepdims=True)
            drive.append(jnp.where(floor, buoy * amp, 0.0))
        s_ref[0, x] = drive[1]
        s_ref[1, x] = drive[2]
        p_ref[2, x] = drive[0]

    def ready(name):
        if name == "f":
            copies[6].wait()
        elif name == "u":
            copies[7].wait()
        elif name == "p":
            copies[8].wait()
            for x in range(nx):
                for k in range(3):
                    p = 2.0 * u_ref[0, k, x] - v_ref[0, k, x]
                    p_ref[k, x] = p + p_ref[k, x] if k == 2 else p

    units = edge_units(u_ref, f_ref, p_ref, c_ref, s_ref, even_j == 1, ready)
    for n, block in enumerate(unit_blocks(units)):
        y0_ref[n] = block


def face_kernel(
    u_ref, f_ref, p_ref, c_ref, s_ref, x0_ref, x1_ref, y1_ref, c0_ref, c1_ref, wide_ref, fz_ref
):
    nx = c_ref.shape[1]
    even_i, even_j = position()[:2]
    units = edge_units(u_ref, f_ref, p_ref, c_ref, s_ref, even_j == 0)
    for n, block in enumerate(unit_blocks(units)):
        y1_ref[n] = block
    for ref, high in ((c0_ref, even_i == 1), (c1_ref, even_i == 0)):
        for n, block in enumerate(corner_blocks(units, high)):
            ref[n] = block
    for dst, high in ((x0_ref, even_i == 1), (x1_ref, even_i == 0)):
        at = [jnp.where(high, nx - ring, ring - 1) for ring in (1, 2, 3)]
        rigid = rigid_units(c_ref[0, at[0]], c_ref[0, at[1]], s_ref[0, at[0]])
        for n, (name, k, ring, part) in enumerate(UNITS):
            x = at[ring - 1]
            if name == "f":
                dst[n] = f_ref[0, k // 3, k % 3, x]
            elif name == "a":
                dst[n] = rigid[ring - 1].astype(BF16)
            else:
                value = u_ref[0, k, x] if name == "u" else p_ref[k, x] if name == "p" else c_ref[1, x]
                dst[n] = (split(value)[1] if part == "lo" else value).astype(BF16)
    stage_forward(f_ref, wide_ref, fz_ref)


def stage_forward(f_in, f_ref, fz_ref):
    nx, ny, nz = fz_ref.shape[1:]
    wide = f_ref.shape[2]
    for k in range(3 * STEPS):
        for x in range(nx):
            value = f_in[0, k // 3, k % 3, x].astype(F32)
            f_ref[k, x + 1, :ny, :] = value
            f_ref[k, x + 1, ny:, :] = jnp.zeros((wide - ny, nz), F32)
            up, down = beside_z(value)
            fz_ref[k, x] = up - down
        for x in (0, nx + 1):
            f_ref[k, x] = jnp.zeros(f_ref.shape[2:], F32)


def corner_kernel(y0_ref, x0_in, x1_in, x0_ref, x1_ref):
    del x0_in, x1_in
    even_i = position()[0]
    units = side_units(y0_ref, y0_ref.shape[1] // 2)
    for dst, high in ((x0_ref, even_i == 1), (x1_ref, even_i == 0)):
        for n, block in enumerate(corner_blocks(units, high)):
            dst[FACE_BLOCKS + n] = block


def beside_z(value):
    tiles = [value[:, n : n + 128] for n in range(0, value.shape[1], 128)]
    lane = lax.broadcasted_iota(jnp.int32, tiles[0].shape, 1)
    zero = jnp.zeros_like(tiles[0])
    ups = [pltpu.roll(tile, 127, 1) for tile in tiles] + [zero]
    downs = [zero] + [pltpu.roll(tile, 1, 1) for tile in tiles]
    up = [jnp.where(lane == 127, ups[n + 1], ups[n]) for n in range(len(tiles))]
    down = [jnp.where(lane == 0, downs[n], downs[n + 1]) for n in range(len(tiles))]
    return jnp.concatenate(up, axis=1), jnp.concatenate(down, axis=1)


def beside_y(value):
    return pltpu.roll(value, value.shape[0] - 1, 0), pltpu.roll(value, 1, 0)


class Row:
    def __init__(self, x, cur, zd):
        self.x = x
        self.um, self.uc, self.up = ([cur[k, x + d] for k in range(3)] for d in (-1, 0, 1))
        self.ys = [beside_y(self.uc[k]) for k in range(3)]
        self.zd = zd
        self.dx = [self.up[k] - self.um[k] for k in range(3)]

    def slopes(self, rows):
        return [
            (self.dx[k][:rows], (self.ys[k][0] - self.ys[k][1])[:rows], self.zd[k, self.x, :rows])
            for k in range(3)
        ]


def advance_row(t, row, before, p_ref, c_ref, s_ref, zs, rows):
    x, um, uc, up, dx, ys, zd = row.x, row.um, row.uc, row.up, row.dx, row.ys, row.zd
    dz1 = zd[1, x]
    tilt = [beside_y(value) for value in (dx[1], dx[0] + zd[2, x], dz1)]
    cross = (
        (tilt[0][0] - tilt[0][1]) + (zd[2, x + 1] - zd[2, x - 1]),
        tilt[1][0] - tilt[1][1],
        (tilt[2][0] - tilt[2][1]) + (zd[0, x + 1] - zd[0, x - 1]),
    )
    rigid, bulk = c_ref[0, x, :rows], c_ref[1, x, :rows]
    fresh = []
    for k in range(3):
        pairs = (um[k] + up[k], ys[k][0] + ys[k][1], zs[k, x])
        laplace = pairs[0] + pairs[1] + pairs[2] - 6.0 * uc[k]
        grad_div = pairs[k] - 2.0 * uc[k] + 0.25 * cross[k]
        if t == 0:
            carry = p_ref[k, x, :rows]
        else:
            carry = 2.0 * uc[k][:rows] - before[k, x, :rows]
            if k == 2:
                carry = carry + s_ref[t - 1, x, :rows]
        fresh.append(carry + rigid * laplace[:rows] + bulk * grad_div[:rows])
    return fresh


def imprint_row(t, row, c_ref, f_ref, fz_ref, rows):
    x = row.x
    ga = row.slopes(rows)
    gf = []
    for k in range(3):
        n, r = 3 * t + k, x - RING + 1
        yp, ym = beside_y(f_ref[n, r])
        gf.append(
            (
                f_ref[n, r + 1, :rows] - f_ref[n, r - 1, :rows],
                (yp - ym)[:rows],
                fz_ref[n, x - RING],
            )
        )
    div = (ga[0][0] + ga[1][1] + ga[2][2]) * (gf[0][0] + gf[1][1] + gf[2][2])
    both = ga[0][0] * gf[0][0]
    for k in range(3):
        for d in range(3):
            if k + d > 0:
                both = both + ga[k][d] * gf[k][d]
    return div, jnp.where(c_ref[0, x, :rows] > 0.0, both, 0.0)


def joined(get):
    n = 0
    while n < len(UNITS):
        name, k, ring, _ = UNITS[n]
        if name == "a":
            for entry in zip("ccs", (0, 0, 0), (1, 2, 1), rigid_rows(get(n), get(n + 1))):
                yield entry
            n += 2
            continue
        value = get(n)
        if name in "up" and ring == 1:
            value = value + get(n + 1)
            n += 1
        n += 1
        yield ("c", 1, ring, value) if name == "b" else (name, k, ring, value)


def joined_corner(get):
    n = 0
    while n < len(CORNERS):
        name, k, ring_x, ring_y, _ = CORNERS[n]
        if name == "a":
            for x in (1, 2):
                ring1, ring2, drive = rigid_rows(get(n), get(n + 1))
                yield "c", 0, x, 1, ring1
                yield "c", 0, x, 2, ring2
                if x == 1:
                    yield "s", 0, 1, 1, drive
                n += 2
            continue
        yield ("c", 1, ring_x, ring_y, get(n)) if name == "b" else (name, k, ring_x, ring_y, get(n))
        n += 1


def keep_z(k, x, value, zd, zs, rows=slice(None)):
    up, down = beside_z(value)
    zd[k, x, rows] = up - down
    zs[k, x, rows] = up + down


def middle_rows(nx):
    spans = [range(RING + 1 + t, RING + nx - 1 - t) for t in range(STEPS)]
    return [(span if t < STEPS - 1 else (), span) for t, span in enumerate(spans)]


def side_rows():
    steps = []
    for t in range(STEPS):
        outer = range(t + 1, RING + 1 + t) if t < STEPS - 1 else ()
        steps.append((outer, range(RING, RING + 1 + t)))
    return steps


def run_steps(refs, fz_ref, sum_ref, sums, rows, at):
    nx, ny, nz = fz_ref.shape[1:]
    fields, c_ref = refs["fields"], refs["c"]
    wide_y = c_ref.shape[2]
    for t, (outer, inner) in enumerate(rows):
        cur, zd, zs = fields[t]
        for m in sorted({*outer, *inner}):
            row = Row(at(m), cur, zd)
            x = row.x
            if m in outer:
                nxt, nd, ns = fields[t + 1]
                fresh = advance_row(
                    t, row, fields[t - 1][0], refs["p"], c_ref, refs["s"], zs, wide_y
                )
                for k in range(3):
                    nxt[k, x] = fresh[k]
                    keep_z(k, x, fresh[k], nd, ns)
            if m not in inner:
                continue
            terms = imprint_row(t, row, c_ref, refs["f"], fz_ref, ny)
            for n in range(2):
                value = terms[n]
                own = x - RING
                if t > 0:
                    value = value + sum_ref[n, own]
                if t < STEPS - 1:
                    sum_ref[n, own] = value
                elif len(sums) == 1:
                    sums[0][n, own] = value
                else:
                    half = nz // 2
                    first = position()[4] == 0
                    sums[0][n, own] = jnp.where(first, value[:, :half], value[:, half:])
                    sums[1][n, own] = jnp.where(first, value[:, half:], value[:, :half])


def lay_out(theirs, message):
    top = jnp.zeros((1, 1), F32)
    for n in range(2):
        for row in range(theirs.shape[1]):
            top = jnp.maximum(top, jnp.max(jnp.abs(theirs[n, row]), axis=(0, 1), keepdims=True))
    power = jnp.floor(jnp.log(jnp.maximum(top, 1e-30)) * (1.0 / math.log(2.0)))
    scale = jnp.exp((TARGET - power) * math.log(2.0))
    for n in range(2):
        for row in range(theirs.shape[1]):
            message[n, row] = theirs[n, row] * scale
    message[0, theirs.shape[1]] = jnp.broadcast_to(power, theirs.shape[2:])
    message[1, theirs.shape[1]] = jnp.broadcast_to(power, theirs.shape[2:])


def run_side(refs, fz_ref, sum_ref, sums, high):
    nx = fz_ref.shape[1]
    wide = nx + 2 * RING
    field, zd, zs = refs["fields"][0]
    for row in range(RING):
        x = jnp.where(high, wide - 1 - row, row)
        for k in range(3):
            keep_z(k, x, field[k, x], zd, zs)
    at = lambda row: jnp.where(high, wide - 1 - row, row)
    run_steps(refs, fz_ref, sum_ref, sums, side_rows(), at)


def named(held):
    u, p, c, s, f, ud, us, v, w, vd, vs, wd, ws, under_way, *sums = held
    refs = {"u": u, "p": p, "c": c, "s": s, "f": f}
    refs["fields"] = ((u, ud, us), (v, vd, vs), (w, wd, ws))
    return refs, under_way, sums


def beyond(axis, even, index):
    other = jnp.where(even == 1, index - 1, index + 1)
    return (other >= 0) & (other < lax.axis_size(axis))


def stage_kernel(u_in, p_in, c_in, s_in, u_ref, p_ref, c_ref, s_ref, ud_ref, us_ref):
    nx, ny, nz = c_in.shape[1:]
    wide = u_ref.shape[2]
    for src, ref in ((u_in, u_ref), (p_in, p_ref), (c_in, c_ref), (s_in, s_ref)):
        lead = (0,) if src is u_in else ()
        for k in range(ref.shape[0]):
            for x in range(ref.shape[1]):
                if RING <= x < RING + nx:
                    value = src[lead + (k, x - RING)]
                    ref[k, x, :ny, :] = value
                    ref[k, x, ny:, :] = jnp.zeros((wide - ny, nz), F32)
                    if src is u_in:
                        keep_z(k, x, value, ud_ref, us_ref, slice(0, ny))
                else:
                    ref[k, x] = jnp.zeros(ref.shape[2:], F32)


def early_kernel(fz_ref, y0_in, y1_in, *rest):
    refs, under_way, sums = named(rest[7:])
    u_ref, ud_ref, us_ref = refs["fields"][0]
    nx, ny, nz = fz_ref.shape[1:]
    wide = u_ref.shape[2]
    even_i, even_j, i, j, _ = position()
    ok_y1 = beyond("ty", even_j, j)

    near = side_units(y0_in, nx)
    far = [jnp.where(ok_y1, value, 0.0) for value in side_units(y1_in, nx)]
    top = [jnp.where(even_j == 1, a, b) for a, b in zip(near, far)]
    low = [jnp.where(even_j == 1, b, a) for a, b in zip(near, far)]
    for values, high in ((top, True), (low, False)):
        for name, k, ring, value in joined(lambda n: values[n]):
            y = ny - 1 + ring if high else wide - ring
            first = 1 if name == "f" else RING
            for x in range(nx):
                refs[name][k, first + x, y : y + 1, :] = value[x : x + 1]
    for x in range(RING, RING + nx):
        for k in range(3):
            keep_z(k, x, u_ref[k, x, ny:], ud_ref, us_ref, slice(ny, wide))
    run_steps(refs, fz_ref, under_way, sums, middle_rows(nx), lambda row: row)

    @pl.when(jnp.logical_not(beyond("tx", even_i, i)))
    def _():
        run_side(refs, fz_ref, under_way, sums, even_i == 0)


def side_kernel(second, fz_ref, faces, corners, *rest):
    if second:
        *rest, message = rest
    refs, under_way, sums = named(rest[len(rest) // 2 :])
    nx, ny, nz = fz_ref.shape[1:]
    wide = refs["u"].shape[2]
    even_i, even_j, i, j, _ = position()
    high = even_i == (0 if second else 1)

    def run():
        for name, k, ring, value in joined(lambda n: faces[n].astype(F32)):
            first = 1 if name == "f" else RING
            x = jnp.where(high, first + nx - 1 + ring, first - ring)
            refs[name][k, x, :ny, :] = value
        near = [faces[FACE_BLOCKS + n].astype(F32) for n in range(CORNER_BLOCKS)]
        ok_y1 = beyond("ty", even_j, j)
        far = [jnp.where(ok_y1, corners[n].astype(F32), 0.0) for n in range(CORNER_BLOCKS)]
        for y_high in (True, False):
            flag = even_j == (1 if y_high else 0)
            values = [jnp.where(flag, a, b) for a, b in zip(near, far)]
            row = lambda n: values[n // 16][n % 16 : n % 16 + 1]
            for name, k, ring_x, ring_y, value in joined_corner(row):
                x = jnp.where(high, RING + nx - 1 + ring_x, RING - ring_x)
                y = ny - 1 + ring_y if y_high else wide - ring_y
                refs[name][k, x, y : y + 1, :] = value
        run_side(refs, fz_ref, under_way, sums, high)

    if second:
        pl.when(beyond("tx", even_i, i))(run)
    else:
        run()
    if second:
        lay_out(sums[-1], message)


def total_kernel(scale, own_ref, sent_ref, out_ref, stage, sems):
    nx = own_ref.shape[1]
    back = jnp.exp((sent_ref[0, nx] - TARGET) * math.log(2.0))
    copies = []
    for n in range(2):
        for x in range(nx):
            stage[n, x] = (own_ref[n, x] + sent_ref[n, x] * back) * scale
        copies.append(pltpu.make_async_copy(stage.at[n], out_ref.at[n], sems.at[n]))
        copies[n].start()
    for copy in copies:
        copy.wait()


def last_kernel(w_ref, wd_ref, ws_ref, v_ref, c_ref, s_ref, out_ref):
    nx, ny = out_ref.shape[2:4]

    @pl.loop(RING, RING + nx, unroll=UNROLL)
    def _(x):
        fresh = advance_row(
            STEPS - 1, Row(x, w_ref, wd_ref), v_ref, None, c_ref, s_ref, ws_ref, ny
        )
        for k in range(3):
            out_ref[0, k, x - RING] = fresh[k]


def swap_map(sizes, partner):
    nx, ny, ns = sizes

    def meets(i, j):
        a, b = partner(i, j)
        return 0 <= a < nx and 0 <= b < ny

    pairs = []
    for i in range(nx):
        for j in range(ny):
            for s in range(ns):
                if meets(i, j):
                    to = (*partner(i, j), s)
                elif not meets(i, j ^ 1):
                    to = (i, j ^ 1, s)
                else:
                    to = (i, j, s ^ 1 if s ^ 1 < ns else s)
                pairs.append(((i * ny + j) * ns + s, (to[0] * ny + to[1]) * ns + to[2]))
    return pairs


def body(
    adj_now,
    adj_later,
    forward_field,
    lame_first,
    shear,
    buoyancy,
    seafloor_depth,
    station_columns,
    station_traces,
):
    nx, ny, nz = lame_first.shape
    sizes = tuple(lax.axis_size(axis) for axis in AXES)
    count_s = sizes[2]
    vmem = pl.BlockSpec(memory_space=pltpu.VMEM)
    anywhere = pl.BlockSpec(memory_space=pl.ANY)
    limit = 30 * 1024 * 1024
    params = pltpu.CompilerParams(vmem_limit_bytes=limit)
    face = jax.ShapeDtypeStruct((FACE_BLOCKS + CORNER_BLOCKS, ny, nz), BF16)
    edge = jax.ShapeDtypeStruct((SIDE_BLOCKS, 2 * nx, nz), BF16)
    corner = jax.ShapeDtypeStruct((CORNER_BLOCKS + 1, 16, nz), BF16)
    grid = lambda n: jax.ShapeDtypeStruct((n, nx, ny, nz), F32)

    like = lambda value: jax.ShapeDtypeStruct(value.shape, value.dtype)
    traces = jnp.transpose(station_traces, (1, 0, 2))
    held = (adj_later, lame_first, shear, buoyancy, seafloor_depth, station_columns, traces)
    u0, fwd, carry, coeff, drive, y0 = pl.pallas_call(
        pack_kernel,
        out_shape=(
            like(adj_now),
            like(forward_field),
            grid(3),
            grid(2),
            grid(2),
            edge,
        ),
        in_specs=[anywhere] * 9,
        out_specs=(vmem,) * 6,
        scratch_shapes=[pltpu.VMEM(value.shape, value.dtype) for value in held]
        + [pltpu.SemaphoreType.DMA((9,))],
        compiler_params=params,
        name="pack",
    )(
        *(
            pltpu.with_memory_space_constraint(value, pltpu.HBM)
            for value in (adj_now, adj_later, forward_field, *held[1:])
        )
    )

    def exchange(value, partner):
        return lax.ppermute(value, AXES, swap_map(sizes, partner))

    flip = lambda n: n + 1 if n % 2 == 0 else n - 1
    back = lambda n: n - 1 if n % 2 == 0 else n + 1
    y0 = exchange(y0, lambda a, b: (a, flip(b)))
    wide_x, wide_y = nx + 2 * RING, ny + PAD
    padded = lambda n, x=wide_x: jax.ShapeDtypeStruct((n, x, wide_y, nz), F32)
    x0, x1, y1, c0, c1, fwd, fwd_z = pl.pallas_call(
        face_kernel,
        out_shape=(
            face,
            face,
            edge,
            corner,
            corner,
            padded(3 * STEPS, nx + 2),
            grid(3 * STEPS),
        ),
        in_specs=[vmem] * 5,
        out_specs=(vmem,) * 7,
        compiler_params=params,
        name="faces",
    )(u0, fwd, carry, coeff, drive)
    x0, x1 = pl.pallas_call(
        corner_kernel,
        out_shape=(face, face),
        in_specs=[vmem] * 3,
        out_specs=(vmem,) * 2,
        input_output_aliases={1: 0, 2: 1},
        compiler_params=params,
        name="corners",
    )(y0, x0, x1)
    x0 = exchange(x0, lambda a, b: (flip(a), b))
    x1 = exchange(x1, lambda a, b: (back(a), b))
    y1 = exchange(y1, lambda a, b: (a, back(b)))
    c0 = exchange(c0, lambda a, b: (flip(a), back(b)))
    c1 = exchange(c1, lambda a, b: (back(a), back(b)))

    tile = (padded(3), padded(3), padded(2), padded(2))
    split_up = count_s == 2
    depth = nz // 2 if split_up else nz
    sums = (jax.ShapeDtypeStruct((2, nx, ny, depth), F32),) * (1 + split_up)
    held = pl.pallas_call(
        stage_kernel,
        out_shape=(*tile, padded(3), padded(3)),
        in_specs=[vmem] * 4,
        out_specs=(vmem,) * 6,
        compiler_params=params,
        name="stage",
    )(u0, carry, coeff, drive)
    held = (*held[:4], fwd, *held[4:])
    staged = (*tile, like(fwd), padded(3), padded(3))
    shapes = (*staged, *(padded(3),) * 6, grid(2), *sums)
    held = pl.pallas_call(
        early_kernel,
        out_shape=shapes,
        in_specs=[vmem] * 10,
        out_specs=(vmem,) * len(shapes),
        input_output_aliases={3 + n: n for n in range(7)},
        compiler_params=params,
        name="early",
    )(fwd_z, y0, y1, *held)

    def side(second, faces, corners, held):
        message = (jax.ShapeDtypeStruct((2, nx + 1, ny, depth), F32),) * second
        return pl.pallas_call(
            functools.partial(side_kernel, second),
            out_shape=(*shapes, *message),
            in_specs=[vmem] * (3 + len(shapes)),
            out_specs=(vmem,) * (len(shapes) + second),
            input_output_aliases={3 + n: n for n in range(len(shapes))},
            compiler_params=params,
            name="second" if second else "first",
        )(fwd_z, faces, corners, *held)

    held = side(False, x0, c0, held)
    *held, message = side(True, x1, c1, held)
    coeff, drive = held[2:4]
    u1, u2 = held[7:9]
    u2_d, u2_s = held[11:13]

    sums = held[14:]
    scale = 0.25 / (adj_now.shape[0] * count_s)
    if split_up:
        sent = lax.ppermute(message.astype(jnp.float16), "src", [(0, 1), (1, 0)])
        summed = pl.pallas_call(
            functools.partial(total_kernel, scale),
            out_shape=like(sums[0]),
            in_specs=[vmem] * 2,
            out_specs=anywhere,
            scratch_shapes=[
                pltpu.VMEM(sums[0].shape, F32),
                pltpu.SemaphoreType.DMA((2,)),
            ],
            compiler_params=params,
            name="total",
        )(sums[0], sent.astype(F32))
    else:
        summed = lax.psum_scatter(sums[0] * scale, "src", scatter_dimension=3, tiled=True)
    final = pl.pallas_call(
        last_kernel,
        out_shape=like(adj_now),
        in_specs=[vmem] * 6,
        out_specs=vmem,
        compiler_params=params,
        name="last",
    )(u2, u2_d, u2_s, u1, coeff, drive)
    return final, summed


def solution(mesh):
    in_specs = (
        P("src", None, "tx", "ty", None),
        P("src", None, "tx", "ty", None),
        P("src", None, None, "tx", "ty", None),
        P("tx", "ty", None),
        P("tx", "ty", None),
        P("tx", "ty", None),
        P("tx", "ty"),
        P("src", None),
        P("src", None, None),
    )
    out_specs = (P("src", None, "tx", "ty", None), P(None, "tx", "ty", "src"))
    return jax.shard_map(body, mesh=mesh, in_specs=in_specs, out_specs=out_specs, check_vma=False)
```

```python
import functools
import math

import jax
import jax.numpy as jnp
from jax import lax
from jax.experimental import pallas as pl
from jax.experimental.pallas import tpu as pltpu
from jax.sharding import PartitionSpec as P

STEPS = 3
STEP_SQUARED = 0.04
RING = 3
SOLID = 126
PAD = 8
AXES = ("tx", "ty", "src")
F32 = jnp.float32
BF16 = jnp.bfloat16
UNROLL = 8
TARGET = 13.0


def halo_units():
    units = []
    for name, count, rings in (("u", 3, 3), ("p", 3, 2), ("b", 1, 2)):
        for k in range(count):
            for ring in range(1, rings + 1):
                units.append((name, k, ring, "hi"))
                if ring == 1 and name != "b":
                    units.append((name, k, ring, "lo"))
    units += [("a", 0, 1, "hi"), ("a", 0, 2, "hi")]
    for k in range(3 * STEPS):
        units.append(("f", k, 1, "hi"))
    return units


def corner_entries():
    entries = []
    for name, count, rings in (("u", 3, 3), ("p", 3, 2), ("b", 1, 2), ("a", 1, 2)):
        for k in range(count):
            for ring_x in range(1, rings + 1):
                for ring_y in range(1, rings + 1):
                    if name in "up" and k == 2 and ring_x == ring_y == rings:
                        continue
                    entries.append((name, k, ring_x, ring_y, "hi"))
    return entries


UNITS = halo_units()
ROWS = [unit for unit in UNITS if unit[0] != "u" or unit[2] < 3]
CORNERS = corner_entries()
FACE_BLOCKS = len(ROWS)
SIDE_BLOCKS = (len(UNITS) + 1) // 2
CORNER_BLOCKS = (len(CORNERS) + 2 + 15) // 16


def position():
    i, j, s = (lax.axis_index(axis) for axis in AXES)
    return (i + 1) % 2, (j + 1) % 2, i, j, s


def split(value):
    top = value.astype(BF16).astype(F32)
    return top, value - top


def rigid_units(ring1, ring2, drive):
    lane = lax.broadcasted_iota(jnp.int32, ring1.shape, 1)
    half = ring1.shape[1] // 2
    top, rest = split(ring1)
    turned = pltpu.roll(rest, half, 1)
    first = jnp.where(lane < SOLID, turned, top)
    second = jnp.where(
        lane < 2, pltpu.roll(turned, half + 2, 1), pltpu.roll(turned, 4, 1)
    )
    strength = jnp.sum(drive, axis=1, keepdims=True)
    where = jnp.sum(jnp.where(drive != 0.0, lane.astype(F32), 0.0), axis=1, keepdims=True)
    hi, lo = split(strength)
    extra = jnp.where(lane == 4, hi, jnp.where(lane == 5, lo, where))
    second = jnp.where(lane < 4, second, jnp.where(lane < 7, extra, 0.0))
    return first, jnp.where(lane < SOLID, second, ring2)


def rigid_rows(first, second):
    lane = lax.broadcasted_iota(jnp.int32, first.shape, 1)
    size = first.shape[1]
    half = size // 2
    rest = jnp.where(lane < half, pltpu.roll(second, half - 4, 1), pltpu.roll(first, half, 1))
    rest = jnp.where(lane < size - 2, rest, pltpu.roll(second, size - 2, 1))
    ring1 = jnp.where(lane >= SOLID, first + rest, 0.0)
    ring2 = jnp.where(lane >= SOLID, second, 0.0)
    strength = second[:, 4:5] + second[:, 5:6]
    return ring1, ring2, jnp.where(lane.astype(F32) == second[:, 6:7], strength, 0.0)


def corner_blocks(units, high, more=None, behind=()):
    at = {unit: value for unit, value in zip(UNITS, units)}
    nx = units[0].shape[0]
    rows = []
    for entry in CORNERS:
        name, k, ring_x, ring_y, part = entry
        unit = at[name, k, ring_y, part]
        row = jnp.where(high, unit[nx - ring_x : nx - ring_x + 1], unit[ring_x - 1 : ring_x])
        if more and entry[:4] in more:
            row = row + more[entry[:4]]
        rows.append(row)
    rows += behind
    rows += [jnp.zeros_like(rows[0])] * (-len(rows) % 16)
    return [
        jnp.concatenate(rows[n : n + 16], axis=0).astype(BF16) for n in range(0, len(rows), 16)
    ]


def side_units(ref, nx):
    blocks = [ref[n].astype(F32) for n in range(SIDE_BLOCKS)]
    return [blocks[n // 2][nx * (n % 2) : nx * (n % 2) + nx] for n in range(len(UNITS))]


def edge_units(u_ref, f_ref, p_ref, c_ref, s_ref, high, ready=lambda name: None):
    nx, ny = c_ref.shape[1:3]

    def column(value, ring):
        return jnp.where(high, value[:, ny - ring, :], value[:, ring - 1, :])

    rigid = rigid_units(column(c_ref[0], 1), column(c_ref[0], 2), column(s_ref[0], 1))
    made = {}
    for wanted in "abfup":
        ready(wanted)
        for unit in UNITS:
            name, k, ring, part = unit
            if name != wanted:
                continue
            if name == "a":
                made[unit] = rigid[ring - 1]
                continue
            if name == "f":
                value = f_ref[0, k // 3, k % 3].astype(F32)
            else:
                value = u_ref[0, k] if name == "u" else p_ref[k] if name == "p" else c_ref[1]
            value = column(value, ring)
            made[unit] = split(value)[1] if part == "lo" else value
    return [made[unit] for unit in UNITS]


def unit_blocks(units):
    units = units + [jnp.zeros_like(units[0])] * (len(units) % 2)
    return [
        jnp.concatenate(units[n : n + 2], axis=0).astype(BF16) for n in range(0, len(units), 2)
    ]


def pack_kernel(
    u_in,
    v_in,
    f_in,
    lame_in,
    shear_in,
    buoy_in,
    depth_in,
    cols_in,
    amps_in,
    u_ref,
    f_ref,
    p_ref,
    c_ref,
    s_ref,
    y0_ref,
    v_ref,
    lame_ref,
    shear_ref,
    buoy_ref,
    depth_ref,
    cols_ref,
    amps_ref,
    sems,
):
    copies = [
        pltpu.make_async_copy(src, dst, sems.at[n])
        for n, (src, dst) in enumerate(
            (
                (depth_in, depth_ref),
                (cols_in, cols_ref),
                (amps_in, amps_ref),
                (buoy_in, buoy_ref),
                (shear_in, shear_ref),
                (lame_in, lame_ref),
                (f_in, f_ref),
                (u_in, u_ref),
                (v_in, v_ref),
            )
        )
    ]
    for copy in copies:
        copy.start()
    for copy in copies[:6]:
        copy.wait()
    nx, ny, nz = lame_ref.shape
    _, even_j, i, j, _ = position()
    total_y = ny * lax.axis_size("ty")
    base = i * nx * total_y + j * ny
    levels = lax.broadcasted_iota(jnp.int32, (ny, nz), 1).astype(F32)
    eye = lax.broadcasted_iota(jnp.int32, (ny, ny), 0) == lax.broadcasted_iota(
        jnp.int32, (ny, ny), 1
    )
    own_y = lax.broadcasted_iota(jnp.int32, (ny, cols_ref.shape[1]), 0)
    depth_all = depth_ref[...].astype(F32)
    for x in range(nx):
        depth = jnp.sum(jnp.where(eye, depth_all[x : x + 1, :], 0.0), axis=1, keepdims=True)
        buoy = STEP_SQUARED * buoy_ref[x]
        mu = jnp.where(levels >= depth, shear_ref[x], 0.0)
        c_ref[0, x] = buoy * mu
        c_ref[1, x] = buoy * (lame_ref[x] + mu)
        here = cols_ref[...] == own_y + (base + x * total_y)
        floor = levels == depth
        drive = []
        for t in range(STEPS):
            amp = jnp.sum(jnp.where(here, amps_ref[t], 0.0), axis=1, keepdims=True)
            drive.append(jnp.where(floor, buoy * amp, 0.0))
        s_ref[0, x] = drive[1]
        s_ref[1, x] = drive[2]
        p_ref[2, x] = drive[0]

    def ready(name):
        if name == "f":
            copies[6].wait()
        elif name == "u":
            copies[7].wait()
        elif name == "p":
            copies[8].wait()
            for x in range(nx):
                for k in range(3):
                    p = 2.0 * u_ref[0, k, x] - v_ref[0, k, x]
                    p_ref[k, x] = p + p_ref[k, x] if k == 2 else p

    units = edge_units(u_ref, f_ref, p_ref, c_ref, s_ref, even_j == 1, ready)
    for n, block in enumerate(unit_blocks(units)):
        y0_ref[n] = block


def folded(u_ref, p_ref, c_ref, x2, x3, quarter):
    u = [u_ref[0, k, x3] for k in range(3)]
    row = lax.broadcasted_iota(jnp.int32, u[0].shape, 0)
    ny = u[0].shape[0]

    def slope_y(value):
        up, down = beside_y(value)
        return jnp.where(row == ny - 1, 0.0, up) - jnp.where(row == 0, 0.0, down)

    def slope_z(value):
        up, down = beside_z(value)
        return up - down

    rigid, bulk = c_ref[0, x2], c_ref[1, x2]
    grad_div = (
        u[0] + quarter * (slope_y(u[1]) + slope_z(u[2])),
        quarter * slope_y(u[0]),
        quarter * slope_z(u[0]),
    )
    return [p_ref[k, x2] + rigid * u[k] + bulk * grad_div[k] for k in range(3)]


def face_kernel(
    u_ref, f_ref, p_ref, c_ref, s_ref, x0_ref, x1_ref, y1_ref, c0_ref, c1_ref, wide_ref, fz_ref
):
    nx = c_ref.shape[1]
    even_i, even_j = position()[:2]
    units = edge_units(u_ref, f_ref, p_ref, c_ref, s_ref, even_j == 0)
    for n, block in enumerate(unit_blocks(units)):
        y1_ref[n] = block
    for ref, high in ((c0_ref, even_i == 1), (c1_ref, even_i == 0)):
        for n, block in enumerate(corner_blocks(units, high)):
            ref[n] = block
    for dst, high in ((x0_ref, even_i == 1), (x1_ref, even_i == 0)):
        at = [jnp.where(high, nx - ring, ring - 1) for ring in (1, 2, 3)]
        rigid = rigid_units(c_ref[0, at[0]], c_ref[0, at[1]], s_ref[0, at[0]])
        fresh = folded(u_ref, p_ref, c_ref, at[1], at[2], jnp.where(high, -0.25, 0.25))
        for n, (name, k, ring, part) in enumerate(ROWS):
            x = at[ring - 1]
            if name == "f":
                dst[n] = f_ref[0, k // 3, k % 3, x]
            elif name == "a":
                dst[n] = rigid[ring - 1].astype(BF16)
            else:
                if name == "p" and ring == 2:
                    value = fresh[k]
                else:
                    value = u_ref[0, k, x] if name == "u" else p_ref[k, x] if name == "p" else c_ref[1, x]
                dst[n] = (split(value)[1] if part == "lo" else value).astype(BF16)
    stage_forward(f_ref, wide_ref, fz_ref)


def stage_forward(f_in, f_ref, fz_ref):
    nx, ny, nz = fz_ref.shape[1:]
    wide = f_ref.shape[2]
    for k in range(3 * STEPS):
        for x in range(nx):
            value = f_in[0, k // 3, k % 3, x].astype(F32)
            f_ref[k, x + 1, :ny, :] = value
            f_ref[k, x + 1, ny:, :] = jnp.zeros((wide - ny, nz), F32)
            up, down = beside_z(value)
            fz_ref[k, x] = up - down
        for x in (0, nx + 1):
            f_ref[k, x] = jnp.zeros(f_ref.shape[2:], F32)


def corner_kernel(y0_ref, u_ref, x0_in, x1_in, x0_ref, x1_ref):
    del x0_in, x1_in
    even_i, even_j = position()[:2]
    nx, ny = u_ref.shape[2:4]
    units = side_units(y0_ref, nx)
    bulk = units[UNITS.index(("b", 0, 1, "hi"))]
    for dst, high in ((x0_ref, even_i == 1), (x1_ref, even_i == 0)):
        x3 = jnp.where(high, nx - 3, 2)
        top = [u_ref[0, k, x3, ny - 1 :] for k in range(2)]
        low = [u_ref[0, k, x3, :1] for k in range(2)]
        near = [jnp.where(even_j == 1, a, b) for a, b in zip(top, low)]
        far = [jnp.where(even_j == 1, b, a) for a, b in zip(top, low)]
        weight = jnp.where(high, bulk[nx - 2 : nx - 1], bulk[1:2])
        weight = weight * jnp.where(high == (even_j == 1), 0.25, -0.25)
        more = {("p", 0, 2, 1): weight * near[1], ("p", 1, 2, 1): weight * near[0]}
        for n, block in enumerate(corner_blocks(units, high, more, far)):
            dst[FACE_BLOCKS + n] = block


def beside_z(value):
    tiles = [value[:, n : n + 128] for n in range(0, value.shape[1], 128)]
    lane = lax.broadcasted_iota(jnp.int32, tiles[0].shape, 1)
    zero = jnp.zeros_like(tiles[0])
    ups = [pltpu.roll(tile, 127, 1) for tile in tiles] + [zero]
    downs = [zero] + [pltpu.roll(tile, 1, 1) for tile in tiles]
    up = [jnp.where(lane == 127, ups[n + 1], ups[n]) for n in range(len(tiles))]
    down = [jnp.where(lane == 0, downs[n], downs[n + 1]) for n in range(len(tiles))]
    return jnp.concatenate(up, axis=1), jnp.concatenate(down, axis=1)


def beside_y(value):
    return pltpu.roll(value, value.shape[0] - 1, 0), pltpu.roll(value, 1, 0)


class Row:
    def __init__(self, x, cur, zd):
        self.x = x
        self.um, self.uc, self.up = ([cur[k, x + d] for k in range(3)] for d in (-1, 0, 1))
        self.ys = [beside_y(self.uc[k]) for k in range(3)]
        self.zd = zd
        self.dx = [self.up[k] - self.um[k] for k in range(3)]

    def slopes(self, rows):
        return [
            (self.dx[k][:rows], (self.ys[k][0] - self.ys[k][1])[:rows], self.zd[k, self.x, :rows])
            for k in range(3)
        ]


def advance_row(t, row, before, p_ref, c_ref, s_ref, zs, rows):
    x, um, uc, up, dx, ys, zd = row.x, row.um, row.uc, row.up, row.dx, row.ys, row.zd
    dz1 = zd[1, x]
    tilt = [beside_y(value) for value in (dx[1], dx[0] + zd[2, x], dz1)]
    cross = (
        (tilt[0][0] - tilt[0][1]) + (zd[2, x + 1] - zd[2, x - 1]),
        tilt[1][0] - tilt[1][1],
        (tilt[2][0] - tilt[2][1]) + (zd[0, x + 1] - zd[0, x - 1]),
    )
    rigid, bulk = c_ref[0, x, :rows], c_ref[1, x, :rows]
    fresh = []
    for k in range(3):
        pairs = (um[k] + up[k], ys[k][0] + ys[k][1], zs[k, x])
        laplace = pairs[0] + pairs[1] + pairs[2] - 6.0 * uc[k]
        grad_div = pairs[k] - 2.0 * uc[k] + 0.25 * cross[k]
        if t == 0:
            carry = p_ref[k, x, :rows]
        else:
            carry = 2.0 * uc[k][:rows] - before[k, x, :rows]
            if k == 2:
                carry = carry + s_ref[t - 1, x, :rows]
        fresh.append(carry + rigid * laplace[:rows] + bulk * grad_div[:rows])
    return fresh


def imprint_row(t, row, c_ref, f_ref, fz_ref, rows):
    x = row.x
    ga = row.slopes(rows)
    gf = []
    for k in range(3):
        n, r = 3 * t + k, x - RING + 1
        yp, ym = beside_y(f_ref[n, r])
        gf.append(
            (
                f_ref[n, r + 1, :rows] - f_ref[n, r - 1, :rows],
                (yp - ym)[:rows],
                fz_ref[n, x - RING],
            )
        )
    div = (ga[0][0] + ga[1][1] + ga[2][2]) * (gf[0][0] + gf[1][1] + gf[2][2])
    both = ga[0][0] * gf[0][0]
    for k in range(3):
        for d in range(3):
            if k + d > 0:
                both = both + ga[k][d] * gf[k][d]
    return div, jnp.where(c_ref[0, x, :rows] > 0.0, both, 0.0)


def joined(get, units):
    n = 0
    while n < len(units):
        name, k, ring, _ = units[n]
        if name == "a":
            for entry in zip("ccs", (0, 0, 0), (1, 2, 1), rigid_rows(get(n), get(n + 1))):
                yield entry
            n += 2
            continue
        value = get(n)
        if name in "up" and ring == 1:
            value = value + get(n + 1)
            n += 1
        n += 1
        yield ("c", 1, ring, value) if name == "b" else (name, k, ring, value)


def joined_corner(get):
    n = 0
    while n < len(CORNERS):
        name, k, ring_x, ring_y, _ = CORNERS[n]
        if name == "a":
            for x in (1, 2):
                ring1, ring2, drive = rigid_rows(get(n), get(n + 1))
                yield "c", 0, x, 1, ring1
                yield "c", 0, x, 2, ring2
                if x == 1:
                    yield "s", 0, 1, 1, drive
                n += 2
            continue
        yield ("c", 1, ring_x, ring_y, get(n)) if name == "b" else (name, k, ring_x, ring_y, get(n))
        n += 1


def keep_z(k, x, value, zd, zs, rows=slice(None)):
    up, down = beside_z(value)
    zd[k, x, rows] = up - down
    zs[k, x, rows] = up + down


def middle_rows(nx):
    spans = [range(RING + 1 + t, RING + nx - 1 - t) for t in range(STEPS)]
    return [(span if t < STEPS - 1 else (), span) for t, span in enumerate(spans)]


def side_rows():
    steps = []
    for t in range(STEPS):
        outer = range(t + 1, RING + 1 + t) if t < STEPS - 1 else ()
        steps.append((outer, range(RING, RING + 1 + t)))
    return steps


def run_steps(refs, fz_ref, sum_ref, sums, rows, at):
    nx, ny, nz = fz_ref.shape[1:]
    fields, c_ref = refs["fields"], refs["c"]
    wide_y = c_ref.shape[2]
    for t, (outer, inner) in enumerate(rows):
        cur, zd, zs = fields[t]
        for m in sorted({*outer, *inner}):
            row = Row(at(m), cur, zd)
            x = row.x
            if m in outer:
                nxt, nd, ns = fields[t + 1]
                fresh = advance_row(
                    t, row, fields[t - 1][0], refs["p"], c_ref, refs["s"], zs, wide_y
                )
                for k in range(3):
                    nxt[k, x] = fresh[k]
                    keep_z(k, x, fresh[k], nd, ns)
            if m not in inner:
                continue
            terms = imprint_row(t, row, c_ref, refs["f"], fz_ref, ny)
            for n in range(2):
                value = terms[n]
                own = x - RING
                if t > 0:
                    value = value + sum_ref[n, own]
                if t < STEPS - 1:
                    sum_ref[n, own] = value
                elif len(sums) == 1:
                    sums[0][n, own] = value
                else:
                    half = nz // 2
                    first = position()[4] == 0
                    sums[0][n, own] = jnp.where(first, value[:, :half], value[:, half:])
                    sums[1][n, own] = jnp.where(first, value[:, half:], value[:, :half])


def lay_out(theirs, message):
    top = jnp.zeros((1, 1), F32)
    for n in range(2):
        for row in range(theirs.shape[1]):
            top = jnp.maximum(top, jnp.max(jnp.abs(theirs[n, row]), axis=(0, 1), keepdims=True))
    power = jnp.floor(jnp.log(jnp.maximum(top, 1e-30)) * (1.0 / math.log(2.0)))
    scale = jnp.exp((TARGET - power) * math.log(2.0))
    for n in range(2):
        for row in range(theirs.shape[1]):
            message[n, row] = theirs[n, row] * scale
    message[0, theirs.shape[1]] = jnp.broadcast_to(power, theirs.shape[2:])
    message[1, theirs.shape[1]] = jnp.broadcast_to(power, theirs.shape[2:])


def run_side(refs, fz_ref, sum_ref, sums, high):
    nx = fz_ref.shape[1]
    wide = nx + 2 * RING
    field, zd, zs = refs["fields"][0]
    for row in range(RING):
        x = jnp.where(high, wide - 1 - row, row)
        for k in range(3):
            keep_z(k, x, field[k, x], zd, zs)
    at = lambda row: jnp.where(high, wide - 1 - row, row)
    run_steps(refs, fz_ref, sum_ref, sums, side_rows(), at)


def named(held):
    u, p, c, s, f, ud, us, v, w, vd, vs, wd, ws, under_way, *sums = held
    refs = {"u": u, "p": p, "c": c, "s": s, "f": f}
    refs["fields"] = ((u, ud, us), (v, vd, vs), (w, wd, ws))
    return refs, under_way, sums


def beyond(axis, even, index):
    other = jnp.where(even == 1, index - 1, index + 1)
    return (other >= 0) & (other < lax.axis_size(axis))


def stage_kernel(u_in, p_in, c_in, s_in, u_ref, p_ref, c_ref, s_ref, ud_ref, us_ref):
    nx, ny, nz = c_in.shape[1:]
    wide = u_ref.shape[2]
    for src, ref in ((u_in, u_ref), (p_in, p_ref), (c_in, c_ref), (s_in, s_ref)):
        lead = (0,) if src is u_in else ()
        for k in range(ref.shape[0]):
            for x in range(ref.shape[1]):
                if RING <= x < RING + nx:
                    value = src[lead + (k, x - RING)]
                    ref[k, x, :ny, :] = value
                    ref[k, x, ny:, :] = jnp.zeros((wide - ny, nz), F32)
                    if src is u_in:
                        keep_z(k, x, value, ud_ref, us_ref, slice(0, ny))
                else:
                    ref[k, x] = jnp.zeros(ref.shape[2:], F32)


def early_kernel(fz_ref, y0_in, y1_in, *rest):
    refs, under_way, sums = named(rest[7:])
    u_ref, ud_ref, us_ref = refs["fields"][0]
    nx, ny, nz = fz_ref.shape[1:]
    wide = u_ref.shape[2]
    even_i, even_j, i, j, _ = position()
    ok_y1 = beyond("ty", even_j, j)

    near = side_units(y0_in, nx)
    far = [jnp.where(ok_y1, value, 0.0) for value in side_units(y1_in, nx)]
    top = [jnp.where(even_j == 1, a, b) for a, b in zip(near, far)]
    low = [jnp.where(even_j == 1, b, a) for a, b in zip(near, far)]
    for values, high in ((top, True), (low, False)):
        for name, k, ring, value in joined(lambda n: values[n], UNITS):
            y = ny - 1 + ring if high else wide - ring
            first = 1 if name == "f" else RING
            for x in range(nx):
                refs[name][k, first + x, y : y + 1, :] = value[x : x + 1]
    for x in range(RING, RING + nx):
        for k in range(3):
            keep_z(k, x, u_ref[k, x, ny:], ud_ref, us_ref, slice(ny, wide))
    run_steps(refs, fz_ref, under_way, sums, middle_rows(nx), lambda row: row)

    @pl.when(jnp.logical_not(beyond("tx", even_i, i)))
    def _():
        run_side(refs, fz_ref, under_way, sums, even_i == 0)


def side_kernel(second, fz_ref, faces, corners, *rest):
    if second:
        *rest, message = rest
    refs, under_way, sums = named(rest[len(rest) // 2 :])
    nx, ny, nz = fz_ref.shape[1:]
    wide = refs["u"].shape[2]
    even_i, even_j, i, j, _ = position()
    high = even_i == (0 if second else 1)

    def run():
        for name, k, ring, value in joined(lambda n: faces[n].astype(F32), ROWS):
            first = 1 if name == "f" else RING
            x = jnp.where(high, first + nx - 1 + ring, first - ring)
            refs[name][k, x, :ny, :] = value
        near = [faces[FACE_BLOCKS + n].astype(F32) for n in range(CORNER_BLOCKS)]
        ok_y1 = beyond("ty", even_j, j)
        far = [jnp.where(ok_y1, corners[n].astype(F32), 0.0) for n in range(CORNER_BLOCKS)]
        for y_high in (True, False):
            flag = even_j == (1 if y_high else 0)
            values = [jnp.where(flag, a, b) for a, b in zip(near, far)]
            row = lambda n: values[n // 16][n % 16 : n % 16 + 1]
            for name, k, ring_x, ring_y, value in joined_corner(row):
                x = jnp.where(high, RING + nx - 1 + ring_x, RING - ring_x)
                y = ny - 1 + ring_y if y_high else wide - ring_y
                refs[name][k, x, y : y + 1, :] = value
        place = len(CORNERS)
        u3 = [near[(place + k) // 16][(place + k) % 16 : (place + k) % 16 + 1] for k in range(2)]
        x = jnp.where(high, RING + nx + 1, RING - 2)
        for y_high in (True, False):
            y = ny if y_high else wide - 1
            quarter = jnp.where(high == y_high, -0.25, 0.25)
            quarter = jnp.where(even_j == (0 if y_high else 1), quarter, 0.0)
            weight = refs["c"][1, x, y : y + 1, :] * quarter
            for k in range(2):
                refs["p"][k, x, y : y + 1, :] += weight * u3[1 - k]
        run_side(refs, fz_ref, under_way, sums, high)

    if second:
        pl.when(beyond("tx", even_i, i))(run)
    else:
        run()
    if second:
        lay_out(sums[-1], message)


def total_kernel(scale, own_ref, sent_ref, out_ref, stage, sems):
    nx = own_ref.shape[1]
    back = jnp.exp((sent_ref[0, nx] - TARGET) * math.log(2.0))
    copies = []
    for n in range(2):
        for x in range(nx):
            stage[n, x] = (own_ref[n, x] + sent_ref[n, x] * back) * scale
        copies.append(pltpu.make_async_copy(stage.at[n], out_ref.at[n], sems.at[n]))
        copies[n].start()
    for copy in copies:
        copy.wait()


def last_kernel(w_ref, wd_ref, ws_ref, v_ref, c_ref, s_ref, out_ref):
    nx, ny = out_ref.shape[2:4]

    @pl.loop(RING, RING + nx, unroll=UNROLL)
    def _(x):
        fresh = advance_row(
            STEPS - 1, Row(x, w_ref, wd_ref), v_ref, None, c_ref, s_ref, ws_ref, ny
        )
        for k in range(3):
            out_ref[0, k, x - RING] = fresh[k]


def swap_map(sizes, partner):
    nx, ny, ns = sizes

    def meets(i, j):
        a, b = partner(i, j)
        return 0 <= a < nx and 0 <= b < ny

    pairs = []
    for i in range(nx):
        for j in range(ny):
            for s in range(ns):
                if meets(i, j):
                    to = (*partner(i, j), s)
                elif not meets(i, j ^ 1):
                    to = (i, j ^ 1, s)
                else:
                    to = (i, j, s ^ 1 if s ^ 1 < ns else s)
                pairs.append(((i * ny + j) * ns + s, (to[0] * ny + to[1]) * ns + to[2]))
    return pairs


def body(
    adj_now,
    adj_later,
    forward_field,
    lame_first,
    shear,
    buoyancy,
    seafloor_depth,
    station_columns,
    station_traces,
):
    nx, ny, nz = lame_first.shape
    sizes = tuple(lax.axis_size(axis) for axis in AXES)
    count_s = sizes[2]
    vmem = pl.BlockSpec(memory_space=pltpu.VMEM)
    anywhere = pl.BlockSpec(memory_space=pl.ANY)
    limit = 30 * 1024 * 1024
    params = pltpu.CompilerParams(vmem_limit_bytes=limit)
    face = jax.ShapeDtypeStruct((FACE_BLOCKS + CORNER_BLOCKS, ny, nz), BF16)
    edge = jax.ShapeDtypeStruct((SIDE_BLOCKS, 2 * nx, nz), BF16)
    corner = jax.ShapeDtypeStruct((CORNER_BLOCKS + 1, 16, nz), BF16)
    grid = lambda n: jax.ShapeDtypeStruct((n, nx, ny, nz), F32)

    like = lambda value: jax.ShapeDtypeStruct(value.shape, value.dtype)
    traces = jnp.transpose(station_traces, (1, 0, 2))
    held = (adj_later, lame_first, shear, buoyancy, seafloor_depth, station_columns, traces)
    u0, fwd, carry, coeff, drive, y0 = pl.pallas_call(
        pack_kernel,
        out_shape=(
            like(adj_now),
            like(forward_field),
            grid(3),
            grid(2),
            grid(2),
            edge,
        ),
        in_specs=[anywhere] * 9,
        out_specs=(vmem,) * 6,
        scratch_shapes=[pltpu.VMEM(value.shape, value.dtype) for value in held]
        + [pltpu.SemaphoreType.DMA((9,))],
        compiler_params=params,
        name="pack",
    )(
        *(
            pltpu.with_memory_space_constraint(value, pltpu.HBM)
            for value in (adj_now, adj_later, forward_field, *held[1:])
        )
    )

    def exchange(value, partner):
        return lax.ppermute(value, AXES, swap_map(sizes, partner))

    flip = lambda n: n + 1 if n % 2 == 0 else n - 1
    back = lambda n: n - 1 if n % 2 == 0 else n + 1
    y0 = exchange(y0, lambda a, b: (a, flip(b)))
    wide_x, wide_y = nx + 2 * RING, ny + PAD
    padded = lambda n, x=wide_x: jax.ShapeDtypeStruct((n, x, wide_y, nz), F32)
    x0, x1, y1, c0, c1, fwd, fwd_z = pl.pallas_call(
        face_kernel,
        out_shape=(
            face,
            face,
            edge,
            corner,
            corner,
            padded(3 * STEPS, nx + 2),
            grid(3 * STEPS),
        ),
        in_specs=[vmem] * 5,
        out_specs=(vmem,) * 7,
        compiler_params=params,
        name="faces",
    )(u0, fwd, carry, coeff, drive)
    x0, x1 = pl.pallas_call(
        corner_kernel,
        out_shape=(face, face),
        in_specs=[vmem] * 4,
        out_specs=(vmem,) * 2,
        input_output_aliases={2: 0, 3: 1},
        compiler_params=params,
        name="corners",
    )(y0, u0, x0, x1)
    x0 = exchange(x0, lambda a, b: (flip(a), b))
    x1 = exchange(x1, lambda a, b: (back(a), b))
    y1 = exchange(y1, lambda a, b: (a, back(b)))
    c0 = exchange(c0, lambda a, b: (flip(a), back(b)))
    c1 = exchange(c1, lambda a, b: (back(a), back(b)))

    tile = (padded(3), padded(3), padded(2), padded(2))
    split_up = count_s == 2
    depth = nz // 2 if split_up else nz
    sums = (jax.ShapeDtypeStruct((2, nx, ny, depth), F32),) * (1 + split_up)
    held = pl.pallas_call(
        stage_kernel,
        out_shape=(*tile, padded(3), padded(3)),
        in_specs=[vmem] * 4,
        out_specs=(vmem,) * 6,
        compiler_params=params,
        name="stage",
    )(u0, carry, coeff, drive)
    held = (*held[:4], fwd, *held[4:])
    staged = (*tile, like(fwd), padded(3), padded(3))
    shapes = (*staged, *(padded(3),) * 6, grid(2), *sums)
    held = pl.pallas_call(
        early_kernel,
        out_shape=shapes,
        in_specs=[vmem] * 10,
        out_specs=(vmem,) * len(shapes),
        input_output_aliases={3 + n: n for n in range(7)},
        compiler_params=params,
        name="early",
    )(fwd_z, y0, y1, *held)

    def side(second, faces, corners, held):
        message = (jax.ShapeDtypeStruct((2, nx + 1, ny, depth), F32),) * second
        return pl.pallas_call(
            functools.partial(side_kernel, second),
            out_shape=(*shapes, *message),
            in_specs=[vmem] * (3 + len(shapes)),
            out_specs=(vmem,) * (len(shapes) + second),
            input_output_aliases={3 + n: n for n in range(len(shapes))},
            compiler_params=params,
            name="second" if second else "first",
        )(fwd_z, faces, corners, *held)

    held = side(False, x0, c0, held)
    *held, message = side(True, x1, c1, held)
    coeff, drive = held[2:4]
    u1, u2 = held[7:9]
    u2_d, u2_s = held[11:13]

    sums = held[14:]
    scale = 0.25 / (adj_now.shape[0] * count_s)
    if split_up:
        sent = lax.ppermute(message.astype(jnp.float16), "src", [(0, 1), (1, 0)])
        summed = pl.pallas_call(
            functools.partial(total_kernel, scale),
            out_shape=like(sums[0]),
            in_specs=[vmem] * 2,
            out_specs=anywhere,
            scratch_shapes=[
                pltpu.VMEM(sums[0].shape, F32),
                pltpu.SemaphoreType.DMA((2,)),
            ],
            compiler_params=params,
            name="total",
        )(sums[0], sent.astype(F32))
    else:
        summed = lax.psum_scatter(sums[0] * scale, "src", scatter_dimension=3, tiled=True)
    final = pl.pallas_call(
        last_kernel,
        out_shape=like(adj_now),
        in_specs=[vmem] * 6,
        out_specs=vmem,
        compiler_params=params,
        name="last",
    )(u2, u2_d, u2_s, u1, coeff, drive)
    return final, summed


def solution(mesh):
    in_specs = (
        P("src", None, "tx", "ty", None),
        P("src", None, "tx", "ty", None),
        P("src", None, None, "tx", "ty", None),
        P("tx", "ty", None),
        P("tx", "ty", None),
        P("tx", "ty", None),
        P("tx", "ty"),
        P("src", None),
        P("src", None, None),
    )
    out_specs = (P("src", None, "tx", "ty", None), P(None, "tx", "ty", "src"))
    return jax.shard_map(body, mesh=mesh, in_specs=in_specs, out_specs=out_specs, check_vma=False)
```

```python
import functools
import math

import jax
import jax.numpy as jnp
from jax import lax
from jax.experimental import pallas as pl
from jax.experimental.pallas import tpu as pltpu
from jax.sharding import PartitionSpec as P

STEPS = 3
STEP_SQUARED = 0.04
RING = 3
SOLID = 126
PAD = 8
AXES = ("tx", "ty", "src")
F32 = jnp.float32
BF16 = jnp.bfloat16
UNROLL = 8
TARGET = 13.0


def halo_units():
    units = []
    for name, count, rings in (("u", 3, 3), ("p", 3, 2), ("b", 1, 2)):
        for k in range(count):
            for ring in range(1, rings + 1):
                units.append((name, k, ring, "hi"))
                if ring == 1 and name != "b":
                    units.append((name, k, ring, "lo"))
    units += [("a", 0, 1, "hi"), ("a", 0, 2, "hi")]
    for k in range(3 * STEPS):
        units.append(("f", k, 1, "hi"))
    return units


def corner_entries():
    entries = []
    for name, count, rings in (("u", 3, 3), ("p", 3, 2), ("b", 1, 2), ("a", 1, 2)):
        for k in range(count):
            for ring_x in range(1, rings + 1):
                for ring_y in range(1, rings + 1):
                    if name in "up" and k == 2 and ring_x == ring_y == rings:
                        continue
                    entries.append((name, k, ring_x, ring_y, "hi"))
    return entries


UNITS = halo_units()
ROWS = [unit for unit in UNITS if unit[0] != "u" or unit[2] < 3]
CORNERS = corner_entries()
FACE_BLOCKS = len(ROWS)
SIDE_BLOCKS = (len(UNITS) + 1) // 2
CORNER_BLOCKS = (len(CORNERS) + 2 + 15) // 16


def position():
    i, j, s = (lax.axis_index(axis) for axis in AXES)
    return (i + 1) % 2, (j + 1) % 2, i, j, s


def split(value):
    top = value.astype(BF16).astype(F32)
    return top, value - top


def rigid_units(ring1, ring2, drive):
    lane = lax.broadcasted_iota(jnp.int32, ring1.shape, 1)
    half = ring1.shape[1] // 2
    top, rest = split(ring1)
    turned = pltpu.roll(rest, half, 1)
    first = jnp.where(lane < SOLID, turned, top)
    second = jnp.where(
        lane < 2, pltpu.roll(turned, half + 2, 1), pltpu.roll(turned, 4, 1)
    )
    strength = jnp.sum(drive, axis=1, keepdims=True)
    where = jnp.sum(jnp.where(drive != 0.0, lane.astype(F32), 0.0), axis=1, keepdims=True)
    hi, lo = split(strength)
    extra = jnp.where(lane == 4, hi, jnp.where(lane == 5, lo, where))
    second = jnp.where(lane < 4, second, jnp.where(lane < 7, extra, 0.0))
    return first, jnp.where(lane < SOLID, second, ring2)


def rigid_rows(first, second):
    lane = lax.broadcasted_iota(jnp.int32, first.shape, 1)
    size = first.shape[1]
    half = size // 2
    rest = jnp.where(lane < half, pltpu.roll(second, half - 4, 1), pltpu.roll(first, half, 1))
    rest = jnp.where(lane < size - 2, rest, pltpu.roll(second, size - 2, 1))
    ring1 = jnp.where(lane >= SOLID, first + rest, 0.0)
    ring2 = jnp.where(lane >= SOLID, second, 0.0)
    strength = second[:, 4:5] + second[:, 5:6]
    return ring1, ring2, jnp.where(lane.astype(F32) == second[:, 6:7], strength, 0.0)


def corner_blocks(units, high, more=None, behind=()):
    at = {unit: value for unit, value in zip(UNITS, units)}
    nx = units[0].shape[0]
    rows = []
    for entry in CORNERS:
        name, k, ring_x, ring_y, part = entry
        unit = at[name, k, ring_y, part]
        row = jnp.where(high, unit[nx - ring_x : nx - ring_x + 1], unit[ring_x - 1 : ring_x])
        if more and entry[:4] in more:
            row = row + more[entry[:4]]
        rows.append(row)
    rows += behind
    rows += [jnp.zeros_like(rows[0])] * (-len(rows) % 16)
    return [
        jnp.concatenate(rows[n : n + 16], axis=0).astype(BF16) for n in range(0, len(rows), 16)
    ]


def side_units(ref, nx):
    blocks = [ref[n].astype(F32) for n in range(SIDE_BLOCKS)]
    return [blocks[n // 2][nx * (n % 2) : nx * (n % 2) + nx] for n in range(len(UNITS))]


def edge_units(u_ref, f_ref, p_ref, c_ref, s_ref, high, ready=lambda name: None):
    nx, ny = c_ref.shape[1:3]

    def column(value, ring):
        return jnp.where(high, value[:, ny - ring, :], value[:, ring - 1, :])

    rigid = rigid_units(column(c_ref[0], 1), column(c_ref[0], 2), column(s_ref[0], 1))
    made = {}
    for wanted in "abfup":
        ready(wanted)
        for unit in UNITS:
            name, k, ring, part = unit
            if name != wanted:
                continue
            if name == "a":
                made[unit] = rigid[ring - 1]
                continue
            if name == "f":
                value = f_ref[0, k // 3, k % 3].astype(F32)
            else:
                value = u_ref[0, k] if name == "u" else p_ref[k] if name == "p" else c_ref[1]
            value = column(value, ring)
            made[unit] = split(value)[1] if part == "lo" else value
    return [made[unit] for unit in UNITS]


def unit_blocks(units):
    units = units + [jnp.zeros_like(units[0])] * (len(units) % 2)
    return [
        jnp.concatenate(units[n : n + 2], axis=0).astype(BF16) for n in range(0, len(units), 2)
    ]


def pack_kernel(
    u_in,
    v_in,
    f_in,
    lame_in,
    shear_in,
    buoy_in,
    depth_in,
    cols_in,
    amps_in,
    u_ref,
    f_ref,
    p_ref,
    c_ref,
    s_ref,
    y0_ref,
    v_ref,
    lame_ref,
    shear_ref,
    buoy_ref,
    depth_ref,
    cols_ref,
    amps_ref,
    sems,
):
    copies = [
        pltpu.make_async_copy(src, dst, sems.at[n])
        for n, (src, dst) in enumerate(
            (
                (depth_in, depth_ref),
                (cols_in, cols_ref),
                (amps_in, amps_ref),
                (buoy_in, buoy_ref),
                (shear_in, shear_ref),
                (lame_in, lame_ref),
                (f_in, f_ref),
                (u_in, u_ref),
                (v_in, v_ref),
            )
        )
    ]
    for copy in copies:
        copy.start()
    for copy in copies[:6]:
        copy.wait()
    nx, ny, nz = lame_ref.shape
    _, even_j, i, j, _ = position()
    total_y = ny * lax.axis_size("ty")
    base = i * nx * total_y + j * ny
    levels = lax.broadcasted_iota(jnp.int32, (ny, nz), 1).astype(F32)
    eye = lax.broadcasted_iota(jnp.int32, (ny, ny), 0) == lax.broadcasted_iota(
        jnp.int32, (ny, ny), 1
    )
    own_y = lax.broadcasted_iota(jnp.int32, (ny, cols_ref.shape[1]), 0)
    depth_all = depth_ref[...].astype(F32)
    for x in range(nx):
        depth = jnp.sum(jnp.where(eye, depth_all[x : x + 1, :], 0.0), axis=1, keepdims=True)
        buoy = STEP_SQUARED * buoy_ref[x]
        mu = jnp.where(levels >= depth, shear_ref[x], 0.0)
        c_ref[0, x] = buoy * mu
        c_ref[1, x] = buoy * (lame_ref[x] + mu)
        here = cols_ref[...] == own_y + (base + x * total_y)
        floor = levels == depth
        drive = []
        for t in range(STEPS):
            amp = jnp.sum(jnp.where(here, amps_ref[t], 0.0), axis=1, keepdims=True)
            drive.append(jnp.where(floor, buoy * amp, 0.0))
        s_ref[0, x] = drive[1]
        s_ref[1, x] = drive[2]
        p_ref[2, x] = drive[0]

    def ready(name):
        if name == "f":
            copies[6].wait()
        elif name == "u":
            copies[7].wait()
        elif name == "p":
            copies[8].wait()
            for x in range(nx):
                for k in range(3):
                    p = 2.0 * u_ref[0, k, x] - v_ref[0, k, x]
                    p_ref[k, x] = p + p_ref[k, x] if k == 2 else p

    units = edge_units(u_ref, f_ref, p_ref, c_ref, s_ref, even_j == 1, ready)
    for n, block in enumerate(unit_blocks(units)):
        y0_ref[n] = block


def folded(u_ref, p_ref, c_ref, x2, x3, quarter):
    u = [u_ref[0, k, x3] for k in range(3)]
    row = lax.broadcasted_iota(jnp.int32, u[0].shape, 0)
    ny = u[0].shape[0]

    def slope_y(value):
        up, down = beside_y(value)
        return jnp.where(row == ny - 1, 0.0, up) - jnp.where(row == 0, 0.0, down)

    def slope_z(value):
        up, down = beside_z(value)
        return up - down

    rigid, bulk = c_ref[0, x2], c_ref[1, x2]
    grad_div = (
        u[0] + quarter * (slope_y(u[1]) + slope_z(u[2])),
        quarter * slope_y(u[0]),
        quarter * slope_z(u[0]),
    )
    return [p_ref[k, x2] + rigid * u[k] + bulk * grad_div[k] for k in range(3)]


def face_kernel(
    u_ref, f_ref, p_ref, c_ref, s_ref, x0_ref, x1_ref, y1_ref, c0_ref, c1_ref, wide_ref, fz_ref
):
    nx = c_ref.shape[1]
    even_i, even_j = position()[:2]
    units = edge_units(u_ref, f_ref, p_ref, c_ref, s_ref, even_j == 0)
    for n, block in enumerate(unit_blocks(units)):
        y1_ref[n] = block
    for ref, high in ((c0_ref, even_i == 1), (c1_ref, even_i == 0)):
        for n, block in enumerate(corner_blocks(units, high)):
            ref[n] = block
    for dst, high in ((x0_ref, even_i == 1), (x1_ref, even_i == 0)):
        at = [jnp.where(high, nx - ring, ring - 1) for ring in (1, 2, 3)]
        rigid = rigid_units(c_ref[0, at[0]], c_ref[0, at[1]], s_ref[0, at[0]])
        fresh = folded(u_ref, p_ref, c_ref, at[1], at[2], jnp.where(high, -0.25, 0.25))
        for n, (name, k, ring, part) in enumerate(ROWS):
            x = at[ring - 1]
            if name == "f":
                dst[n] = f_ref[0, k // 3, k % 3, x]
            elif name == "a":
                dst[n] = rigid[ring - 1].astype(BF16)
            else:
                if name == "p" and ring == 2:
                    value = fresh[k]
                else:
                    value = u_ref[0, k, x] if name == "u" else p_ref[k, x] if name == "p" else c_ref[1, x]
                dst[n] = (split(value)[1] if part == "lo" else value).astype(BF16)
    stage_forward(f_ref, wide_ref, fz_ref)


def stage_forward(f_in, f_ref, fz_ref):
    nx, ny, nz = fz_ref.shape[1:]
    wide = f_ref.shape[2]
    for k in range(3 * STEPS):
        for x in range(nx):
            value = f_in[0, k // 3, k % 3, x].astype(F32)
            f_ref[k, x + 1, :ny, :] = value
            f_ref[k, x + 1, ny:, :] = jnp.zeros((wide - ny, nz), F32)
            up, down = beside_z(value)
            fz_ref[k, x] = up - down
        for x in (0, nx + 1):
            f_ref[k, x] = jnp.zeros(f_ref.shape[2:], F32)


def corner_kernel(y0_ref, u_ref, x0_in, x1_in, x0_ref, x1_ref):
    del x0_in, x1_in
    even_i, even_j = position()[:2]
    nx, ny = u_ref.shape[2:4]
    units = side_units(y0_ref, nx)
    bulk = units[UNITS.index(("b", 0, 1, "hi"))]
    for dst, high in ((x0_ref, even_i == 1), (x1_ref, even_i == 0)):
        x3 = jnp.where(high, nx - 3, 2)
        top = [u_ref[0, k, x3, ny - 1 :] for k in range(2)]
        low = [u_ref[0, k, x3, :1] for k in range(2)]
        near = [jnp.where(even_j == 1, a, b) for a, b in zip(top, low)]
        far = [jnp.where(even_j == 1, b, a) for a, b in zip(top, low)]
        weight = jnp.where(high, bulk[nx - 2 : nx - 1], bulk[1:2])
        weight = weight * jnp.where(high == (even_j == 1), 0.25, -0.25)
        more = {("p", 0, 2, 1): weight * near[1], ("p", 1, 2, 1): weight * near[0]}
        for n, block in enumerate(corner_blocks(units, high, more, far)):
            dst[FACE_BLOCKS + n] = block


def beside_z(value):
    tiles = [value[:, n : n + 128] for n in range(0, value.shape[1], 128)]
    lane = lax.broadcasted_iota(jnp.int32, tiles[0].shape, 1)
    zero = jnp.zeros_like(tiles[0])
    ups = [pltpu.roll(tile, 127, 1) for tile in tiles] + [zero]
    downs = [zero] + [pltpu.roll(tile, 1, 1) for tile in tiles]
    up = [jnp.where(lane == 127, ups[n + 1], ups[n]) for n in range(len(tiles))]
    down = [jnp.where(lane == 0, downs[n], downs[n + 1]) for n in range(len(tiles))]
    return jnp.concatenate(up, axis=1), jnp.concatenate(down, axis=1)


def beside_y(value):
    return pltpu.roll(value, value.shape[0] - 1, 0), pltpu.roll(value, 1, 0)


class Row:
    def __init__(self, x, cur, zd):
        self.x = x
        self.um, self.uc, self.up = ([cur[k, x + d] for k in range(3)] for d in (-1, 0, 1))
        self.ys = [beside_y(self.uc[k]) for k in range(3)]
        self.zd = zd
        self.dx = [self.up[k] - self.um[k] for k in range(3)]

    def slopes(self, rows):
        return [
            (self.dx[k][:rows], (self.ys[k][0] - self.ys[k][1])[:rows], self.zd[k, self.x, :rows])
            for k in range(3)
        ]


def advance_row(t, row, before, p_ref, c_ref, s_ref, zs, rows):
    x, um, uc, up, dx, ys, zd = row.x, row.um, row.uc, row.up, row.dx, row.ys, row.zd
    dz1 = zd[1, x]
    tilt = [beside_y(value) for value in (dx[1], dx[0] + zd[2, x], dz1)]
    cross = (
        (tilt[0][0] - tilt[0][1]) + (zd[2, x + 1] - zd[2, x - 1]),
        tilt[1][0] - tilt[1][1],
        (tilt[2][0] - tilt[2][1]) + (zd[0, x + 1] - zd[0, x - 1]),
    )
    rigid, bulk = c_ref[0, x, :rows], c_ref[1, x, :rows]
    fresh = []
    for k in range(3):
        pairs = (um[k] + up[k], ys[k][0] + ys[k][1], zs[k, x])
        laplace = pairs[0] + pairs[1] + pairs[2] - 6.0 * uc[k]
        grad_div = pairs[k] - 2.0 * uc[k] + 0.25 * cross[k]
        if t == 0:
            carry = p_ref[k, x, :rows]
        else:
            carry = 2.0 * uc[k][:rows] - before[k, x, :rows]
            if k == 2:
                carry = carry + s_ref[t - 1, x, :rows]
        fresh.append(carry + rigid * laplace[:rows] + bulk * grad_div[:rows])
    return fresh


def imprint_row(t, row, c_ref, f_ref, fz_ref, rows):
    x = row.x
    ga = row.slopes(rows)
    gf = []
    for k in range(3):
        n, r = 3 * t + k, x - RING + 1
        yp, ym = beside_y(f_ref[n, r])
        gf.append(
            (
                f_ref[n, r + 1, :rows] - f_ref[n, r - 1, :rows],
                (yp - ym)[:rows],
                fz_ref[n, x - RING],
            )
        )
    div = (ga[0][0] + ga[1][1] + ga[2][2]) * (gf[0][0] + gf[1][1] + gf[2][2])
    both = ga[0][0] * gf[0][0]
    for k in range(3):
        for d in range(3):
            if k + d > 0:
                both = both + ga[k][d] * gf[k][d]
    return div, jnp.where(c_ref[0, x, :rows] > 0.0, both, 0.0)


def joined(get, units):
    n = 0
    while n < len(units):
        name, k, ring, _ = units[n]
        if name == "a":
            for entry in zip("ccs", (0, 0, 0), (1, 2, 1), rigid_rows(get(n), get(n + 1))):
                yield entry
            n += 2
            continue
        value = get(n)
        if name in "up" and ring == 1:
            value = value + get(n + 1)
            n += 1
        n += 1
        yield ("c", 1, ring, value) if name == "b" else (name, k, ring, value)


def joined_corner(get):
    n = 0
    while n < len(CORNERS):
        name, k, ring_x, ring_y, _ = CORNERS[n]
        if name == "a":
            for x in (1, 2):
                ring1, ring2, drive = rigid_rows(get(n), get(n + 1))
                yield "c", 0, x, 1, ring1
                yield "c", 0, x, 2, ring2
                if x == 1:
                    yield "s", 0, 1, 1, drive
                n += 2
            continue
        yield ("c", 1, ring_x, ring_y, get(n)) if name == "b" else (name, k, ring_x, ring_y, get(n))
        n += 1


def keep_z(k, x, value, zd, zs, rows=slice(None)):
    up, down = beside_z(value)
    zd[k, x, rows] = up - down
    zs[k, x, rows] = up + down


def middle_rows(nx):
    spans = [range(RING + 1 + t, RING + nx - 1 - t) for t in range(STEPS)]
    return [(span if t < STEPS - 1 else (), span) for t, span in enumerate(spans)]


def side_rows():
    steps = []
    for t in range(STEPS):
        outer = range(t + 1, RING + 1 + t) if t < STEPS - 1 else ()
        steps.append((outer, range(RING, RING + 1 + t)))
    return steps


def run_steps(refs, fz_ref, sum_ref, sums, rows, at):
    nx, ny, nz = fz_ref.shape[1:]
    fields, c_ref = refs["fields"], refs["c"]
    wide_y = c_ref.shape[2]
    for t, (outer, inner) in enumerate(rows):
        cur, zd, zs = fields[t]
        for m in sorted({*outer, *inner}):
            row = Row(at(m), cur, zd)
            x = row.x
            if m in outer:
                nxt, nd, ns = fields[t + 1]
                fresh = advance_row(
                    t, row, fields[t - 1][0], refs["p"], c_ref, refs["s"], zs, wide_y
                )
                for k in range(3):
                    nxt[k, x] = fresh[k]
                    keep_z(k, x, fresh[k], nd, ns)
            if m not in inner:
                continue
            terms = imprint_row(t, row, c_ref, refs["f"], fz_ref, ny)
            for n in range(2):
                value = terms[n]
                own = x - RING
                if t > 0:
                    value = value + sum_ref[n, own]
                if t < STEPS - 1:
                    sum_ref[n, own] = value
                elif len(sums) == 1:
                    sums[0][n, own] = value
                else:
                    half = nz // 2
                    first = position()[4] == 0
                    sums[0][n, own] = jnp.where(first, value[:, :half], value[:, half:])
                    sums[1][n, own] = jnp.where(first, value[:, half:], value[:, :half])


def lay_out(theirs, message):
    nx = theirs.shape[1]
    top = jnp.full(theirs.shape[2:], 1e-30, F32)
    for n in range(2):
        for row in range(nx):
            top = jnp.maximum(top, jnp.abs(theirs[n, row]))
    power = jnp.floor(jnp.log(top) * (1.0 / math.log(2.0)))
    scale = jnp.exp((TARGET - power) * math.log(2.0))
    for n in range(2):
        for row in range(nx):
            message[n * nx + row] = theirs[n, row] * scale
    message[2 * nx] = power


def run_side(refs, fz_ref, sum_ref, sums, high):
    nx = fz_ref.shape[1]
    wide = nx + 2 * RING
    field, zd, zs = refs["fields"][0]
    for row in range(RING):
        x = jnp.where(high, wide - 1 - row, row)
        for k in range(3):
            keep_z(k, x, field[k, x], zd, zs)
    at = lambda row: jnp.where(high, wide - 1 - row, row)
    run_steps(refs, fz_ref, sum_ref, sums, side_rows(), at)


def named(held):
    u, p, c, s, f, ud, us, v, w, vd, vs, wd, ws, under_way, *sums = held
    refs = {"u": u, "p": p, "c": c, "s": s, "f": f}
    refs["fields"] = ((u, ud, us), (v, vd, vs), (w, wd, ws))
    return refs, under_way, sums


def beyond(axis, even, index):
    other = jnp.where(even == 1, index - 1, index + 1)
    return (other >= 0) & (other < lax.axis_size(axis))


def stage_kernel(u_in, p_in, c_in, s_in, u_ref, p_ref, c_ref, s_ref, ud_ref, us_ref):
    nx, ny, nz = c_in.shape[1:]
    wide = u_ref.shape[2]
    for src, ref in ((u_in, u_ref), (p_in, p_ref), (c_in, c_ref), (s_in, s_ref)):
        lead = (0,) if src is u_in else ()
        for k in range(ref.shape[0]):
            for x in range(ref.shape[1]):
                if RING <= x < RING + nx:
                    value = src[lead + (k, x - RING)]
                    ref[k, x, :ny, :] = value
                    ref[k, x, ny:, :] = jnp.zeros((wide - ny, nz), F32)
                    if src is u_in:
                        keep_z(k, x, value, ud_ref, us_ref, slice(0, ny))
                else:
                    ref[k, x] = jnp.zeros(ref.shape[2:], F32)


def early_kernel(fz_ref, y0_in, y1_in, *rest):
    refs, under_way, sums = named(rest[7:])
    u_ref, ud_ref, us_ref = refs["fields"][0]
    nx, ny, nz = fz_ref.shape[1:]
    wide = u_ref.shape[2]
    even_i, even_j, i, j, _ = position()
    ok_y1 = beyond("ty", even_j, j)

    near = side_units(y0_in, nx)
    far = [jnp.where(ok_y1, value, 0.0) for value in side_units(y1_in, nx)]
    top = [jnp.where(even_j == 1, a, b) for a, b in zip(near, far)]
    low = [jnp.where(even_j == 1, b, a) for a, b in zip(near, far)]
    for values, high in ((top, True), (low, False)):
        for name, k, ring, value in joined(lambda n: values[n], UNITS):
            y = ny - 1 + ring if high else wide - ring
            first = 1 if name == "f" else RING
            for x in range(nx):
                refs[name][k, first + x, y : y + 1, :] = value[x : x + 1]
    for x in range(RING, RING + nx):
        for k in range(3):
            keep_z(k, x, u_ref[k, x, ny:], ud_ref, us_ref, slice(ny, wide))
    run_steps(refs, fz_ref, under_way, sums, middle_rows(nx), lambda row: row)

    @pl.when(jnp.logical_not(beyond("tx", even_i, i)))
    def _():
        run_side(refs, fz_ref, under_way, sums, even_i == 0)


def side_kernel(second, fz_ref, faces, corners, *rest):
    if second:
        *rest, message = rest
    refs, under_way, sums = named(rest[len(rest) // 2 :])
    nx, ny, nz = fz_ref.shape[1:]
    wide = refs["u"].shape[2]
    even_i, even_j, i, j, _ = position()
    high = even_i == (0 if second else 1)

    def run():
        for name, k, ring, value in joined(lambda n: faces[n].astype(F32), ROWS):
            first = 1 if name == "f" else RING
            x = jnp.where(high, first + nx - 1 + ring, first - ring)
            refs[name][k, x, :ny, :] = value
        near = [faces[FACE_BLOCKS + n].astype(F32) for n in range(CORNER_BLOCKS)]
        ok_y1 = beyond("ty", even_j, j)
        far = [jnp.where(ok_y1, corners[n].astype(F32), 0.0) for n in range(CORNER_BLOCKS)]
        for y_high in (True, False):
            flag = even_j == (1 if y_high else 0)
            values = [jnp.where(flag, a, b) for a, b in zip(near, far)]
            row = lambda n: values[n // 16][n % 16 : n % 16 + 1]
            for name, k, ring_x, ring_y, value in joined_corner(row):
                x = jnp.where(high, RING + nx - 1 + ring_x, RING - ring_x)
                y = ny - 1 + ring_y if y_high else wide - ring_y
                refs[name][k, x, y : y + 1, :] = value
        place = len(CORNERS)
        u3 = [near[(place + k) // 16][(place + k) % 16 : (place + k) % 16 + 1] for k in range(2)]
        x = jnp.where(high, RING + nx + 1, RING - 2)
        for y_high in (True, False):
            y = ny if y_high else wide - 1
            quarter = jnp.where(high == y_high, -0.25, 0.25)
            quarter = jnp.where(even_j == (0 if y_high else 1), quarter, 0.0)
            weight = refs["c"][1, x, y : y + 1, :] * quarter
            for k in range(2):
                refs["p"][k, x, y : y + 1, :] += weight * u3[1 - k]
        run_side(refs, fz_ref, under_way, sums, high)

    if second:
        pl.when(beyond("tx", even_i, i))(run)
    else:
        run()
    if second:
        lay_out(sums[-1], message)


def total_kernel(scale, own_ref, sent_ref, out_ref, stage, sems):
    nx = own_ref.shape[1]
    back = jnp.exp((sent_ref[2 * nx] - TARGET) * math.log(2.0))
    copies = []
    for n in range(2):
        for x in range(nx):
            stage[n, x] = (own_ref[n, x] + sent_ref[n * nx + x] * back) * scale
        copies.append(pltpu.make_async_copy(stage.at[n], out_ref.at[n], sems.at[n]))
        copies[n].start()
    for copy in copies:
        copy.wait()


def last_kernel(w_ref, wd_ref, ws_ref, v_ref, c_ref, s_ref, out_ref):
    nx, ny = out_ref.shape[2:4]

    @pl.loop(RING, RING + nx, unroll=UNROLL)
    def _(x):
        fresh = advance_row(
            STEPS - 1, Row(x, w_ref, wd_ref), v_ref, None, c_ref, s_ref, ws_ref, ny
        )
        for k in range(3):
            out_ref[0, k, x - RING] = fresh[k]


def swap_map(sizes, partner):
    nx, ny, ns = sizes

    def meets(i, j):
        a, b = partner(i, j)
        return 0 <= a < nx and 0 <= b < ny

    pairs = []
    for i in range(nx):
        for j in range(ny):
            for s in range(ns):
                if meets(i, j):
                    to = (*partner(i, j), s)
                elif not meets(i, j ^ 1):
                    to = (i, j ^ 1, s)
                else:
                    to = (i, j, s ^ 1 if s ^ 1 < ns else s)
                pairs.append(((i * ny + j) * ns + s, (to[0] * ny + to[1]) * ns + to[2]))
    return pairs


def body(
    adj_now,
    adj_later,
    forward_field,
    lame_first,
    shear,
    buoyancy,
    seafloor_depth,
    station_columns,
    station_traces,
):
    nx, ny, nz = lame_first.shape
    sizes = tuple(lax.axis_size(axis) for axis in AXES)
    count_s = sizes[2]
    vmem = pl.BlockSpec(memory_space=pltpu.VMEM)
    anywhere = pl.BlockSpec(memory_space=pl.ANY)
    limit = 30 * 1024 * 1024
    params = pltpu.CompilerParams(vmem_limit_bytes=limit)
    face = jax.ShapeDtypeStruct((FACE_BLOCKS + CORNER_BLOCKS, ny, nz), BF16)
    edge = jax.ShapeDtypeStruct((SIDE_BLOCKS, 2 * nx, nz), BF16)
    corner = jax.ShapeDtypeStruct((CORNER_BLOCKS + 1, 16, nz), BF16)
    grid = lambda n: jax.ShapeDtypeStruct((n, nx, ny, nz), F32)

    like = lambda value: jax.ShapeDtypeStruct(value.shape, value.dtype)
    traces = jnp.transpose(station_traces, (1, 0, 2))
    held = (adj_later, lame_first, shear, buoyancy, seafloor_depth, station_columns, traces)
    u0, fwd, carry, coeff, drive, y0 = pl.pallas_call(
        pack_kernel,
        out_shape=(
            like(adj_now),
            like(forward_field),
            grid(3),
            grid(2),
            grid(2),
            edge,
        ),
        in_specs=[anywhere] * 9,
        out_specs=(vmem,) * 6,
        scratch_shapes=[pltpu.VMEM(value.shape, value.dtype) for value in held]
        + [pltpu.SemaphoreType.DMA((9,))],
        compiler_params=params,
        name="pack",
    )(
        *(
            pltpu.with_memory_space_constraint(value, pltpu.HBM)
            for value in (adj_now, adj_later, forward_field, *held[1:])
        )
    )

    def exchange(value, partner):
        return lax.ppermute(value, AXES, swap_map(sizes, partner))

    flip = lambda n: n + 1 if n % 2 == 0 else n - 1
    back = lambda n: n - 1 if n % 2 == 0 else n + 1
    y0 = exchange(y0, lambda a, b: (a, flip(b)))
    wide_x, wide_y = nx + 2 * RING, ny + PAD
    padded = lambda n, x=wide_x: jax.ShapeDtypeStruct((n, x, wide_y, nz), F32)
    x0, x1, y1, c0, c1, fwd, fwd_z = pl.pallas_call(
        face_kernel,
        out_shape=(
            face,
            face,
            edge,
            corner,
            corner,
            padded(3 * STEPS, nx + 2),
            grid(3 * STEPS),
        ),
        in_specs=[vmem] * 5,
        out_specs=(vmem,) * 7,
        compiler_params=params,
        name="faces",
    )(u0, fwd, carry, coeff, drive)
    x0, x1 = pl.pallas_call(
        corner_kernel,
        out_shape=(face, face),
        in_specs=[vmem] * 4,
        out_specs=(vmem,) * 2,
        input_output_aliases={2: 0, 3: 1},
        compiler_params=params,
        name="corners",
    )(y0, u0, x0, x1)
    x0 = exchange(x0, lambda a, b: (flip(a), b))
    x1 = exchange(x1, lambda a, b: (back(a), b))
    y1 = exchange(y1, lambda a, b: (a, back(b)))
    c0 = exchange(c0, lambda a, b: (flip(a), back(b)))
    c1 = exchange(c1, lambda a, b: (back(a), back(b)))

    tile = (padded(3), padded(3), padded(2), padded(2))
    split_up = count_s == 2
    depth = nz // 2 if split_up else nz
    sums = (jax.ShapeDtypeStruct((2, nx, ny, depth), F32),) * (1 + split_up)
    held = pl.pallas_call(
        stage_kernel,
        out_shape=(*tile, padded(3), padded(3)),
        in_specs=[vmem] * 4,
        out_specs=(vmem,) * 6,
        compiler_params=params,
        name="stage",
    )(u0, carry, coeff, drive)
    held = (*held[:4], fwd, *held[4:])
    staged = (*tile, like(fwd), padded(3), padded(3))
    shapes = (*staged, *(padded(3),) * 6, grid(2), *sums)
    held = pl.pallas_call(
        early_kernel,
        out_shape=shapes,
        in_specs=[vmem] * 10,
        out_specs=(vmem,) * len(shapes),
        input_output_aliases={3 + n: n for n in range(7)},
        compiler_params=params,
        name="early",
    )(fwd_z, y0, y1, *held)

    def side(second, faces, corners, held):
        message = (jax.ShapeDtypeStruct((2 * nx + 1, ny, depth), F32),) * second
        return pl.pallas_call(
            functools.partial(side_kernel, second),
            out_shape=(*shapes, *message),
            in_specs=[vmem] * (3 + len(shapes)),
            out_specs=(vmem,) * (len(shapes) + second),
            input_output_aliases={3 + n: n for n in range(len(shapes))},
            compiler_params=params,
            name="second" if second else "first",
        )(fwd_z, faces, corners, *held)

    held = side(False, x0, c0, held)
    *held, message = side(True, x1, c1, held)
    coeff, drive = held[2:4]
    u1, u2 = held[7:9]
    u2_d, u2_s = held[11:13]

    sums = held[14:]
    scale = 0.25 / (adj_now.shape[0] * count_s)
    if split_up:
        sent = lax.ppermute(message.astype(jnp.float16), "src", [(0, 1), (1, 0)])
        summed = pl.pallas_call(
            functools.partial(total_kernel, scale),
            out_shape=like(sums[0]),
            in_specs=[vmem] * 2,
            out_specs=anywhere,
            scratch_shapes=[
                pltpu.VMEM(sums[0].shape, F32),
                pltpu.SemaphoreType.DMA((2,)),
            ],
            compiler_params=params,
            name="total",
        )(sums[0], sent.astype(F32))
    else:
        summed = lax.psum_scatter(sums[0] * scale, "src", scatter_dimension=3, tiled=True)
    final = pl.pallas_call(
        last_kernel,
        out_shape=like(adj_now),
        in_specs=[vmem] * 6,
        out_specs=vmem,
        compiler_params=params,
        name="last",
    )(u2, u2_d, u2_s, u1, coeff, drive)
    return final, summed


def solution(mesh):
    in_specs = (
        P("src", None, "tx", "ty", None),
        P("src", None, "tx", "ty", None),
        P("src", None, None, "tx", "ty", None),
        P("tx", "ty", None),
        P("tx", "ty", None),
        P("tx", "ty", None),
        P("tx", "ty"),
        P("src", None),
        P("src", None, None),
    )
    out_specs = (P("src", None, "tx", "ty", None), P(None, "tx", "ty", "src"))
    return jax.shard_map(body, mesh=mesh, in_specs=in_specs, out_specs=out_specs, check_vma=False)
```

```python
import functools
import math

import jax
import jax.numpy as jnp
from jax import lax
from jax.experimental import pallas as pl
from jax.experimental.pallas import tpu as pltpu
from jax.sharding import PartitionSpec as P

STEPS = 3
STEP_SQUARED = 0.04
RING = 3
SOLID = 126
PAD = 8
AXES = ("tx", "ty", "src")
F32 = jnp.float32
BF16 = jnp.bfloat16
UNROLL = 8
TARGET = 13.0


def halo_units():
    units = []
    for name, count, rings in (("u", 3, 3), ("p", 3, 2), ("b", 1, 2)):
        for k in range(count):
            for ring in range(1, rings + 1):
                units.append((name, k, ring, "hi"))
                if ring == 1 and name != "b":
                    units.append((name, k, ring, "lo"))
    units += [("a", 0, 1, "hi"), ("a", 0, 2, "hi")]
    for k in range(3 * STEPS):
        units.append(("f", k, 1, "hi"))
    return units


def corner_entries():
    entries = []
    for name, count, rings in (("u", 3, 3), ("p", 3, 2), ("b", 1, 2), ("a", 1, 2)):
        for k in range(count):
            for ring_x in range(1, rings + 1):
                for ring_y in range(1, rings + 1):
                    if name in "up" and k == 2 and ring_x == ring_y == rings:
                        continue
                    entries.append((name, k, ring_x, ring_y, "hi"))
    return entries


UNITS = halo_units()
ROWS = [unit for unit in UNITS if unit[0] != "u" or unit[2] < 3]
CORNERS = corner_entries()
FACE_BLOCKS = len(ROWS)
SIDE_BLOCKS = (len(UNITS) + 1) // 2
CORNER_BLOCKS = (len(CORNERS) + 2 + 15) // 16


def position():
    i, j, s = (lax.axis_index(axis) for axis in AXES)
    return (i + 1) % 2, (j + 1) % 2, i, j, s


def split(value):
    top = value.astype(BF16).astype(F32)
    return top, value - top


def rigid_units(ring1, ring2, drive):
    lane = lax.broadcasted_iota(jnp.int32, ring1.shape, 1)
    half = ring1.shape[1] // 2
    top, rest = split(ring1)
    turned = pltpu.roll(rest, half, 1)
    first = jnp.where(lane < SOLID, turned, top)
    second = jnp.where(
        lane < 2, pltpu.roll(turned, half + 2, 1), pltpu.roll(turned, 4, 1)
    )
    strength = jnp.sum(drive, axis=1, keepdims=True)
    where = jnp.sum(jnp.where(drive != 0.0, lane.astype(F32), 0.0), axis=1, keepdims=True)
    hi, lo = split(strength)
    extra = jnp.where(lane == 4, hi, jnp.where(lane == 5, lo, where))
    second = jnp.where(lane < 4, second, jnp.where(lane < 7, extra, 0.0))
    return first, jnp.where(lane < SOLID, second, ring2)


def rigid_rows(first, second):
    lane = lax.broadcasted_iota(jnp.int32, first.shape, 1)
    size = first.shape[1]
    half = size // 2
    rest = jnp.where(lane < half, pltpu.roll(second, half - 4, 1), pltpu.roll(first, half, 1))
    rest = jnp.where(lane < size - 2, rest, pltpu.roll(second, size - 2, 1))
    ring1 = jnp.where(lane >= SOLID, first + rest, 0.0)
    ring2 = jnp.where(lane >= SOLID, second, 0.0)
    strength = second[:, 4:5] + second[:, 5:6]
    return ring1, ring2, jnp.where(lane.astype(F32) == second[:, 6:7], strength, 0.0)


def corner_blocks(units, high, more=None, behind=()):
    at = {unit: value for unit, value in zip(UNITS, units)}
    nx = units[0].shape[0]
    rows = []
    for entry in CORNERS:
        name, k, ring_x, ring_y, part = entry
        unit = at[name, k, ring_y, part]
        row = jnp.where(high, unit[nx - ring_x : nx - ring_x + 1], unit[ring_x - 1 : ring_x])
        if more and entry[:4] in more:
            row = row + more[entry[:4]]
        rows.append(row)
    rows += behind
    rows += [jnp.zeros_like(rows[0])] * (-len(rows) % 16)
    return [
        jnp.concatenate(rows[n : n + 16], axis=0).astype(BF16) for n in range(0, len(rows), 16)
    ]


def side_units(ref, nx):
    blocks = [ref[n].astype(F32) for n in range(SIDE_BLOCKS)]
    return [blocks[n // 2][nx * (n % 2) : nx * (n % 2) + nx] for n in range(len(UNITS))]


def edge_units(u_ref, f_ref, p_ref, c_ref, s_ref, high, ready=lambda name: None):
    nx, ny = c_ref.shape[1:3]

    def column(value, ring):
        return jnp.where(high, value[:, ny - ring, :], value[:, ring - 1, :])

    rigid = rigid_units(column(c_ref[0], 1), column(c_ref[0], 2), column(s_ref[0], 1))
    made = {}
    for wanted in "abfup":
        ready(wanted)
        for unit in UNITS:
            name, k, ring, part = unit
            if name != wanted:
                continue
            if name == "a":
                made[unit] = rigid[ring - 1]
                continue
            if name == "f":
                value = f_ref[0, k // 3, k % 3].astype(F32)
            else:
                value = u_ref[0, k] if name == "u" else p_ref[k] if name == "p" else c_ref[1]
            value = column(value, ring)
            made[unit] = split(value)[1] if part == "lo" else value
    return [made[unit] for unit in UNITS]


def unit_blocks(units):
    units = units + [jnp.zeros_like(units[0])] * (len(units) % 2)
    return [
        jnp.concatenate(units[n : n + 2], axis=0).astype(BF16) for n in range(0, len(units), 2)
    ]


def pack_kernel(
    u_in,
    v_in,
    f_in,
    lame_in,
    shear_in,
    buoy_in,
    depth_in,
    cols_in,
    amps_in,
    u_ref,
    f_ref,
    p_ref,
    c_ref,
    s_ref,
    y0_ref,
    v_ref,
    lame_ref,
    shear_ref,
    buoy_ref,
    depth_ref,
    cols_ref,
    amps_ref,
    sems,
):
    copies = [
        pltpu.make_async_copy(src, dst, sems.at[n])
        for n, (src, dst) in enumerate(
            (
                (depth_in, depth_ref),
                (cols_in, cols_ref),
                (amps_in, amps_ref),
                (buoy_in, buoy_ref),
                (shear_in, shear_ref),
                (lame_in, lame_ref),
                (f_in, f_ref),
                (u_in, u_ref),
                (v_in, v_ref),
            )
        )
    ]
    for copy in copies:
        copy.start()
    for copy in copies[:6]:
        copy.wait()
    nx, ny, nz = lame_ref.shape
    _, even_j, i, j, _ = position()
    total_y = ny * lax.axis_size("ty")
    base = i * nx * total_y + j * ny
    levels = lax.broadcasted_iota(jnp.int32, (ny, nz), 1).astype(F32)
    eye = lax.broadcasted_iota(jnp.int32, (ny, ny), 0) == lax.broadcasted_iota(
        jnp.int32, (ny, ny), 1
    )
    own_y = lax.broadcasted_iota(jnp.int32, (ny, cols_ref.shape[1]), 0)
    depth_all = depth_ref[...].astype(F32)
    for x in range(nx):
        depth = jnp.sum(jnp.where(eye, depth_all[x : x + 1, :], 0.0), axis=1, keepdims=True)
        buoy = STEP_SQUARED * buoy_ref[x]
        mu = jnp.where(levels >= depth, shear_ref[x], 0.0)
        c_ref[0, x] = buoy * mu
        c_ref[1, x] = buoy * (lame_ref[x] + mu)
        here = cols_ref[...] == own_y + (base + x * total_y)
        floor = levels == depth
        drive = []
        for t in range(STEPS):
            amp = jnp.sum(jnp.where(here, amps_ref[t], 0.0), axis=1, keepdims=True)
            drive.append(jnp.where(floor, buoy * amp, 0.0))
        s_ref[0, x] = drive[1]
        s_ref[1, x] = drive[2]
        p_ref[2, x] = drive[0]

    def ready(name):
        if name == "f":
            copies[6].wait()
        elif name == "u":
            copies[7].wait()
        elif name == "p":
            copies[8].wait()
            for x in range(nx):
                for k in range(3):
                    p = 2.0 * u_ref[0, k, x] - v_ref[0, k, x]
                    p_ref[k, x] = p + p_ref[k, x] if k == 2 else p

    units = edge_units(u_ref, f_ref, p_ref, c_ref, s_ref, even_j == 1, ready)
    for n, block in enumerate(unit_blocks(units)):
        y0_ref[n] = block


def folded(u_ref, p_ref, c_ref, x2, x3, quarter):
    u = [u_ref[0, k, x3] for k in range(3)]
    row = lax.broadcasted_iota(jnp.int32, u[0].shape, 0)
    ny = u[0].shape[0]

    def slope_y(value):
        up, down = beside_y(value)
        return jnp.where(row == ny - 1, 0.0, up) - jnp.where(row == 0, 0.0, down)

    def slope_z(value):
        up, down = beside_z(value)
        return up - down

    rigid, bulk = c_ref[0, x2], c_ref[1, x2]
    grad_div = (
        u[0] + quarter * (slope_y(u[1]) + slope_z(u[2])),
        quarter * slope_y(u[0]),
        quarter * slope_z(u[0]),
    )
    return [p_ref[k, x2] + rigid * u[k] + bulk * grad_div[k] for k in range(3)]


def face_kernel(
    u_ref, f_ref, p_ref, c_ref, s_ref, x0_ref, x1_ref, y1_ref, c0_ref, c1_ref
):
    nx = c_ref.shape[1]
    even_i, even_j = position()[:2]
    units = edge_units(u_ref, f_ref, p_ref, c_ref, s_ref, even_j == 0)
    for n, block in enumerate(unit_blocks(units)):
        y1_ref[n] = block
    for ref, high in ((c0_ref, even_i == 1), (c1_ref, even_i == 0)):
        for n, block in enumerate(corner_blocks(units, high)):
            ref[n] = block
    for dst, high in ((x0_ref, even_i == 1), (x1_ref, even_i == 0)):
        at = [jnp.where(high, nx - ring, ring - 1) for ring in (1, 2, 3)]
        rigid = rigid_units(c_ref[0, at[0]], c_ref[0, at[1]], s_ref[0, at[0]])
        fresh = folded(u_ref, p_ref, c_ref, at[1], at[2], jnp.where(high, -0.25, 0.25))
        for n, (name, k, ring, part) in enumerate(ROWS):
            x = at[ring - 1]
            if name == "f":
                dst[n] = f_ref[0, k // 3, k % 3, x]
            elif name == "a":
                dst[n] = rigid[ring - 1].astype(BF16)
            else:
                if name == "p" and ring == 2:
                    value = fresh[k]
                else:
                    value = u_ref[0, k, x] if name == "u" else p_ref[k, x] if name == "p" else c_ref[1, x]
                dst[n] = (split(value)[1] if part == "lo" else value).astype(BF16)


def stage_forward(f_in, f_ref, fz_ref):
    nx, ny, nz = fz_ref.shape[1:]
    wide = f_ref.shape[2]
    for k in range(3 * STEPS):
        for x in range(nx):
            value = f_in[0, k // 3, k % 3, x].astype(F32)
            f_ref[k, x + 1, :ny, :] = value
            f_ref[k, x + 1, ny:, :] = jnp.zeros((wide - ny, nz), F32)
            up, down = beside_z(value)
            fz_ref[k, x] = up - down
        for x in (0, nx + 1):
            f_ref[k, x] = jnp.zeros(f_ref.shape[2:], F32)


def corner_kernel(y0_ref, u_ref, x0_in, x1_in, x0_ref, x1_ref):
    del x0_in, x1_in
    even_i, even_j = position()[:2]
    nx, ny = u_ref.shape[2:4]
    units = side_units(y0_ref, nx)
    bulk = units[UNITS.index(("b", 0, 1, "hi"))]
    for dst, high in ((x0_ref, even_i == 1), (x1_ref, even_i == 0)):
        x3 = jnp.where(high, nx - 3, 2)
        top = [u_ref[0, k, x3, ny - 1 :] for k in range(2)]
        low = [u_ref[0, k, x3, :1] for k in range(2)]
        near = [jnp.where(even_j == 1, a, b) for a, b in zip(top, low)]
        far = [jnp.where(even_j == 1, b, a) for a, b in zip(top, low)]
        weight = jnp.where(high, bulk[nx - 2 : nx - 1], bulk[1:2])
        weight = weight * jnp.where(high == (even_j == 1), 0.25, -0.25)
        more = {("p", 0, 2, 1): weight * near[1], ("p", 1, 2, 1): weight * near[0]}
        for n, block in enumerate(corner_blocks(units, high, more, far)):
            dst[FACE_BLOCKS + n] = block


def beside_z(value):
    tiles = [value[:, n : n + 128] for n in range(0, value.shape[1], 128)]
    lane = lax.broadcasted_iota(jnp.int32, tiles[0].shape, 1)
    zero = jnp.zeros_like(tiles[0])
    ups = [pltpu.roll(tile, 127, 1) for tile in tiles] + [zero]
    downs = [zero] + [pltpu.roll(tile, 1, 1) for tile in tiles]
    up = [jnp.where(lane == 127, ups[n + 1], ups[n]) for n in range(len(tiles))]
    down = [jnp.where(lane == 0, downs[n], downs[n + 1]) for n in range(len(tiles))]
    return jnp.concatenate(up, axis=1), jnp.concatenate(down, axis=1)


def beside_y(value):
    return pltpu.roll(value, value.shape[0] - 1, 0), pltpu.roll(value, 1, 0)


class Row:
    def __init__(self, x, cur, zd):
        self.x = x
        self.um, self.uc, self.up = ([cur[k, x + d] for k in range(3)] for d in (-1, 0, 1))
        self.ys = [beside_y(self.uc[k]) for k in range(3)]
        self.zd = zd
        self.dx = [self.up[k] - self.um[k] for k in range(3)]

    def slopes(self, rows):
        return [
            (self.dx[k][:rows], (self.ys[k][0] - self.ys[k][1])[:rows], self.zd[k, self.x, :rows])
            for k in range(3)
        ]


def advance_row(t, row, before, p_ref, c_ref, s_ref, zs, rows):
    x, um, uc, up, dx, ys, zd = row.x, row.um, row.uc, row.up, row.dx, row.ys, row.zd
    dz1 = zd[1, x]
    tilt = [beside_y(value) for value in (dx[1], dx[0] + zd[2, x], dz1)]
    cross = (
        (tilt[0][0] - tilt[0][1]) + (zd[2, x + 1] - zd[2, x - 1]),
        tilt[1][0] - tilt[1][1],
        (tilt[2][0] - tilt[2][1]) + (zd[0, x + 1] - zd[0, x - 1]),
    )
    rigid, bulk = c_ref[0, x, :rows], c_ref[1, x, :rows]
    fresh = []
    for k in range(3):
        pairs = (um[k] + up[k], ys[k][0] + ys[k][1], zs[k, x])
        laplace = pairs[0] + pairs[1] + pairs[2] - 6.0 * uc[k]
        grad_div = pairs[k] - 2.0 * uc[k] + 0.25 * cross[k]
        if t == 0:
            carry = p_ref[k, x, :rows]
        else:
            carry = 2.0 * uc[k][:rows] - before[k, x, :rows]
            if k == 2:
                carry = carry + s_ref[t - 1, x, :rows]
        fresh.append(carry + rigid * laplace[:rows] + bulk * grad_div[:rows])
    return fresh


def imprint_row(t, row, c_ref, f_ref, fz_ref, rows):
    x = row.x
    ga = row.slopes(rows)
    gf = []
    for k in range(3):
        n, r = 3 * t + k, x - RING + 1
        yp, ym = beside_y(f_ref[n, r])
        gf.append(
            (
                f_ref[n, r + 1, :rows] - f_ref[n, r - 1, :rows],
                (yp - ym)[:rows],
                fz_ref[n, x - RING],
            )
        )
    div = (ga[0][0] + ga[1][1] + ga[2][2]) * (gf[0][0] + gf[1][1] + gf[2][2])
    both = ga[0][0] * gf[0][0]
    for k in range(3):
        for d in range(3):
            if k + d > 0:
                both = both + ga[k][d] * gf[k][d]
    return div, jnp.where(c_ref[0, x, :rows] > 0.0, both, 0.0)


def joined(get, units):
    n = 0
    while n < len(units):
        name, k, ring, _ = units[n]
        if name == "a":
            for entry in zip("ccs", (0, 0, 0), (1, 2, 1), rigid_rows(get(n), get(n + 1))):
                yield entry
            n += 2
            continue
        value = get(n)
        if name in "up" and ring == 1:
            value = value + get(n + 1)
            n += 1
        n += 1
        yield ("c", 1, ring, value) if name == "b" else (name, k, ring, value)


def joined_corner(get):
    n = 0
    while n < len(CORNERS):
        name, k, ring_x, ring_y, _ = CORNERS[n]
        if name == "a":
            for x in (1, 2):
                ring1, ring2, drive = rigid_rows(get(n), get(n + 1))
                yield "c", 0, x, 1, ring1
                yield "c", 0, x, 2, ring2
                if x == 1:
                    yield "s", 0, 1, 1, drive
                n += 2
            continue
        yield ("c", 1, ring_x, ring_y, get(n)) if name == "b" else (name, k, ring_x, ring_y, get(n))
        n += 1


def keep_z(k, x, value, zd, zs, rows=slice(None)):
    up, down = beside_z(value)
    zd[k, x, rows] = up - down
    zs[k, x, rows] = up + down


def middle_rows(nx):
    spans = [range(RING + 1 + t, RING + nx - 1 - t) for t in range(STEPS)]
    return [(span if t < STEPS - 1 else (), span) for t, span in enumerate(spans)]


def side_rows():
    steps = []
    for t in range(STEPS):
        outer = range(t + 1, RING + 1 + t) if t < STEPS - 1 else ()
        steps.append((outer, range(RING, RING + 1 + t)))
    return steps


def run_steps(refs, fz_ref, sum_ref, sums, rows, at):
    nx, ny, nz = fz_ref.shape[1:]
    fields, c_ref = refs["fields"], refs["c"]
    wide_y = c_ref.shape[2]
    for t, (outer, inner) in enumerate(rows):
        cur, zd, zs = fields[t]
        for m in sorted({*outer, *inner}):
            row = Row(at(m), cur, zd)
            x = row.x
            if m in outer:
                nxt, nd, ns = fields[t + 1]
                fresh = advance_row(
                    t, row, fields[t - 1][0], refs["p"], c_ref, refs["s"], zs, wide_y
                )
                for k in range(3):
                    nxt[k, x] = fresh[k]
                    keep_z(k, x, fresh[k], nd, ns)
            if m not in inner:
                continue
            terms = imprint_row(t, row, c_ref, refs["f"], fz_ref, ny)
            for n in range(2):
                value = terms[n]
                own = x - RING
                if t > 0:
                    value = value + sum_ref[n, own]
                if t < STEPS - 1:
                    sum_ref[n, own] = value
                elif len(sums) == 1:
                    sums[0][n, own] = value
                else:
                    half = nz // 2
                    first = position()[4] == 0
                    sums[0][n, own] = jnp.where(first, value[:, :half], value[:, half:])
                    sums[1][n, own] = jnp.where(first, value[:, half:], value[:, :half])


def lay_out(theirs, message):
    nx = theirs.shape[1]
    top = jnp.full(theirs.shape[2:], 1e-30, F32)
    for n in range(2):
        for row in range(nx):
            top = jnp.maximum(top, jnp.abs(theirs[n, row]))
    power = jnp.floor(jnp.log(top) * (1.0 / math.log(2.0)))
    scale = jnp.exp((TARGET - power) * math.log(2.0))
    for n in range(2):
        for row in range(nx):
            message[n * nx + row] = theirs[n, row] * scale
    message[2 * nx] = power


def run_side(refs, fz_ref, sum_ref, sums, high):
    nx = fz_ref.shape[1]
    wide = nx + 2 * RING
    field, zd, zs = refs["fields"][0]
    for row in range(RING):
        x = jnp.where(high, wide - 1 - row, row)
        for k in range(3):
            keep_z(k, x, field[k, x], zd, zs)
    at = lambda row: jnp.where(high, wide - 1 - row, row)
    run_steps(refs, fz_ref, sum_ref, sums, side_rows(), at)


def named(held):
    u, p, c, s, f, ud, us, v, w, vd, vs, wd, ws, under_way, *sums = held
    refs = {"u": u, "p": p, "c": c, "s": s, "f": f}
    refs["fields"] = ((u, ud, us), (v, vd, vs), (w, wd, ws))
    return refs, under_way, sums


def beyond(axis, even, index):
    other = jnp.where(even == 1, index - 1, index + 1)
    return (other >= 0) & (other < lax.axis_size(axis))


def stage_kernel(
    u_in, p_in, c_in, s_in, f_in, u_ref, p_ref, c_ref, s_ref, f_ref, ud_ref, us_ref, fz_ref
):
    nx, ny, nz = c_in.shape[1:]
    wide = u_ref.shape[2]
    for src, ref in ((u_in, u_ref), (p_in, p_ref), (c_in, c_ref), (s_in, s_ref)):
        lead = (0,) if src is u_in else ()
        for k in range(ref.shape[0]):
            for x in range(ref.shape[1]):
                if RING <= x < RING + nx:
                    value = src[lead + (k, x - RING)]
                    ref[k, x, :ny, :] = value
                    ref[k, x, ny:, :] = jnp.zeros((wide - ny, nz), F32)
                    if src is u_in:
                        keep_z(k, x, value, ud_ref, us_ref, slice(0, ny))
                else:
                    ref[k, x] = jnp.zeros(ref.shape[2:], F32)
    stage_forward(f_in, f_ref, fz_ref)


def early_kernel(fz_ref, y0_in, y1_in, *rest):
    refs, under_way, sums = named(rest[7:])
    u_ref, ud_ref, us_ref = refs["fields"][0]
    nx, ny, nz = fz_ref.shape[1:]
    wide = u_ref.shape[2]
    even_i, even_j, i, j, _ = position()
    ok_y1 = beyond("ty", even_j, j)

    near = side_units(y0_in, nx)
    far = [jnp.where(ok_y1, value, 0.0) for value in side_units(y1_in, nx)]
    top = [jnp.where(even_j == 1, a, b) for a, b in zip(near, far)]
    low = [jnp.where(even_j == 1, b, a) for a, b in zip(near, far)]
    for values, high in ((top, True), (low, False)):
        for name, k, ring, value in joined(lambda n: values[n], UNITS):
            y = ny - 1 + ring if high else wide - ring
            first = 1 if name == "f" else RING
            for x in range(nx):
                refs[name][k, first + x, y : y + 1, :] = value[x : x + 1]
    for x in range(RING, RING + nx):
        for k in range(3):
            keep_z(k, x, u_ref[k, x, ny:], ud_ref, us_ref, slice(ny, wide))
    run_steps(refs, fz_ref, under_way, sums, middle_rows(nx), lambda row: row)

    @pl.when(jnp.logical_not(beyond("tx", even_i, i)))
    def _():
        run_side(refs, fz_ref, under_way, sums, even_i == 0)


def side_kernel(second, fz_ref, faces, corners, *rest):
    if second:
        *rest, message = rest
    refs, under_way, sums = named(rest[len(rest) // 2 :])
    nx, ny, nz = fz_ref.shape[1:]
    wide = refs["u"].shape[2]
    even_i, even_j, i, j, _ = position()
    high = even_i == (0 if second else 1)

    def run():
        for name, k, ring, value in joined(lambda n: faces[n].astype(F32), ROWS):
            first = 1 if name == "f" else RING
            x = jnp.where(high, first + nx - 1 + ring, first - ring)
            refs[name][k, x, :ny, :] = value
        near = [faces[FACE_BLOCKS + n].astype(F32) for n in range(CORNER_BLOCKS)]
        ok_y1 = beyond("ty", even_j, j)
        far = [jnp.where(ok_y1, corners[n].astype(F32), 0.0) for n in range(CORNER_BLOCKS)]
        for y_high in (True, False):
            flag = even_j == (1 if y_high else 0)
            values = [jnp.where(flag, a, b) for a, b in zip(near, far)]
            row = lambda n: values[n // 16][n % 16 : n % 16 + 1]
            for name, k, ring_x, ring_y, value in joined_corner(row):
                x = jnp.where(high, RING + nx - 1 + ring_x, RING - ring_x)
                y = ny - 1 + ring_y if y_high else wide - ring_y
                refs[name][k, x, y : y + 1, :] = value
        place = len(CORNERS)
        u3 = [near[(place + k) // 16][(place + k) % 16 : (place + k) % 16 + 1] for k in range(2)]
        x = jnp.where(high, RING + nx + 1, RING - 2)
        for y_high in (True, False):
            y = ny if y_high else wide - 1
            quarter = jnp.where(high == y_high, -0.25, 0.25)
            quarter = jnp.where(even_j == (0 if y_high else 1), quarter, 0.0)
            weight = refs["c"][1, x, y : y + 1, :] * quarter
            for k in range(2):
                refs["p"][k, x, y : y + 1, :] += weight * u3[1 - k]
        run_side(refs, fz_ref, under_way, sums, high)

    if second:
        pl.when(beyond("tx", even_i, i))(run)
    else:
        run()
    if second:
        lay_out(sums[-1], message)


def total_kernel(scale, own_ref, sent_ref, out_ref, stage, sems):
    nx = own_ref.shape[1]
    back = jnp.exp((sent_ref[2 * nx] - TARGET) * math.log(2.0))
    copies = []
    for n in range(2):
        for x in range(nx):
            stage[n, x] = (own_ref[n, x] + sent_ref[n * nx + x] * back) * scale
        copies.append(pltpu.make_async_copy(stage.at[n], out_ref.at[n], sems.at[n]))
        copies[n].start()
    for copy in copies:
        copy.wait()


def last_kernel(w_ref, wd_ref, ws_ref, v_ref, c_ref, s_ref, out_ref):
    nx, ny = out_ref.shape[2:4]

    @pl.loop(RING, RING + nx, unroll=UNROLL)
    def _(x):
        fresh = advance_row(
            STEPS - 1, Row(x, w_ref, wd_ref), v_ref, None, c_ref, s_ref, ws_ref, ny
        )
        for k in range(3):
            out_ref[0, k, x - RING] = fresh[k]


def swap_map(sizes, partner):
    nx, ny, ns = sizes

    def meets(i, j):
        a, b = partner(i, j)
        return 0 <= a < nx and 0 <= b < ny

    pairs = []
    for i in range(nx):
        for j in range(ny):
            for s in range(ns):
                if meets(i, j):
                    to = (*partner(i, j), s)
                elif not (meets(i, j ^ 1) or meets(0, 1) or meets(1, 0)):
                    across = j + 1 if j % 2 else j - 1
                    to = (i, across, s) if 0 <= across < ny else (i, j, s ^ 1 if s ^ 1 < ns else s)
                elif not meets(i, j ^ 1):
                    to = (i, j ^ 1, s)
                else:
                    to = (i, j, s ^ 1 if s ^ 1 < ns else s)
                pairs.append(((i * ny + j) * ns + s, (to[0] * ny + to[1]) * ns + to[2]))
    return pairs


def body(
    adj_now,
    adj_later,
    forward_field,
    lame_first,
    shear,
    buoyancy,
    seafloor_depth,
    station_columns,
    station_traces,
):
    nx, ny, nz = lame_first.shape
    sizes = tuple(lax.axis_size(axis) for axis in AXES)
    count_s = sizes[2]
    vmem = pl.BlockSpec(memory_space=pltpu.VMEM)
    anywhere = pl.BlockSpec(memory_space=pl.ANY)
    limit = 30 * 1024 * 1024
    params = pltpu.CompilerParams(vmem_limit_bytes=limit)
    face = jax.ShapeDtypeStruct((FACE_BLOCKS + CORNER_BLOCKS, ny, nz), BF16)
    edge = jax.ShapeDtypeStruct((SIDE_BLOCKS, 2 * nx, nz), BF16)
    corner = jax.ShapeDtypeStruct((CORNER_BLOCKS, 16, nz), BF16)
    grid = lambda n: jax.ShapeDtypeStruct((n, nx, ny, nz), F32)

    like = lambda value: jax.ShapeDtypeStruct(value.shape, value.dtype)
    traces = jnp.transpose(station_traces, (1, 0, 2))
    held = (adj_later, lame_first, shear, buoyancy, seafloor_depth, station_columns, traces)
    u0, fwd, carry, coeff, drive, y0 = pl.pallas_call(
        pack_kernel,
        out_shape=(
            like(adj_now),
            like(forward_field),
            grid(3),
            grid(2),
            grid(2),
            edge,
        ),
        in_specs=[anywhere] * 9,
        out_specs=(vmem,) * 6,
        scratch_shapes=[pltpu.VMEM(value.shape, value.dtype) for value in held]
        + [pltpu.SemaphoreType.DMA((9,))],
        compiler_params=params,
        name="pack",
    )(
        *(
            pltpu.with_memory_space_constraint(value, pltpu.HBM)
            for value in (adj_now, adj_later, forward_field, *held[1:])
        )
    )

    def exchange(value, partner):
        return lax.ppermute(value, AXES, swap_map(sizes, partner))

    flip = lambda n: n + 1 if n % 2 == 0 else n - 1
    back = lambda n: n - 1 if n % 2 == 0 else n + 1
    y0 = exchange(y0, lambda a, b: (a, flip(b)))
    wide_x, wide_y = nx + 2 * RING, ny + PAD
    padded = lambda n, x=wide_x: jax.ShapeDtypeStruct((n, x, wide_y, nz), F32)
    x0, x1, y1, c0, c1 = pl.pallas_call(
        face_kernel,
        out_shape=(
            face,
            face,
            edge,
            corner,
            corner,
        ),
        in_specs=[vmem] * 5,
        out_specs=(vmem,) * 5,
        compiler_params=params,
        name="faces",
    )(u0, fwd, carry, coeff, drive)
    x0, x1 = pl.pallas_call(
        corner_kernel,
        out_shape=(face, face),
        in_specs=[vmem] * 4,
        out_specs=(vmem,) * 2,
        input_output_aliases={2: 0, 3: 1},
        compiler_params=params,
        name="corners",
    )(y0, u0, x0, x1)
    x0 = exchange(x0, lambda a, b: (flip(a), b))
    x1 = exchange(x1, lambda a, b: (back(a), b))
    y1 = exchange(y1, lambda a, b: (a, back(b)))
    c0 = exchange(c0, lambda a, b: (flip(a), back(b)))
    c1 = exchange(c1, lambda a, b: (back(a), back(b)))

    tile = (padded(3), padded(3), padded(2), padded(2))
    split_up = count_s == 2
    depth = nz // 2 if split_up else nz
    sums = (jax.ShapeDtypeStruct((2, nx, ny, depth), F32),) * (1 + split_up)
    staged = (*tile, padded(3 * STEPS, nx + 2), padded(3), padded(3))
    *held, fwd_z = pl.pallas_call(
        stage_kernel,
        out_shape=(*staged, grid(3 * STEPS)),
        in_specs=[vmem] * 5,
        out_specs=(vmem,) * 8,
        compiler_params=params,
        name="stage",
    )(u0, carry, coeff, drive, fwd)
    shapes = (*staged, *(padded(3),) * 6, grid(2), *sums)
    held = pl.pallas_call(
        early_kernel,
        out_shape=shapes,
        in_specs=[vmem] * 10,
        out_specs=(vmem,) * len(shapes),
        input_output_aliases={3 + n: n for n in range(7)},
        compiler_params=params,
        name="early",
    )(fwd_z, y0, y1, *held)

    def side(second, faces, corners, held):
        message = (jax.ShapeDtypeStruct((2 * nx + 1, ny, depth), F32),) * second
        return pl.pallas_call(
            functools.partial(side_kernel, second),
            out_shape=(*shapes, *message),
            in_specs=[vmem] * (3 + len(shapes)),
            out_specs=(vmem,) * (len(shapes) + second),
            input_output_aliases={3 + n: n for n in range(len(shapes))},
            compiler_params=params,
            name="second" if second else "first",
        )(fwd_z, faces, corners, *held)

    held = side(False, x0, c0, held)
    *held, message = side(True, x1, c1, held)
    coeff, drive = held[2:4]
    u1, u2 = held[7:9]
    u2_d, u2_s = held[11:13]

    sums = held[14:]
    scale = 0.25 / (adj_now.shape[0] * count_s)
    if split_up:
        sent = lax.ppermute(message.astype(jnp.float16), "src", [(0, 1), (1, 0)])
        summed = pl.pallas_call(
            functools.partial(total_kernel, scale),
            out_shape=like(sums[0]),
            in_specs=[vmem] * 2,
            out_specs=anywhere,
            scratch_shapes=[
                pltpu.VMEM(sums[0].shape, F32),
                pltpu.SemaphoreType.DMA((2,)),
            ],
            compiler_params=params,
            name="total",
        )(sums[0], sent.astype(F32))
    else:
        summed = lax.psum_scatter(sums[0] * scale, "src", scatter_dimension=3, tiled=True)
    final = pl.pallas_call(
        last_kernel,
        out_shape=like(adj_now),
        in_specs=[vmem] * 6,
        out_specs=vmem,
        compiler_params=params,
        name="last",
    )(u2, u2_d, u2_s, u1, coeff, drive)
    return final, summed


def solution(mesh):
    in_specs = (
        P("src", None, "tx", "ty", None),
        P("src", None, "tx", "ty", None),
        P("src", None, None, "tx", "ty", None),
        P("tx", "ty", None),
        P("tx", "ty", None),
        P("tx", "ty", None),
        P("tx", "ty"),
        P("src", None),
        P("src", None, None),
    )
    out_specs = (P("src", None, "tx", "ty", None), P(None, "tx", "ty", "src"))
    return jax.shard_map(body, mesh=mesh, in_specs=in_specs, out_specs=out_specs, check_vma=False)
```

```python
import functools
import math

import jax
import jax.numpy as jnp
from jax import lax
from jax.experimental import pallas as pl
from jax.experimental.pallas import tpu as pltpu
from jax.sharding import PartitionSpec as P

STEPS = 3
STEP_SQUARED = 0.04
RING = 3
SOLID = 126
PAD = 8
AXES = ("tx", "ty", "src")
F32 = jnp.float32
BF16 = jnp.bfloat16
UNROLL = 8
TARGET = 13.0


def halo_units():
    units = []
    for name, count, rings in (("u", 3, 3), ("p", 3, 2), ("b", 1, 2)):
        for k in range(count):
            for ring in range(1, rings + 1):
                units.append((name, k, ring, "hi"))
                if ring == 1 and name != "b":
                    units.append((name, k, ring, "lo"))
    units += [("a", 0, 1, "hi"), ("a", 0, 2, "hi")]
    for k in range(3 * STEPS):
        units.append(("f", k, 1, "hi"))
    return units


def corner_entries():
    entries = []
    for name, count, rings in (("u", 3, 3), ("p", 3, 2), ("b", 1, 2), ("a", 1, 2)):
        for k in range(count):
            for ring_x in range(1, rings + 1):
                for ring_y in range(1, rings + 1):
                    if name in "up" and k == 2 and ring_x == ring_y == rings:
                        continue
                    entries.append((name, k, ring_x, ring_y, "hi"))
    return entries


UNITS = halo_units()
ROWS = [unit for unit in UNITS if unit[0] != "u" or unit[2] < 3]
CORNERS = corner_entries()
FACE_BLOCKS = len(ROWS)
SIDE_BLOCKS = (len(UNITS) + 1) // 2
CORNER_BLOCKS = (len(CORNERS) + 2 + 15) // 16


def position():
    i, j, s = (lax.axis_index(axis) for axis in AXES)
    return (i + 1) % 2, (j + 1) % 2, i, j, s


def split(value):
    top = value.astype(BF16).astype(F32)
    return top, value - top


def rigid_units(ring1, ring2, drive):
    lane = lax.broadcasted_iota(jnp.int32, ring1.shape, 1)
    half = ring1.shape[1] // 2
    top, rest = split(ring1)
    turned = pltpu.roll(rest, half, 1)
    first = jnp.where(lane < SOLID, turned, top)
    second = jnp.where(
        lane < 2, pltpu.roll(turned, half + 2, 1), pltpu.roll(turned, 4, 1)
    )
    strength = jnp.sum(drive, axis=1, keepdims=True)
    where = jnp.sum(jnp.where(drive != 0.0, lane.astype(F32), 0.0), axis=1, keepdims=True)
    hi, lo = split(strength)
    extra = jnp.where(lane == 4, hi, jnp.where(lane == 5, lo, where))
    second = jnp.where(lane < 4, second, jnp.where(lane < 7, extra, 0.0))
    return first, jnp.where(lane < SOLID, second, ring2)


def rigid_rows(first, second):
    lane = lax.broadcasted_iota(jnp.int32, first.shape, 1)
    size = first.shape[1]
    half = size // 2
    rest = jnp.where(lane < half, pltpu.roll(second, half - 4, 1), pltpu.roll(first, half, 1))
    rest = jnp.where(lane < size - 2, rest, pltpu.roll(second, size - 2, 1))
    ring1 = jnp.where(lane >= SOLID, first + rest, 0.0)
    ring2 = jnp.where(lane >= SOLID, second, 0.0)
    strength = second[:, 4:5] + second[:, 5:6]
    return ring1, ring2, jnp.where(lane.astype(F32) == second[:, 6:7], strength, 0.0)


def corner_blocks(units, high, more=None, behind=()):
    at = {unit: value for unit, value in zip(UNITS, units)}
    nx = units[0].shape[0]
    rows = []
    for entry in CORNERS:
        name, k, ring_x, ring_y, part = entry
        unit = at[name, k, ring_y, part]
        row = jnp.where(high, unit[nx - ring_x : nx - ring_x + 1], unit[ring_x - 1 : ring_x])
        if more and entry[:4] in more:
            row = row + more[entry[:4]]
        rows.append(row)
    rows += behind
    rows += [jnp.zeros_like(rows[0])] * (-len(rows) % 16)
    return [
        jnp.concatenate(rows[n : n + 16], axis=0).astype(BF16) for n in range(0, len(rows), 16)
    ]


def side_units(ref, nx):
    blocks = [ref[n].astype(F32) for n in range(SIDE_BLOCKS)]
    return [blocks[n // 2][nx * (n % 2) : nx * (n % 2) + nx] for n in range(len(UNITS))]


def edge_units(u_ref, f_ref, p_ref, c_ref, s_ref, high, ready=lambda name: None):
    nx, ny = c_ref.shape[1:3]

    def column(value, ring):
        return jnp.where(high, value[:, ny - ring, :], value[:, ring - 1, :])

    rigid = rigid_units(column(c_ref[0], 1), column(c_ref[0], 2), column(s_ref[0], 1))
    made = {}
    for wanted in "abfup":
        ready(wanted)
        for unit in UNITS:
            name, k, ring, part = unit
            if name != wanted:
                continue
            if name == "a":
                made[unit] = rigid[ring - 1]
                continue
            if name == "f":
                value = f_ref[0, k // 3, k % 3].astype(F32)
            else:
                value = u_ref[0, k] if name == "u" else p_ref[k] if name == "p" else c_ref[1]
            value = column(value, ring)
            made[unit] = split(value)[1] if part == "lo" else value
    return [made[unit] for unit in UNITS]


def unit_blocks(units):
    units = units + [jnp.zeros_like(units[0])] * (len(units) % 2)
    return [
        jnp.concatenate(units[n : n + 2], axis=0).astype(BF16) for n in range(0, len(units), 2)
    ]


def pack_kernel(
    u_in,
    v_in,
    f_in,
    lame_in,
    shear_in,
    buoy_in,
    depth_in,
    cols_in,
    amps_in,
    u_ref,
    f_ref,
    p_ref,
    c_ref,
    s_ref,
    y0_ref,
    v_ref,
    lame_ref,
    shear_ref,
    buoy_ref,
    depth_ref,
    cols_ref,
    amps_ref,
    sems,
):
    copies = [
        pltpu.make_async_copy(src, dst, sems.at[n])
        for n, (src, dst) in enumerate(
            (
                (depth_in, depth_ref),
                (cols_in, cols_ref),
                (amps_in, amps_ref),
                (buoy_in, buoy_ref),
                (shear_in, shear_ref),
                (lame_in, lame_ref),
                (f_in, f_ref),
                (u_in, u_ref),
                (v_in, v_ref),
            )
        )
    ]
    for copy in copies:
        copy.start()
    for copy in copies[:6]:
        copy.wait()
    nx, ny, nz = lame_ref.shape
    _, even_j, i, j, _ = position()
    total_y = ny * lax.axis_size("ty")
    base = i * nx * total_y + j * ny
    levels = lax.broadcasted_iota(jnp.int32, (ny, nz), 1).astype(F32)
    eye = lax.broadcasted_iota(jnp.int32, (ny, ny), 0) == lax.broadcasted_iota(
        jnp.int32, (ny, ny), 1
    )
    own_y = lax.broadcasted_iota(jnp.int32, (ny, cols_ref.shape[1]), 0)
    depth_all = depth_ref[...].astype(F32)
    for x in range(nx):
        depth = jnp.sum(jnp.where(eye, depth_all[x : x + 1, :], 0.0), axis=1, keepdims=True)
        buoy = STEP_SQUARED * buoy_ref[x]
        mu = jnp.where(levels >= depth, shear_ref[x], 0.0)
        c_ref[0, x] = buoy * mu
        c_ref[1, x] = buoy * (lame_ref[x] + mu)
        here = cols_ref[...] == own_y + (base + x * total_y)
        floor = levels == depth
        drive = []
        for t in range(STEPS):
            amp = jnp.sum(jnp.where(here, amps_ref[t], 0.0), axis=1, keepdims=True)
            drive.append(jnp.where(floor, buoy * amp, 0.0))
        s_ref[0, x] = drive[1]
        s_ref[1, x] = drive[2]
        p_ref[2, x] = drive[0]

    def ready(name):
        if name == "f":
            copies[6].wait()
        elif name == "u":
            copies[7].wait()
        elif name == "p":
            copies[8].wait()
            for x in range(nx):
                for k in range(3):
                    p = 2.0 * u_ref[0, k, x] - v_ref[0, k, x]
                    p_ref[k, x] = p + p_ref[k, x] if k == 2 else p

    units = edge_units(u_ref, f_ref, p_ref, c_ref, s_ref, even_j == 1, ready)
    for n, block in enumerate(unit_blocks(units)):
        y0_ref[n] = block


def folded(u_ref, p_ref, c_ref, x2, x3, quarter):
    u = [u_ref[0, k, x3] for k in range(3)]
    row = lax.broadcasted_iota(jnp.int32, u[0].shape, 0)
    ny = u[0].shape[0]

    def slope_y(value):
        up, down = beside_y(value)
        return jnp.where(row == ny - 1, 0.0, up) - jnp.where(row == 0, 0.0, down)

    def slope_z(value):
        up, down = beside_z(value)
        return up - down

    rigid, bulk = c_ref[0, x2], c_ref[1, x2]
    grad_div = (
        u[0] + quarter * (slope_y(u[1]) + slope_z(u[2])),
        quarter * slope_y(u[0]),
        quarter * slope_z(u[0]),
    )
    return [p_ref[k, x2] + rigid * u[k] + bulk * grad_div[k] for k in range(3)]


def face_kernel(
    u_ref, f_ref, p_ref, c_ref, s_ref, x0_ref, x1_ref, y1_ref, c0_ref, c1_ref
):
    nx = c_ref.shape[1]
    even_i, even_j = position()[:2]
    units = edge_units(u_ref, f_ref, p_ref, c_ref, s_ref, even_j == 0)
    for n, block in enumerate(unit_blocks(units)):
        y1_ref[n] = block
    for ref, high in ((c0_ref, even_i == 1), (c1_ref, even_i == 0)):
        for n, block in enumerate(corner_blocks(units, high)):
            ref[n] = block
    for dst, high in ((x0_ref, even_i == 1), (x1_ref, even_i == 0)):
        at = [jnp.where(high, nx - ring, ring - 1) for ring in (1, 2, 3)]
        rigid = rigid_units(c_ref[0, at[0]], c_ref[0, at[1]], s_ref[0, at[0]])
        fresh = folded(u_ref, p_ref, c_ref, at[1], at[2], jnp.where(high, -0.25, 0.25))
        for n, (name, k, ring, part) in enumerate(ROWS):
            x = at[ring - 1]
            if name == "f":
                dst[n] = f_ref[0, k // 3, k % 3, x]
            elif name == "a":
                dst[n] = rigid[ring - 1].astype(BF16)
            else:
                if name == "p" and ring == 2:
                    value = fresh[k]
                else:
                    value = u_ref[0, k, x] if name == "u" else p_ref[k, x] if name == "p" else c_ref[1, x]
                dst[n] = (split(value)[1] if part == "lo" else value).astype(BF16)


def stage_forward(f_in, f_ref, fz_ref):
    nx, ny, nz = fz_ref.shape[1:]
    wide = f_ref.shape[2]
    for k in range(3 * STEPS):
        for x in range(nx):
            value = f_in[0, k // 3, k % 3, x].astype(F32)
            f_ref[k, x + 1, :ny, :] = value
            f_ref[k, x + 1, ny:, :] = jnp.zeros((wide - ny, nz), F32)
            up, down = beside_z(value)
            fz_ref[k, x] = up - down
        for x in (0, nx + 1):
            f_ref[k, x] = jnp.zeros(f_ref.shape[2:], F32)


def corner_kernel(y0_ref, u_ref, x0_in, x1_in, x0_ref, x1_ref):
    del x0_in, x1_in
    even_i, even_j = position()[:2]
    nx, ny = u_ref.shape[2:4]
    units = side_units(y0_ref, nx)
    bulk = units[UNITS.index(("b", 0, 1, "hi"))]
    for dst, high in ((x0_ref, even_i == 1), (x1_ref, even_i == 0)):
        x3 = jnp.where(high, nx - 3, 2)
        top = [u_ref[0, k, x3, ny - 1 :] for k in range(2)]
        low = [u_ref[0, k, x3, :1] for k in range(2)]
        near = [jnp.where(even_j == 1, a, b) for a, b in zip(top, low)]
        far = [jnp.where(even_j == 1, b, a) for a, b in zip(top, low)]
        weight = jnp.where(high, bulk[nx - 2 : nx - 1], bulk[1:2])
        weight = weight * jnp.where(high == (even_j == 1), 0.25, -0.25)
        more = {("p", 0, 2, 1): weight * near[1], ("p", 1, 2, 1): weight * near[0]}
        for n, block in enumerate(corner_blocks(units, high, more, far)):
            dst[FACE_BLOCKS + n] = block


def beside_z(value):
    tiles = [value[:, n : n + 128] for n in range(0, value.shape[1], 128)]
    lane = lax.broadcasted_iota(jnp.int32, tiles[0].shape, 1)
    zero = jnp.zeros_like(tiles[0])
    ups = [pltpu.roll(tile, 127, 1) for tile in tiles] + [zero]
    downs = [zero] + [pltpu.roll(tile, 1, 1) for tile in tiles]
    up = [jnp.where(lane == 127, ups[n + 1], ups[n]) for n in range(len(tiles))]
    down = [jnp.where(lane == 0, downs[n], downs[n + 1]) for n in range(len(tiles))]
    return jnp.concatenate(up, axis=1), jnp.concatenate(down, axis=1)


def beside_y(value):
    return pltpu.roll(value, value.shape[0] - 1, 0), pltpu.roll(value, 1, 0)


class Row:
    def __init__(self, x, cur, zd):
        self.x = x
        self.um, self.uc, self.up = ([cur[k, x + d] for k in range(3)] for d in (-1, 0, 1))
        self.ys = [beside_y(self.uc[k]) for k in range(3)]
        self.zd = zd
        self.dx = [self.up[k] - self.um[k] for k in range(3)]

    def slopes(self, rows):
        return [
            (self.dx[k][:rows], (self.ys[k][0] - self.ys[k][1])[:rows], self.zd[k, self.x, :rows])
            for k in range(3)
        ]


def advance_row(t, row, before, p_ref, c_ref, s_ref, zs, rows):
    x, um, uc, up, dx, ys, zd = row.x, row.um, row.uc, row.up, row.dx, row.ys, row.zd
    dz1 = zd[1, x]
    tilt = [beside_y(value) for value in (dx[1], dx[0] + zd[2, x], dz1)]
    cross = (
        (tilt[0][0] - tilt[0][1]) + (zd[2, x + 1] - zd[2, x - 1]),
        tilt[1][0] - tilt[1][1],
        (tilt[2][0] - tilt[2][1]) + (zd[0, x + 1] - zd[0, x - 1]),
    )
    rigid, bulk = c_ref[0, x, :rows], c_ref[1, x, :rows]
    fresh = []
    for k in range(3):
        pairs = (um[k] + up[k], ys[k][0] + ys[k][1], zs[k, x])
        laplace = pairs[0] + pairs[1] + pairs[2] - 6.0 * uc[k]
        grad_div = pairs[k] - 2.0 * uc[k] + 0.25 * cross[k]
        if t == 0:
            carry = p_ref[k, x, :rows]
        else:
            carry = 2.0 * uc[k][:rows] - before[k, x, :rows]
            if k == 2:
                carry = carry + s_ref[t - 1, x, :rows]
        fresh.append(carry + rigid * laplace[:rows] + bulk * grad_div[:rows])
    return fresh


def imprint_row(t, row, c_ref, f_ref, fz_ref, rows):
    x = row.x
    ga = row.slopes(rows)
    gf = []
    for k in range(3):
        n, r = 3 * t + k, x - RING + 1
        yp, ym = beside_y(f_ref[n, r])
        gf.append(
            (
                f_ref[n, r + 1, :rows] - f_ref[n, r - 1, :rows],
                (yp - ym)[:rows],
                fz_ref[n, x - RING],
            )
        )
    div = (ga[0][0] + ga[1][1] + ga[2][2]) * (gf[0][0] + gf[1][1] + gf[2][2])
    both = ga[0][0] * gf[0][0]
    for k in range(3):
        for d in range(3):
            if k + d > 0:
                both = both + ga[k][d] * gf[k][d]
    return div, jnp.where(c_ref[0, x, :rows] > 0.0, both, 0.0)


def joined(get, units):
    n = 0
    while n < len(units):
        name, k, ring, _ = units[n]
        if name == "a":
            for entry in zip("ccs", (0, 0, 0), (1, 2, 1), rigid_rows(get(n), get(n + 1))):
                yield entry
            n += 2
            continue
        value = get(n)
        if name in "up" and ring == 1:
            value = value + get(n + 1)
            n += 1
        n += 1
        yield ("c", 1, ring, value) if name == "b" else (name, k, ring, value)


def joined_corner(get):
    n = 0
    while n < len(CORNERS):
        name, k, ring_x, ring_y, _ = CORNERS[n]
        if name == "a":
            for x in (1, 2):
                ring1, ring2, drive = rigid_rows(get(n), get(n + 1))
                yield "c", 0, x, 1, ring1
                yield "c", 0, x, 2, ring2
                if x == 1:
                    yield "s", 0, 1, 1, drive
                n += 2
            continue
        yield ("c", 1, ring_x, ring_y, get(n)) if name == "b" else (name, k, ring_x, ring_y, get(n))
        n += 1


def keep_z(k, x, value, zd, zs, rows=slice(None)):
    up, down = beside_z(value)
    zd[k, x, rows] = up - down
    zs[k, x, rows] = up + down


def middle_rows(nx):
    spans = [range(RING + 1 + t, RING + nx - 1 - t) for t in range(STEPS)]
    return [(span if t < STEPS - 1 else (), span) for t, span in enumerate(spans)]


def side_rows():
    steps = []
    for t in range(STEPS):
        outer = range(t + 1, RING + 1 + t) if t < STEPS - 1 else ()
        steps.append((outer, range(RING, RING + 1 + t)))
    return steps


def run_steps(refs, fz_ref, sum_ref, sums, rows, at):
    nx, ny, nz = fz_ref.shape[1:]
    fields, c_ref = refs["fields"], refs["c"]
    wide_y = c_ref.shape[2]
    for t, (outer, inner) in enumerate(rows):
        cur, zd, zs = fields[t]
        for m in sorted({*outer, *inner}):
            row = Row(at(m), cur, zd)
            x = row.x
            if m in outer:
                nxt, nd, ns = fields[t + 1]
                fresh = advance_row(
                    t, row, fields[t - 1][0], refs["p"], c_ref, refs["s"], zs, wide_y
                )
                for k in range(3):
                    nxt[k, x] = fresh[k]
                    keep_z(k, x, fresh[k], nd, ns)
            if m not in inner:
                continue
            terms = imprint_row(t, row, c_ref, refs["f"], fz_ref, ny)
            for n in range(2):
                value = terms[n]
                own = x - RING
                if t > 0:
                    value = value + sum_ref[n, own]
                if t < STEPS - 1:
                    sum_ref[n, own] = value
                elif len(sums) == 1:
                    sums[0][n, own] = value
                else:
                    half = nz // 2
                    first = position()[4] == 0
                    sums[0][n, own] = jnp.where(first, value[:, :half], value[:, half:])
                    sums[1][n, own] = jnp.where(first, value[:, half:], value[:, :half])


def lay_out(theirs, message):
    nx = theirs.shape[1]
    top = jnp.full(theirs.shape[2:], 1e-30, F32)
    for n in range(2):
        for row in range(nx):
            top = jnp.maximum(top, jnp.abs(theirs[n, row]))
    power = jnp.floor(jnp.log(top) * (1.0 / math.log(2.0)))
    scale = jnp.exp((TARGET - power) * math.log(2.0))
    for n in range(2):
        for row in range(nx):
            message[n * nx + row] = theirs[n, row] * scale
    message[2 * nx] = power


def run_side(refs, fz_ref, sum_ref, sums, high):
    nx = fz_ref.shape[1]
    wide = nx + 2 * RING
    field, zd, zs = refs["fields"][0]
    for row in range(RING):
        x = jnp.where(high, wide - 1 - row, row)
        for k in range(3):
            keep_z(k, x, field[k, x], zd, zs)
    at = lambda row: jnp.where(high, wide - 1 - row, row)
    run_steps(refs, fz_ref, sum_ref, sums, side_rows(), at)


def named(held):
    u, p, c, s, f, ud, us, v, w, vd, vs, wd, ws, under_way, *sums = held
    refs = {"u": u, "p": p, "c": c, "s": s, "f": f}
    refs["fields"] = ((u, ud, us), (v, vd, vs), (w, wd, ws))
    return refs, under_way, sums


def beyond(axis, even, index):
    other = jnp.where(even == 1, index - 1, index + 1)
    return (other >= 0) & (other < lax.axis_size(axis))


def lay_side(values, refs, high):
    nx, wide = values[0].shape[0], refs["u"].shape[2]
    ny = wide - PAD
    for name, k, ring, value in joined(lambda n: values[n], UNITS):
        y = ny - 1 + ring if high else wide - ring
        first = 1 if name == "f" else RING
        for x in range(nx):
            refs[name][k, first + x, y : y + 1, :] = value[x : x + 1]


def stage_kernel(
    y0_in, u_in, p_in, c_in, s_in, f_in, u_ref, p_ref, c_ref, s_ref, f_ref, ud_ref, us_ref, fz_ref
):
    nx, ny, nz = c_in.shape[1:]
    wide = u_ref.shape[2]
    for src, ref in ((u_in, u_ref), (p_in, p_ref), (c_in, c_ref), (s_in, s_ref)):
        lead = (0,) if src is u_in else ()
        for k in range(ref.shape[0]):
            for x in range(ref.shape[1]):
                if RING <= x < RING + nx:
                    value = src[lead + (k, x - RING)]
                    ref[k, x, :ny, :] = value
                    ref[k, x, ny:, :] = jnp.zeros((wide - ny, nz), F32)
                    if src is u_in:
                        keep_z(k, x, value, ud_ref, us_ref, slice(0, ny))
                else:
                    ref[k, x] = jnp.zeros(ref.shape[2:], F32)
    stage_forward(f_in, f_ref, fz_ref)
    refs = {"u": u_ref, "p": p_ref, "c": c_ref, "s": s_ref, "f": f_ref}
    even_j = position()[1]
    near = side_units(y0_in, nx)
    pl.when(even_j == 1)(lambda: lay_side(near, refs, True))
    pl.when(even_j == 0)(lambda: lay_side(near, refs, False))


def early_kernel(fz_ref, y1_in, *rest):
    refs, under_way, sums = named(rest[7:])
    u_ref, ud_ref, us_ref = refs["fields"][0]
    nx, ny, nz = fz_ref.shape[1:]
    wide = u_ref.shape[2]
    even_i, even_j, i, j, _ = position()
    ok_y1 = beyond("ty", even_j, j)

    far = [jnp.where(ok_y1, value, 0.0) for value in side_units(y1_in, nx)]
    pl.when(even_j == 1)(lambda: lay_side(far, refs, False))
    pl.when(even_j == 0)(lambda: lay_side(far, refs, True))
    for x in range(RING, RING + nx):
        for k in range(3):
            keep_z(k, x, u_ref[k, x, ny:], ud_ref, us_ref, slice(ny, wide))
    run_steps(refs, fz_ref, under_way, sums, middle_rows(nx), lambda row: row)

    @pl.when(jnp.logical_not(beyond("tx", even_i, i)))
    def _():
        run_side(refs, fz_ref, under_way, sums, even_i == 0)


def side_kernel(second, fz_ref, faces, corners, *rest):
    if second:
        *rest, message = rest
    refs, under_way, sums = named(rest[len(rest) // 2 :])
    nx, ny, nz = fz_ref.shape[1:]
    wide = refs["u"].shape[2]
    even_i, even_j, i, j, _ = position()
    high = even_i == (0 if second else 1)

    def run():
        for name, k, ring, value in joined(lambda n: faces[n].astype(F32), ROWS):
            first = 1 if name == "f" else RING
            x = jnp.where(high, first + nx - 1 + ring, first - ring)
            refs[name][k, x, :ny, :] = value
        near = [faces[FACE_BLOCKS + n].astype(F32) for n in range(CORNER_BLOCKS)]
        ok_y1 = beyond("ty", even_j, j)
        far = [jnp.where(ok_y1, corners[n].astype(F32), 0.0) for n in range(CORNER_BLOCKS)]
        for y_high in (True, False):
            flag = even_j == (1 if y_high else 0)
            values = [jnp.where(flag, a, b) for a, b in zip(near, far)]
            row = lambda n: values[n // 16][n % 16 : n % 16 + 1]
            for name, k, ring_x, ring_y, value in joined_corner(row):
                x = jnp.where(high, RING + nx - 1 + ring_x, RING - ring_x)
                y = ny - 1 + ring_y if y_high else wide - ring_y
                refs[name][k, x, y : y + 1, :] = value
        place = len(CORNERS)
        u3 = [near[(place + k) // 16][(place + k) % 16 : (place + k) % 16 + 1] for k in range(2)]
        x = jnp.where(high, RING + nx + 1, RING - 2)
        for y_high in (True, False):
            y = ny if y_high else wide - 1
            quarter = jnp.where(high == y_high, -0.25, 0.25)
            quarter = jnp.where(even_j == (0 if y_high else 1), quarter, 0.0)
            weight = refs["c"][1, x, y : y + 1, :] * quarter
            for k in range(2):
                refs["p"][k, x, y : y + 1, :] += weight * u3[1 - k]
        run_side(refs, fz_ref, under_way, sums, high)

    if second:
        pl.when(beyond("tx", even_i, i))(run)
    else:
        run()
    if second:
        lay_out(sums[-1], message)


def total_kernel(scale, own_ref, sent_ref, out_ref, stage, sems):
    nx = own_ref.shape[1]
    back = jnp.exp((sent_ref[2 * nx] - TARGET) * math.log(2.0))
    copies = []
    for n in range(2):
        for x in range(nx):
            stage[n, x] = (own_ref[n, x] + sent_ref[n * nx + x] * back) * scale
        copies.append(pltpu.make_async_copy(stage.at[n], out_ref.at[n], sems.at[n]))
        copies[n].start()
    for copy in copies:
        copy.wait()


def last_kernel(w_ref, wd_ref, ws_ref, v_ref, c_ref, s_ref, out_ref):
    nx, ny = out_ref.shape[2:4]

    @pl.loop(RING, RING + nx, unroll=UNROLL)
    def _(x):
        fresh = advance_row(
            STEPS - 1, Row(x, w_ref, wd_ref), v_ref, None, c_ref, s_ref, ws_ref, ny
        )
        for k in range(3):
            out_ref[0, k, x - RING] = fresh[k]


def swap_map(sizes, partner):
    nx, ny, ns = sizes

    def meets(i, j):
        a, b = partner(i, j)
        return 0 <= a < nx and 0 <= b < ny

    pairs = []
    for i in range(nx):
        for j in range(ny):
            for s in range(ns):
                if meets(i, j):
                    to = (*partner(i, j), s)
                elif not (meets(i, j ^ 1) or meets(0, 1) or meets(1, 0)):
                    across = j + 1 if j % 2 else j - 1
                    to = (i, across, s) if 0 <= across < ny else (i, j, s ^ 1 if s ^ 1 < ns else s)
                elif not meets(i, j ^ 1):
                    to = (i, j ^ 1, s)
                else:
                    to = (i, j, s ^ 1 if s ^ 1 < ns else s)
                pairs.append(((i * ny + j) * ns + s, (to[0] * ny + to[1]) * ns + to[2]))
    return pairs


def body(
    adj_now,
    adj_later,
    forward_field,
    lame_first,
    shear,
    buoyancy,
    seafloor_depth,
    station_columns,
    station_traces,
):
    nx, ny, nz = lame_first.shape
    sizes = tuple(lax.axis_size(axis) for axis in AXES)
    count_s = sizes[2]
    vmem = pl.BlockSpec(memory_space=pltpu.VMEM)
    anywhere = pl.BlockSpec(memory_space=pl.ANY)
    limit = 30 * 1024 * 1024
    params = pltpu.CompilerParams(vmem_limit_bytes=limit)
    face = jax.ShapeDtypeStruct((FACE_BLOCKS + CORNER_BLOCKS, ny, nz), BF16)
    edge = jax.ShapeDtypeStruct((SIDE_BLOCKS, 2 * nx, nz), BF16)
    corner = jax.ShapeDtypeStruct((CORNER_BLOCKS, 16, nz), BF16)
    grid = lambda n: jax.ShapeDtypeStruct((n, nx, ny, nz), F32)

    like = lambda value: jax.ShapeDtypeStruct(value.shape, value.dtype)
    traces = jnp.transpose(station_traces, (1, 0, 2))
    held = (adj_later, lame_first, shear, buoyancy, seafloor_depth, station_columns, traces)
    u0, fwd, carry, coeff, drive, y0 = pl.pallas_call(
        pack_kernel,
        out_shape=(
            like(adj_now),
            like(forward_field),
            grid(3),
            grid(2),
            grid(2),
            edge,
        ),
        in_specs=[anywhere] * 9,
        out_specs=(vmem,) * 6,
        scratch_shapes=[pltpu.VMEM(value.shape, value.dtype) for value in held]
        + [pltpu.SemaphoreType.DMA((9,))],
        compiler_params=params,
        name="pack",
    )(
        *(
            pltpu.with_memory_space_constraint(value, pltpu.HBM)
            for value in (adj_now, adj_later, forward_field, *held[1:])
        )
    )

    def exchange(value, partner):
        return lax.ppermute(value, AXES, swap_map(sizes, partner))

    flip = lambda n: n + 1 if n % 2 == 0 else n - 1
    back = lambda n: n - 1 if n % 2 == 0 else n + 1
    y0 = exchange(y0, lambda a, b: (a, flip(b)))
    wide_x, wide_y = nx + 2 * RING, ny + PAD
    padded = lambda n, x=wide_x: jax.ShapeDtypeStruct((n, x, wide_y, nz), F32)
    x0, x1, y1, c0, c1 = pl.pallas_call(
        face_kernel,
        out_shape=(
            face,
            face,
            edge,
            corner,
            corner,
        ),
        in_specs=[vmem] * 5,
        out_specs=(vmem,) * 5,
        compiler_params=params,
        name="faces",
    )(u0, fwd, carry, coeff, drive)
    x0, x1 = pl.pallas_call(
        corner_kernel,
        out_shape=(face, face),
        in_specs=[vmem] * 4,
        out_specs=(vmem,) * 2,
        input_output_aliases={2: 0, 3: 1},
        compiler_params=params,
        name="corners",
    )(y0, u0, x0, x1)
    x0 = exchange(x0, lambda a, b: (flip(a), b))
    x1 = exchange(x1, lambda a, b: (back(a), b))
    y1 = exchange(y1, lambda a, b: (a, back(b)))
    c0 = exchange(c0, lambda a, b: (flip(a), back(b)))
    c1 = exchange(c1, lambda a, b: (back(a), back(b)))

    tile = (padded(3), padded(3), padded(2), padded(2))
    split_up = count_s == 2
    depth = nz // 2 if split_up else nz
    sums = (jax.ShapeDtypeStruct((2, nx, ny, depth), F32),) * (1 + split_up)
    staged = (*tile, padded(3 * STEPS, nx + 2), padded(3), padded(3))
    *held, fwd_z = pl.pallas_call(
        stage_kernel,
        out_shape=(*staged, grid(3 * STEPS)),
        in_specs=[vmem] * 6,
        out_specs=(vmem,) * 8,
        compiler_params=params,
        name="stage",
    )(y0, u0, carry, coeff, drive, fwd)
    shapes = (*staged, *(padded(3),) * 6, grid(2), *sums)
    held = pl.pallas_call(
        early_kernel,
        out_shape=shapes,
        in_specs=[vmem] * 9,
        out_specs=(vmem,) * len(shapes),
        input_output_aliases={2 + n: n for n in range(7)},
        compiler_params=params,
        name="early",
    )(fwd_z, y1, *held)

    def side(second, faces, corners, held):
        message = (jax.ShapeDtypeStruct((2 * nx + 1, ny, depth), F32),) * second
        return pl.pallas_call(
            functools.partial(side_kernel, second),
            out_shape=(*shapes, *message),
            in_specs=[vmem] * (3 + len(shapes)),
            out_specs=(vmem,) * (len(shapes) + second),
            input_output_aliases={3 + n: n for n in range(len(shapes))},
            compiler_params=params,
            name="second" if second else "first",
        )(fwd_z, faces, corners, *held)

    held = side(False, x0, c0, held)
    *held, message = side(True, x1, c1, held)
    coeff, drive = held[2:4]
    u1, u2 = held[7:9]
    u2_d, u2_s = held[11:13]

    sums = held[14:]
    scale = 0.25 / (adj_now.shape[0] * count_s)
    if split_up:
        sent = lax.ppermute(message.astype(jnp.float16), "src", [(0, 1), (1, 0)])
        summed = pl.pallas_call(
            functools.partial(total_kernel, scale),
            out_shape=like(sums[0]),
            in_specs=[vmem] * 2,
            out_specs=anywhere,
            scratch_shapes=[
                pltpu.VMEM(sums[0].shape, F32),
                pltpu.SemaphoreType.DMA((2,)),
            ],
            compiler_params=params,
            name="total",
        )(sums[0], sent.astype(F32))
    else:
        summed = lax.psum_scatter(sums[0] * scale, "src", scatter_dimension=3, tiled=True)
    final = pl.pallas_call(
        last_kernel,
        out_shape=like(adj_now),
        in_specs=[vmem] * 6,
        out_specs=vmem,
        compiler_params=params,
        name="last",
    )(u2, u2_d, u2_s, u1, coeff, drive)
    return final, summed


def solution(mesh):
    in_specs = (
        P("src", None, "tx", "ty", None),
        P("src", None, "tx", "ty", None),
        P("src", None, None, "tx", "ty", None),
        P("tx", "ty", None),
        P("tx", "ty", None),
        P("tx", "ty", None),
        P("tx", "ty"),
        P("src", None),
        P("src", None, None),
    )
    out_specs = (P("src", None, "tx", "ty", None), P(None, "tx", "ty", "src"))
    return jax.shard_map(body, mesh=mesh, in_specs=in_specs, out_specs=out_specs, check_vma=False)
```
